32 devices in a mesh: strip: 8 (over z, x), sub: 4 (over y, core).
Axes of the slice: x: 2, y: 2, z: 4, core: 2. Of those that a mesh axis runs over, the one named last changes fastest.
Arguments:
- features: bfloat16 [32768, 128], P(('strip', 'sub')), may hold values from -6 to 6
- position: bfloat16 [2, 32768, 128], P(None, ('strip', 'sub')), may hold values from -6 to 6
- cotangent: bfloat16 [32768, 128], P(('strip', 'sub')), may hold values from -6 to 6
- w_qkv: bfloat16 [2, 128, 384], replicated, may hold values from -0.5 to 0.5
- w_out: bfloat16 [2, 128, 128], replicated, may hold values from -1.5 to 1.5
- w_up: bfloat16 [2, 128, 256], replicated, may hold values from -0.5 to 0.5
- w_down: bfloat16 [2, 256, 128], replicated, may hold values from -0.375 to 0.375
- b_up: float32 [2, 256], replicated, may hold values from -3 to 3
- gains: float32 [2, 2, 128], replicated, may hold values from 0.5 to 1.5
- shifts: float32 [2, 4, 128], replicated, may hold values from -3 to 3
- window: int32 [32768], P(('strip', 'sub')), may hold values from 0 to 31
- shifted_window: int32 [32768], P(('strip', 'sub')), may hold values from 0 to 63
- dest: int32 [32768], P(('strip', 'sub')), may hold values from 0 to 7, as said below
- slot: int32 [32768], P(('strip', 'sub')), may hold values from 0 to 255, as said below
- valid: int32 [32768], P(('strip', 'sub')), may hold values 0 or 1
Outputs:
- output: bfloat16 [32768, 128], P(('strip', 'sub'))
- grad_features: float32 [32768, 128], P(('strip', 'sub'))
- grad_w_qkv: float32 [2, 128, 384], replicated
- grad_w_out: float32 [2, 128, 128], replicated
- grad_w_up: float32 [2, 128, 256], replicated
- grad_w_down: float32 [2, 256, 128], replicated
- grad_b_up: float32 [2, 256], replicated
- grad_gains: float32 [2, 2, 128], replicated
- grad_shifts: float32 [2, 4, 128], replicated
The draws below stay inside these ranges and needn't reach their ends.
Inputs may be any that keep to these rules, and one draw needn't show every extreme that they name: On each device no two pillars share both dest and slot; the pillars of one device with one dest have slots 0 up to their count minus one. In every draw one strip receives 256 pillars from every device and another receives none. Some pillar of every device has slot 255.
All inputs are finite; a program needn't handle non-finite values. No bound on the sum of `valid` on one device may be relied on, other than what follows from the above.
Results may differ from the reference program's by a relative error of at most 0.019.
The reference program's roundings to bfloat16 on the way count: a program that leaves them out, or rounds other values in their place, can miss the bound.
Values may be sent and summed in bfloat16 or wider, within the bound.
No kernel may reach another device: no remote copies, remote signals or barrier semaphores. Data moves between devices by JAX's collectives and lax.ppermute only.
A program may use at most 192 MiB of HBM per device.

```python
import math
import jax
import jax.numpy as jnp
import numpy as np
from jax import lax

D = 128
HEADS = 8
FF = 256
TOK_DEV = 1024
HEAD_DIM = 16
STRIPS = 8
SUBS = 4
DEVS = 32
CAP = 256
WIN_DEV = 32
TOKENS = 32768


def route_pair(key):
    order_key, turn_key, shuffle_key = jax.random.split(jax.random.fold_in(key, 17), 3)
    order = jax.random.permutation(order_key, STRIPS)
    half = CAP // 2
    turns = jax.random.randint(turn_key, (DEVS, STRIPS // 2), -half, half + 1)
    turns = turns.at[:, 0].set(half)
    counts = jnp.zeros((DEVS, STRIPS), jnp.int32)
    counts = counts.at[:, order[0::2]].set(half + turns).at[:, order[1::2]].set(half - turns)
    bounds = jnp.cumsum(counts, axis=1)
    seats = jnp.arange(TOK_DEV, dtype=jnp.int32)
    groups = jnp.sum((seats[None, :, None] >= bounds[:, None, :]).astype(jnp.int32), axis=2)
    starts = bounds - counts
    ranks = seats[None, :] - jnp.take_along_axis(starts, groups, axis=1)
    shuffles = jax.vmap(lambda single: jax.random.permutation(single, TOK_DEV))(jax.random.split(shuffle_key, DEVS))
    owners = jnp.arange(DEVS, dtype=jnp.int32)[:, None]
    dests = jnp.zeros((DEVS, TOK_DEV), jnp.int32).at[owners, shuffles].set(groups)
    slots = jnp.zeros((DEVS, TOK_DEV), jnp.int32).at[owners, shuffles].set(ranks)
    return (dests.reshape(-1), slots.reshape(-1))


def draw_dest(key, part):
    return route_pair(key)[0]


def draw_slot(key, part):
    return route_pair(key)[1]


def set_ends(entries, key, smallest, top_value):
    spot = [jax.random.randint(jax.random.fold_in(key, axis), (), 0, length) for axis, length in enumerate(entries.shape)]
    main_axis = entries.shape.index(max(entries.shape))
    neighbour = spot[:main_axis] + [(spot[main_axis] + 1) % entries.shape[main_axis]] + spot[main_axis + 1:]
    return entries.at[tuple(spot)].set(smallest).at[tuple(neighbour)].set(top_value)


def block_scale(own_key, extent, cuts, least, top_value):
    def one(dim, blocks):
        heights = jax.random.uniform(jax.random.fold_in(jax.random.fold_in(own_key, 6), dim), (blocks,), jnp.float32, least / len(cuts), top_value / len(cuts))
        return jnp.repeat(jnp.exp(heights), extent[dim] // blocks).reshape((-1,) + (1,) * (len(extent) - dim - 1))

    level = one(*cuts[0])
    for cut in cuts[1:]:
        level = level * one(*cut)
    return level


def cumulative_ranks(number_of, lean):
    weights = [(1 << 20) // math.isqrt(standing ** lean) + 1 for standing in range(1, number_of + 1)]
    scale = 1 + sum(weights) // (1 << 30)
    return np.cumsum(np.array([max(1, weight // scale) for weight in weights]))


def skewed_ids(own_key, shape, number_of, slope):
    table = cumulative_ranks(number_of, slope)
    pick = jax.random.randint(jax.random.fold_in(own_key, 1), shape, 0, int(table[number_of - 1]))
    standing = jnp.searchsorted(jnp.asarray(table, jnp.int32), pick, side="right")
    return jax.random.permutation(jax.random.fold_in(own_key, 2), number_of)[standing].astype(jnp.int32)


def scatter_about(own_key, dims, scale, bound, cuts=(), held_as=jnp.bfloat16):
    factor_of = block_scale(own_key, dims, cuts, -0.22, 0.18) if cuts else 1.0
    values = jax.random.normal(own_key, dims, jnp.float32) * scale * factor_of
    return jnp.minimum(jnp.maximum(values, -bound), bound).astype(held_as)


def setup_inputs(seed: int = 0) -> dict:
    seeds = jax.random.split(jax.random.key(seed), 16)
    return {
        "features": scatter_about(seeds[0], (TOKENS, D), 1.0, 6.0, ((0, 32),)),
        "position": scatter_about(seeds[1], (2, TOKENS, D), 1.0, 6.0, ((1, 32),)),
        "cotangent": scatter_about(seeds[2], (TOKENS, D), 1.0, 6.0, ((0, 32),)),
        "w_qkv": scatter_about(seeds[3], (2, D, 3 * D), D ** -0.5, 0.5),
        "w_out": scatter_about(seeds[4], (2, D, D), (D // 8) ** -0.5, 1.5),
        "w_up": scatter_about(seeds[5], (2, D, FF), D ** -0.5, 0.5),
        "w_down": scatter_about(seeds[6], (2, FF, D), FF ** -0.5, 0.375),
        "b_up": scatter_about(seeds[7], (2, FF), 0.3, 3.0, (), jnp.float32),
        "gains": jnp.clip(1.0 + 0.1 * jax.random.normal(seeds[8], (2, 2, D), jnp.float32), 0.5, 1.5),
        "shifts": scatter_about(seeds[9], (2, 4, D), 0.3, 3.0, (), jnp.float32),
        "window": set_ends(skewed_ids(seeds[10], (TOKENS,), WIN_DEV, 1), jax.random.fold_in(seeds[10], 3), 0, WIN_DEV - 1).astype(jnp.int32),
        "shifted_window": set_ends(skewed_ids(seeds[11], (TOKENS,), 2 * WIN_DEV, 1), jax.random.fold_in(seeds[11], 3), 0, (2 * WIN_DEV) - 1).astype(jnp.int32),
        "dest": draw_dest(jax.random.fold_in(seeds[15], 71), 0),
        "slot": draw_slot(jax.random.fold_in(seeds[15], 71), 0),
        "valid": set_ends((jax.random.randint(seeds[14], (TOKENS,), 0, 8) < 7).astype(jnp.int32), jax.random.fold_in(seeds[14], 1), 0, 1),
    }


@jax.custom_vjp
def low(v):
    return lax.optimization_barrier(v.astype(jnp.bfloat16)).astype(jnp.float32)

@jax.custom_vjp
def low_back(v):
    return v

def low_keep(v):
    return (low(v), None)

def low_pass(kept, grad):
    return (grad,)

def back_keep(v):
    return (v, None)

def back_low(kept, grad):
    return (low(grad),)
low.defvjp(low_keep, low_pass)
low_back.defvjp(back_keep, back_low)
EPS = 1e-05
HIGHEST = lax.Precision.HIGHEST

def norm_rows(hidden, gain, shift):
    average = lax.optimization_barrier(jnp.mean(hidden, axis=-1, keepdims=True))
    centered = hidden - average
    variance = lax.optimization_barrier(jnp.mean(centered * centered, axis=-1, keepdims=True))
    return centered * lax.rsqrt(variance + EPS) * gain + shift

def layer(inputs, placing, live, window_ids, params):
    w_qkv, w_out, w_up, w_down, b_up, gains, shifts = params
    row_total = inputs.shape[0]
    joined = low(inputs + placing)
    query_key = low_back(low(jnp.dot(joined, w_qkv[:, :2 * D], precision=HIGHEST)))
    values = low_back(low(jnp.dot(inputs, w_qkv[:, 2 * D:], precision=HIGHEST)))
    queries = query_key[:, :D].reshape(row_total, HEADS, HEAD_DIM)
    keys = query_key[:, D:].reshape(row_total, HEADS, HEAD_DIM)
    head_values = values.reshape(row_total, HEADS, HEAD_DIM)
    scores = low_back(jnp.einsum('ihd,jhd->hij', queries, keys, precision=HIGHEST) * HEAD_DIM ** (-0.5))
    allowed = (window_ids[:, None] == window_ids[None, :]) & (live[None, :] > 0)
    attention = low(jax.nn.softmax(jnp.where(allowed[None], scores, -1e+30), axis=-1))
    mixed = jnp.einsum('hij,jhd->ihd', attention, head_values, precision=HIGHEST).reshape(row_total, D)
    mixed = low_back(low(mixed))
    attended = low_back(jnp.dot(mixed, w_out, precision=HIGHEST) + shifts[0])
    first_out = norm_rows(inputs + attended, gains[0], shifts[1])
    before = low_back(jnp.dot(low(first_out), w_up, precision=HIGHEST) + b_up)
    activated = low(jax.nn.gelu(before))
    branch = low_back(jnp.dot(activated, w_down, precision=HIGHEST) + shifts[2])
    result = norm_rows(first_out + branch, gains[1], shifts[3])
    return result * live[:, None].astype(jnp.float32)

def reference(features, position, cotangent, w_qkv, w_out, w_up, w_down, b_up, gains, shifts, window, shifted_window, dest, slot, valid):
    device_total = STRIPS * SUBS
    buffer_rows = STRIPS * CAP
    place = (dest * CAP + slot).reshape(device_total, TOK_DEV).astype(jnp.int32)
    owner = jnp.arange(device_total, dtype=jnp.int32)[:, None]

    def relayout(buffer):
        shaped = buffer.reshape(STRIPS, SUBS, STRIPS, CAP, buffer.shape[-1])
        return shaped.transpose(2, 1, 0, 3, 4).reshape(device_total, buffer_rows, buffer.shape[-1])
    placing = position.astype(jnp.float32).reshape(2, device_total, TOK_DEV, D)
    live_one = valid.reshape(device_total, TOK_DEV)
    ids_one = window.reshape(device_total, TOK_DEV)
    meta = jnp.stack([shifted_window.reshape(device_total, TOK_DEV), live_one], axis=2)
    meta_in = relayout(jnp.zeros((device_total, buffer_rows, 2), jnp.int32).at[owner, place].set(meta))
    ids_two = meta_in[..., 0]
    live_two = meta_in[..., 1]
    placing_two = relayout(jnp.zeros((device_total, buffer_rows, D), jnp.float32).at[owner, place].set(placing[1]))

    def forward(feats, wqkv, wout, wup, wdown, bup, gain_set, shift_set):

        def layer_zero(items):
            return layer(items[0], items[1], items[2], items[3], (wqkv[0], wout[0], wup[0], wdown[0], bup[0], gain_set[0], shift_set[0]))

        def layer_one(items):
            return layer(items[0], items[1], items[2], items[3], (wqkv[1], wout[1], wup[1], wdown[1], bup[1], gain_set[1], shift_set[1]))
        out_zero = lax.map(jax.checkpoint(layer_zero), (feats.reshape(device_total, TOK_DEV, D), placing[0], live_one, ids_one))
        out_zero = low_back(low(out_zero))
        inputs_two = relayout(jnp.zeros((device_total, buffer_rows, D), jnp.float32).at[owner, place].set(out_zero))
        out_one = low(lax.map(jax.checkpoint(layer_one), (inputs_two, placing_two, live_two, ids_two)))
        returned = relayout(out_one)
        return returned[owner, place].reshape(TOKENS, D)
    output, pullback = jax.vjp(forward, features.astype(jnp.float32), w_qkv.astype(jnp.float32), w_out.astype(jnp.float32), w_up.astype(jnp.float32), w_down.astype(jnp.float32), b_up, gains, shifts)
    grads = pullback(cotangent.astype(jnp.float32))
    return (output.astype(jnp.bfloat16), grads[0], grads[1], grads[2], grads[3], grads[4], grads[5], grads[6], grads[7])
```

```python
import functools

import jax
import jax.numpy as jnp
from jax import lax
from jax.experimental import pallas as pl
from jax.experimental.pallas import tpu as pltpu
from jax.sharding import PartitionSpec as P

HEADS = 8
EPS = 1e-05
NEGATIVE = -1e30
BLK = 128
CH = 256
WINDOWS = 64
VMEM = 60 * 1024 * 1024
F32, BF16, I32 = jnp.float32, jnp.bfloat16, jnp.int32
GRAD_ROWS = 1040


def dot(a, b):
    return lax.dot_general(a, b, (((1,), (0,)), ((), ())), preferred_element_type=F32)


def dot_nt(a, b):
    return lax.dot_general(a, b, (((1,), (1,)), ((), ())), preferred_element_type=F32)


def flip(x):
    return jnp.transpose(x.astype(F32)).astype(BF16)


def iota(shape, dim):
    return lax.broadcasted_iota(I32, shape, dim)


def column(row):
    return jnp.transpose(jnp.broadcast_to(row, (BLK, BLK)))


def twice(x):
    return jnp.concatenate([x, x], axis=1)


def seat_rows(win, live, cnt_ref, start_ref, pcol_ref):
    total = win.shape[1]
    blocks = total // BLK
    key = jnp.where(live, win, -1)
    hot = (iota((WINDOWS, total), 0) == key).astype(F32)
    hot_low = hot.astype(BF16)
    stacked = jnp.concatenate([hot_low[:, b * BLK : (b + 1) * BLK] for b in range(blocks)], axis=0)
    row_at, col_at = iota((BLK, 2 * BLK), 0), iota((BLK, 2 * BLK), 1)
    counter = ((row_at < col_at) | (col_at >= BLK)).astype(F32).astype(BF16)
    sums = dot(stacked, counter)
    carry = jnp.zeros((WINDOWS, BLK), F32)
    before = []
    for b in range(blocks):
        part = sums[b * WINDOWS : (b + 1) * WINDOWS]
        before.append(part[:, :BLK] + carry)
        carry = carry + part[:, BLK:]
    counts = carry.astype(I32)
    cnt_ref[...] = counts
    cursor = jnp.zeros((8, BLK), I32)
    room = jnp.zeros((8, BLK), I32)
    largest = jnp.zeros((8, BLK), I32)
    sub = iota((8, BLK), 0)
    for g in range(WINDOWS // 8):
        tile = jnp.zeros((8, BLK), I32)
        for i in range(8):
            w = 8 * g + i
            count = jnp.broadcast_to(counts[w : w + 1, :], (8, BLK))
            fits = count <= room
            start = jnp.where(fits, cursor, cursor + room)
            tile = jnp.where(sub == i, start, tile)
            cursor = start + count
            room = jnp.where(fits, room - count, (-count) & (BLK - 1))
            largest = jnp.maximum(largest, count)
        start_ref[8 * g : 8 * g + 8, :] = tile
    starts = start_ref[...].astype(F32)
    for b in range(blocks):
        sl = slice(b * BLK, (b + 1) * BLK)
        seat = jnp.sum(hot[:, sl] * (before[b] + starts), axis=0, keepdims=True)
        seat = jnp.where(live[:, sl], seat, -1.0)
        pcol_ref[sl, :] = column(seat).astype(I32)
    used = (jnp.max(cursor) + (BLK - 1)) // BLK
    return used, jnp.max(largest)


def norm_forward(hidden, gain, shift):
    size = hidden.shape[0]
    average = jnp.sum(hidden, axis=0, keepdims=True) * (1.0 / size)
    centered = hidden - average
    inverse = lax.rsqrt(jnp.sum(centered * centered, axis=0, keepdims=True) * (1.0 / size) + EPS)
    normed = centered * inverse
    return normed * gain + shift, normed, inverse


def norm_backward(upstream, normed, inverse, gain):
    size = upstream.shape[0]
    scaled = upstream * gain
    center = jnp.sum(scaled, axis=0, keepdims=True) * (1.0 / size)
    along = jnp.sum(scaled * normed, axis=0, keepdims=True) * (1.0 / size)
    return inverse * (scaled - center - normed * along)


GELU_A = 0.7978845608028654
GELU_B = 0.044715


def tiles(x):
    return x.reshape(x.shape[0] // 8, 8, x.shape[1])


def own_heads(x):
    size = x.shape[0] // HEADS
    return jnp.concatenate(
        [x[h * size : (h + 1) * size, h * BLK : (h + 1) * BLK] for h in range(HEADS)], axis=0
    )


def whole_rows(x):
    return jnp.broadcast_to(x, (8, x.shape[1]))


def head_stack(x):
    size = x.shape[0] // HEADS
    zero = jnp.zeros((size, x.shape[1]), x.dtype)
    blocks = []
    for h in range(HEADS):
        rows = [zero] * HEADS
        rows[h] = x[h * size : (h + 1) * size]
        blocks.append(jnp.concatenate(rows, axis=0))
    return jnp.concatenate(blocks, axis=1)


def layer_kernel(mode, level, cap, *refs):
    refs = list(refs)
    take = lambda n: [refs.pop(0) for _ in range(n)]
    if mode == "mid":
        meta_ref, rest_ref, x_ref = take(3)
    else:
        meta_ref, x_ref, pos_ref = take(3)
        if mode == "bwd":
            (grad_ref,) = take(1)
    wqkv_ref, wout_ref, wup_ref, wdown_ref, bup_ref, gains_ref, shifts_ref = take(7)
    if mode == "fwd":
        (msg_ref,) = take(1)
    else:
        back_ref, wg_ref = take(2)
    (
        cnt_ref, start_ref, pcol_ref, srct_ref, pick_ref, acc_ref,
        wqkvt_ref, woutt_ref, wupt_ref, wdownt_ref, cols_ref,
        xt_ref, ut_ref, qt_ref, kt_ref, vt_ref, k_ref, v_ref, idrow_ref, idcol_ref, place_ref,
    ) = take(21)
    if mode != "fwd":
        (
            dy_ref, yt_ref, dh_ref, dq_ref, dk_ref, dv_ref, a_ref,
            gq_ref, go_ref, gu_ref, gd_ref, gg_ref,
        ) = take(12)
        if mode == "bwd":
            (rowst_ref,) = take(1)
    stat_ref, stack_ref, span_ref = take(3)

    total = meta_ref.shape[1]
    width = x_ref.shape[-1]
    head = width // HEADS
    scale = head ** (-0.5)
    meta = meta_ref[...].astype(I32)
    win, live = meta[0:1], meta[1:2] > 0

    used, largest = seat_rows(win, live, cnt_ref, start_ref, pcol_ref)
    chunks = (used + 1) // 2
    several = largest > BLK

    for b in range(total // BLK):
        sl = slice(b * BLK, (b + 1) * BLK)
        if mode == "mid":
            srct_ref[0:width, sl] = flip(x_ref[sl, :])
            rest = flip(rest_ref[sl, :])
            srct_ref[width : 3 * width, sl] = rest
        else:
            srct_ref[0:width, sl] = flip(x_ref[sl, :])
            srct_ref[width : 2 * width, sl] = flip(pos_ref[0, sl, :])
    tags = srct_ref.shape[0] - 16
    at = iota((16, total), 0)
    rows = jnp.where(at == 0, win + 1, jnp.where(at == 1, 1, 0))
    if mode != "mid":
        rows = jnp.where(at == 2, meta[2:3], jnp.where(at == 3, meta[3:4], rows))
    srct_ref[tags:, :] = rows.astype(F32).astype(BF16)
    if mode == "bwd":
        for b in range(grad_ref.shape[0] // BLK):
            sl = slice(b * BLK, (b + 1) * BLK)
            rowst_ref[:, sl] = flip(grad_ref[sl, :])

    for b in range(3):
        sl = slice(b * BLK, (b + 1) * BLK)
        wqkvt_ref[sl, :] = flip(wqkv_ref[level, :, sl])
    woutt_ref[...] = flip(wout_ref[level])
    for b in range(2):
        sl = slice(b * BLK, (b + 1) * BLK)
        wupt_ref[sl, :] = flip(wup_ref[level, :, sl])
        wdownt_ref[:, sl] = flip(wdown_ref[level, sl, :])
        cols_ref[6 + b] = column(bup_ref[level : level + 1, sl])
    for b in range(2):
        cols_ref[b] = column(gains_ref[level, b : b + 1, :])
    for b in range(4):
        cols_ref[2 + b] = column(shifts_ref[level, b : b + 1, :])

    acc_ref[...] = jnp.zeros(acc_ref.shape, F32)
    if mode != "fwd":
        for ref in (gq_ref, go_ref, gu_ref, gd_ref, gg_ref):
            ref[...] = jnp.zeros(ref.shape, F32)

    @pl.loop(0, chunks)
    def _(c):
        seat = iota((BLK, BLK), 1) + c * CH
        for b in range(total // BLK):
            sl = slice(b * BLK, (b + 1) * BLK)
            col = pcol_ref[sl, :]
            for t in range(2):
                pick_ref[c, sl, t * BLK : (t + 1) * BLK] = (
                    (col == seat + t * BLK).astype(F32).astype(BF16)
                )
        moved = dot(srct_ref[...], pick_ref[c])
        xt = moved[:width]
        low = xt.astype(BF16)
        joined = (xt + moved[width : 2 * width]).astype(BF16)
        xt_ref[c] = low
        ut_ref[c] = joined
        qk = dot(wqkvt_ref[: 2 * width], joined).astype(BF16).astype(F32)
        vt = dot(wqkvt_ref[2 * width :], low).astype(BF16).astype(F32)
        qt_ref[c] = (qk[:width] * scale).astype(BF16)
        kt = qk[width:]
        ids = moved[tags : tags + 1]
        idrow_ref[c] = jnp.broadcast_to(ids, (8, CH))
        for t in range(2):
            sl = slice(t * BLK, (t + 1) * BLK)
            b = 2 * c + t
            kt_ref[b] = kt[:, sl].astype(BF16)
            vt_ref[b] = vt[:, sl].astype(BF16)
            k_ref[b] = jnp.transpose(kt[:, sl]).astype(BF16)
            v_ref[b] = jnp.transpose(vt[:, sl]).astype(BF16)
            idcol_ref[b] = column(ids[:, sl])
            if mode != "fwd":
                dk_ref[b] = jnp.zeros((BLK, width), F32)
                dv_ref[b] = jnp.zeros((BLK, width), F32)
        if mode == "mid":
            dy_ref[c] = moved[2 * width : 3 * width].astype(BF16)
        else:
            spot = moved[tags + 2 : tags + 3] * cap + moved[tags + 3 : tags + 4]
            spot = jnp.where(moved[tags + 1 : tags + 2] > 0.5, spot, -1.0)
            place_ref[c] = jnp.broadcast_to(spot, (8, CH)).astype(I32)

    @pl.when(several)
    def _():
        at = iota((WINDOWS, BLK), 1)
        count, start = cnt_ref[...], start_ref[...]
        first = lax.shift_right_logical(start, 7)
        final = lax.shift_right_logical(start + jnp.maximum(count, 1) - 1, 7)
        touch = (count > 0) & (first <= at) & (at <= final)
        low_at = jnp.min(jnp.where(touch, first, at), axis=0, keepdims=True)
        high_at = jnp.max(jnp.where(touch, final, at), axis=0, keepdims=True)
        for b in range(total // 64):
            span_ref[0, b] = jnp.max(jnp.where(at[0:1] == b, low_at, 0))
            span_ref[1, b] = jnp.max(jnp.where(at[0:1] == b, high_at, 0))

    def scores(stack, key_block, ids):
        bias = jnp.where(idcol_ref[key_block] == ids, 0.0, NEGATIVE)
        return dot(k_ref[key_block], stack), bias

    def chunk(c, single):
        qt = qt_ref[c]
        stacks, stats, mixed = [], [], []
        for t in range(2):
            sl = slice(t * BLK, (t + 1) * BLK)
            b = 2 * c + t
            ids = idrow_ref[c][0:1, sl]
            stack = head_stack(qt[:, sl])
            stacks.append(stack)
            if single:
                sc, bias = scores(stack, b, ids)
                parts = []
                for h in range(HEADS):
                    hs = slice(h * BLK, (h + 1) * BLK)
                    masked = sc[:, hs] + bias
                    top = jnp.max(masked, axis=0, keepdims=True)
                    e = jnp.exp(masked - top)
                    a = e * (1.0 / jnp.sum(e, axis=0, keepdims=True))
                    if mode != "fwd":
                        a_ref[t, :, hs] = a
                    parts.append(dot(vt_ref[b, h * head : (h + 1) * head, :], a.astype(BF16)))
                mixed.append(jnp.concatenate(parts, axis=0))
            else:
                lo, hi = span_ref[0, b], span_ref[1, b] + 1
                stack_ref[t, 0] = stack

                def masked_of(j, t=t, ids=ids):
                    sc, bias = scores(stack_ref[t, 0], j, ids)
                    return sc + jnp.concatenate([bias] * HEADS, axis=1)

                def step_top(j, top):
                    return jnp.maximum(top, jnp.max(tiles(masked_of(j)), axis=0))

                top = lax.fori_loop(lo, hi, step_top, jnp.full((8, HEADS * BLK), 2 * NEGATIVE, F32))
                stat_ref[t, 0] = whole_rows(jnp.max(top, axis=0, keepdims=True))

                def step_sum(j, summed, t=t, masked_of=masked_of):
                    top = stat_ref[t, 0]
                    return summed + jnp.sum(jnp.exp(tiles(masked_of(j)) - top[None]), axis=0)

                summed = lax.fori_loop(lo, hi, step_sum, jnp.zeros((8, HEADS * BLK), F32))
                stat_ref[t, 1] = whole_rows(1.0 / jnp.sum(summed, axis=0, keepdims=True))

                def step_mix(j, out, t=t, masked_of=masked_of):
                    top, inv = stat_ref[t, 0], stat_ref[t, 1]
                    a = jnp.exp(tiles(masked_of(j)) - top[None]) * inv[None]
                    a = a.reshape(BLK, HEADS * BLK).astype(BF16)
                    return out + own_heads(dot(vt_ref[j], a))

                mixed.append(lax.fori_loop(lo, hi, step_mix, jnp.zeros((width, BLK), F32)))
                stats.append((masked_of, lo, hi))
        mixed = jnp.concatenate(mixed, axis=1)
        mixed_low = mixed.astype(BF16)
        gain_one, gain_two = twice(cols_ref[0]), twice(cols_ref[1])
        attended = dot(woutt_ref[...], mixed_low) + twice(cols_ref[2])
        first_out, normed_one, inverse_one = norm_forward(
            xt_ref[c].astype(F32) + attended, gain_one, twice(cols_ref[3])
        )
        first_low = first_out.astype(BF16)
        bias_up = jnp.concatenate([twice(cols_ref[6]), twice(cols_ref[7])], axis=0)
        before = dot(wupt_ref[...], first_low) + bias_up
        square = before * before
        bend = jnp.tanh(GELU_A * before * (1.0 + GELU_B * square))
        activated = (0.5 * before * (1.0 + bend)).astype(BF16)
        branch = dot(wdownt_ref[...], activated) + twice(cols_ref[4])
        result, normed_two, inverse_two = norm_forward(
            first_out + branch, gain_two, twice(cols_ref[5])
        )
        if mode == "fwd":
            out_low = result.astype(BF16)
            at = iota((BLK, CH), 0)
            spot = place_ref[c][0:1]
            for r in range(acc_ref.shape[0] // BLK):
                sl = slice(r * BLK, (r + 1) * BLK)
                hot = (at + r * BLK == spot).astype(F32).astype(BF16)
                acc_ref[sl, :] += dot_nt(hot, out_low)
            return
        if mode == "mid":
            yt_ref[c] = result.astype(BF16)
            upstream = dy_ref[c].astype(F32)
        else:
            at = iota((BLK, CH), 0)
            spot = place_ref[c][0:1]
            hot = jnp.concatenate(
                [
                    (at + r * BLK == spot).astype(F32).astype(BF16)
                    for r in range(rowst_ref.shape[1] // BLK)
                ],
                axis=0,
            )
            upstream = dot(rowst_ref[...], hot)
        ones = jnp.ones((16, CH), BF16)
        gg_ref[0] += upstream * normed_two
        gg_ref[1] += upstream
        second = norm_backward(upstream, normed_two, inverse_two, gain_two)
        branch_low = second.astype(BF16)
        gd_ref[...] += dot_nt(jnp.concatenate([activated, ones], axis=0), branch_low)
        slope = 0.5 * (1.0 + bend) + (0.5 * GELU_A) * before * (1.0 - bend * bend) * (
            1.0 + (3.0 * GELU_B) * square
        )
        before_low = (dot(wdown_ref[level], branch_low) * slope).astype(BF16)
        gu_ref[...] += dot_nt(jnp.concatenate([first_low, ones], axis=0), before_low)
        first_grad = second + dot(wup_ref[level], before_low)
        gg_ref[2] += first_grad * normed_one
        gg_ref[3] += first_grad
        residual = norm_backward(first_grad, normed_one, inverse_one, gain_one)
        dh_ref[c] = residual
        attended_low = residual.astype(BF16)
        go_ref[...] += dot_nt(jnp.concatenate([mixed_low, ones], axis=0), attended_low)
        mixed_grad = dot(wout_ref[level], attended_low).astype(BF16)
        product = mixed_grad.astype(F32) * mixed
        for t in range(2):
            sl = slice(t * BLK, (t + 1) * BLK)
            b = 2 * c + t
            pull = head_stack(mixed_grad[:, sl])
            dots = [
                jnp.sum(product[h * head : (h + 1) * head, sl], axis=0, keepdims=True)
                for h in range(HEADS)
            ]
            if single:
                prob = dot(v_ref[b], pull)
                lows, grads, parts = [], [], []
                for h in range(HEADS):
                    hs = slice(h * BLK, (h + 1) * BLK)
                    a = a_ref[t, :, hs]
                    g = (a * (prob[:, hs] - dots[h])).astype(BF16)
                    lows.append(a.astype(BF16))
                    grads.append(g)
                    parts.append(dot(kt_ref[b, h * head : (h + 1) * head, :], g))
                dv_ref[b] = dot_nt(jnp.concatenate(lows, axis=1), pull)
                dk_ref[b] = dot_nt(jnp.concatenate(grads, axis=1), stacks[t])
                dq = jnp.concatenate(parts, axis=0)
            else:
                masked_of, lo, hi = stats[t]
                stat_ref[t, 2] = whole_rows(jnp.concatenate(dots, axis=1))
                stack_ref[t, 1] = pull

                def step_back(j, dq, t=t, masked_of=masked_of):
                    stack, pull = stack_ref[t, 0], stack_ref[t, 1]
                    top, inv, dots_row = stat_ref[t, 0], stat_ref[t, 1], stat_ref[t, 2]
                    a = jnp.exp(tiles(masked_of(j)) - top[None]) * inv[None]
                    g = a * (tiles(dot(v_ref[j], pull)) - dots_row[None])
                    a = a.reshape(BLK, HEADS * BLK)
                    g = g.reshape(BLK, HEADS * BLK).astype(BF16)
                    dv_ref[j] += dot_nt(a.astype(BF16), pull)
                    dk_ref[j] += dot_nt(g, stack)
                    return dq + own_heads(dot(kt_ref[j], g))

                dq = lax.fori_loop(lo, hi, step_back, jnp.zeros((width, BLK), F32))
            dq_ref[c, :, sl] = (dq * scale).astype(BF16)

    @pl.loop(0, chunks)
    def _(c):
        @pl.when(jnp.logical_not(several))
        def _():
            chunk(c, True)

        @pl.when(several)
        def _():
            chunk(c, False)

    if mode == "fwd":
        for r in range(acc_ref.shape[0] // BLK):
            sl = slice(r * BLK, (r + 1) * BLK)
            msg_ref[sl, :] = acc_ref[sl, :].astype(BF16)
        return

    @pl.loop(0, chunks)
    def _(c):
        dq = dq_ref[c]
        dk = jnp.concatenate([dk_ref[2 * c], dk_ref[2 * c + 1]], axis=0).astype(BF16)
        dv = jnp.concatenate([dv_ref[2 * c], dv_ref[2 * c + 1]], axis=0).astype(BF16)
        dx = (
            dh_ref[c]
            + dot(wqkv_ref[level, :, :width], dq)
            + dot_nt(wqkv_ref[level, :, width : 2 * width], dk)
            + dot_nt(wqkv_ref[level, :, 2 * width :], dv)
        )
        joined = ut_ref[c]
        gq_ref[0] += dot_nt(joined, dq)
        gq_ref[1] += dot(joined, dk)
        gq_ref[2] += dot(xt_ref[c], dv)
        high = dx.astype(BF16)
        if mode == "mid":
            pair = jnp.concatenate([yt_ref[c], high], axis=0)
        else:
            pair = jnp.concatenate([high, (dx - high.astype(F32)).astype(BF16)], axis=0)
        for r in range(total // 256):
            sl = slice(r * 256, (r + 1) * 256)
            acc_ref[sl, :] += dot_nt(pick_ref[c, sl, :], pair)

    for r in range(total // BLK):
        sl = slice(r * BLK, (r + 1) * BLK)
        if mode == "mid":
            back_ref[sl, :] = acc_ref[sl, :].astype(BF16)
        else:
            back_ref[sl, :] = acc_ref[sl, :width] + acc_ref[sl, width:]
    wg = functools.partial(jnp.concatenate, axis=0)
    for b in range(3):
        wg_ref[b * BLK : (b + 1) * BLK, :] = gq_ref[b].astype(BF16)
    wg_ref[384:512, :] = go_ref[:width].astype(BF16)
    for b in range(2):
        sl = slice(b * BLK, (b + 1) * BLK)
        wg_ref[512 + b * BLK : 640 + b * BLK, :] = gu_ref[:width, sl].astype(BF16)
    wg_ref[768:1024, :] = gd_ref[:256].astype(BF16)
    sums = []
    for i in range(4):
        both = gg_ref[i, :, :BLK] + gg_ref[i, :, BLK:]
        sums.append(jnp.sum(jnp.transpose(both), axis=0, keepdims=True))
    out_bias, down_bias = go_ref[width : width + 1], gd_ref[256:257]
    up_bias = gu_ref[width : width + 1]
    small = [
        sums[2], sums[0], out_bias, sums[3], down_bias, sums[1], up_bias[:, :BLK], up_bias[:, BLK:],
        jnp.zeros((8, BLK), F32),
    ]
    wg_ref[1024:GRAD_ROWS, :] = wg(small).astype(BF16)


def run_layer(mode, level, cap, buffer_rows, *args):
    total = args[0].shape[1]
    width = 128
    nb = total // 64
    nc = nb // 2
    extra = 3 if mode == "mid" else 2
    vm = pltpu.VMEM
    if mode == "fwd":
        out_shape = jax.ShapeDtypeStruct((buffer_rows, width), BF16)
        acc = vm((buffer_rows, width), F32)
    else:
        acc = vm((total, 2 * width), F32)
        out_shape = (
            jax.ShapeDtypeStruct((total, 2 * width), BF16)
            if mode == "mid"
            else jax.ShapeDtypeStruct((total, width), F32),
            jax.ShapeDtypeStruct((GRAD_ROWS, width), BF16),
        )
    chunked = lambda dt: vm((nc, width, CH), dt)
    blocked = lambda dt: vm((nb, BLK, BLK), dt)
    scratch = [
        vm((WINDOWS, BLK), I32), vm((WINDOWS, BLK), I32), vm((total, BLK), I32),
        vm((extra * width + 16, total), BF16), vm((nc, total, CH), BF16), acc,
        vm((384, width), BF16), vm((width, width), BF16), vm((256, width), BF16), vm((width, 256), BF16),
        vm((8, BLK, BLK), F32),
        chunked(BF16), chunked(BF16), chunked(BF16),
        blocked(BF16), blocked(BF16), blocked(BF16), blocked(BF16),
        vm((nc, 8, CH), F32), blocked(F32), vm((nc, 8, CH), I32),
    ]
    if mode != "fwd":
        scratch += [
            chunked(BF16), chunked(BF16), chunked(F32), chunked(BF16), blocked(F32), blocked(F32),
            vm((2, BLK, HEADS * BLK), F32),
            vm((3, width, width), F32), vm((width + 16, width), F32), vm((width + 16, 256), F32),
            vm((256 + 16, width), F32), vm((4, width, CH), F32),
        ]
        if mode == "bwd":
            scratch += [vm((width, buffer_rows), BF16)]
    scratch += [vm((2, 3, 8, HEADS * BLK), F32), vm((2, 2, width, HEADS * BLK), BF16), pltpu.SMEM((2, nb), I32)]
    spec = pl.BlockSpec(memory_space=pltpu.VMEM)
    return pl.pallas_call(
        functools.partial(layer_kernel, mode, level, cap),
        out_shape=out_shape,
        in_specs=[spec] * len(args),
        out_specs=spec if mode == "fwd" else (spec, spec),
        scratch_shapes=scratch,
        compiler_params=pltpu.CompilerParams(vmem_limit_bytes=VMEM),
        name="layer_" + mode,
    )(*args)


def send_kernel(cap, meta_ref, pos_ref, cot_ref, out_ref):
    strips = out_ref.shape[0]
    total = meta_ref.shape[1]
    meta = meta_ref[...]
    place = jnp.where(meta[3:4] > 0, meta[0:1] * cap + meta[1:2], -1)
    source = jnp.concatenate([pos_ref[1], cot_ref[...]], axis=1)
    at = iota((16, total), 0)
    rows = jnp.where(at == 0, meta[2:3], jnp.where(at == 1, meta[3:4], 0)).astype(F32).astype(BF16)
    spot = iota((cap, total), 0)
    for d in range(strips):
        hot = (spot + d * cap == place).astype(F32).astype(BF16)
        out_ref[d, :cap, :] = dot(hot, source).astype(BF16)
        out_ref[d, cap:, :] = jnp.zeros((16, 256), BF16)
        out_ref[d, cap:, :cap] = dot_nt(rows, hot).astype(BF16)


def fetch_kernel(place_ref, rows_ref, out_ref):
    total = out_ref.shape[0]
    buffer_rows = rows_ref.shape[0]
    at = iota((BLK, buffer_rows), 1)
    for b in range(total // BLK):
        sl = slice(b * BLK, (b + 1) * BLK)
        col = column(place_ref[:, sl].astype(F32)).astype(I32)
        wide = jnp.concatenate([col] * (buffer_rows // BLK), axis=1)
        hot = (wide == at).astype(F32).astype(BF16)
        out_ref[sl, :] = dot(hot, rows_ref[...]).astype(BF16)


def local(
    features, position, cotangent, w_qkv, w_out, w_up, w_down, b_up, gains, shifts,
    window, shifted_window, dest, slot, valid,
):
    strips = lax.axis_size("strip")
    devices = strips * lax.axis_size("sub")
    rows, width = features.shape
    cap = 2 * rows // strips
    buffer_rows = strips * cap
    weights = (w_qkv, w_out, w_up, w_down, b_up, gains, shifts)
    spec = pl.BlockSpec(memory_space=pltpu.VMEM)
    params = pltpu.CompilerParams(vmem_limit_bytes=VMEM)

    send = pl.pallas_call(
        functools.partial(send_kernel, cap),
        out_shape=jax.ShapeDtypeStruct((strips, cap + 16, 2 * width), BF16),
        in_specs=[spec] * 3,
        out_specs=spec,
        compiler_params=params,
        name="send",
    )(jnp.stack([dest, slot, shifted_window, valid]), position, cotangent)
    arrived = lax.all_to_all(send, "strip", split_axis=0, concat_axis=0, tiled=True)

    meta_zero = jnp.stack([window, valid, dest, slot])
    message = run_layer("fwd", 0, cap, buffer_rows, meta_zero, features, position, *weights)
    moved = lax.all_to_all(message, "strip", split_axis=0, concat_axis=0, tiled=True)

    meta_one = arrived[:, cap : cap + 2, :cap].transpose(1, 0, 2).reshape(2, buffer_rows).astype(F32)
    rest = arrived[:, :cap].reshape(buffer_rows, 2 * width)
    back, grads_one = run_layer("mid", 1, cap, buffer_rows, meta_one, rest, moved, *weights)
    returned = lax.all_to_all(back, "strip", split_axis=0, concat_axis=0, tiled=True)

    grad_features, grads_zero = run_layer(
        "bwd", 0, cap, buffer_rows, meta_zero, features, position, returned[:, width:], *weights
    )
    place = jnp.where(valid > 0, dest * cap + slot, -1)[None]
    output = pl.pallas_call(
        fetch_kernel,
        out_shape=jax.ShapeDtypeStruct((rows, width), BF16),
        in_specs=[spec] * 2,
        out_specs=spec,
        compiler_params=params,
        name="fetch",
    )(place, returned[:, :width])

    both = jnp.concatenate([grads_zero, grads_one], axis=0)
    share = -(-both.shape[0] // (8 * devices)) * 8
    both = jnp.pad(both, ((0, share * devices - both.shape[0]), (0, 0)))
    axes = ("strip", "sub")
    parts = lax.all_to_all(both, axes, split_axis=0, concat_axis=0, tiled=True)
    mine = jnp.sum(parts.reshape(devices, share, width).astype(F32), axis=0).astype(BF16)
    whole = lax.all_to_all(
        jnp.tile(mine, (devices, 1)), axes, split_axis=0, concat_axis=0, tiled=True
    ).astype(F32)
    sums = whole[: 2 * GRAD_ROWS].reshape(2, GRAD_ROWS, width)
    wide = lambda lo, n: jnp.concatenate(
        [sums[:, lo + i * BLK : lo + (i + 1) * BLK] for i in range(n)], axis=2
    )
    return (
        output,
        grad_features,
        wide(0, 3),
        sums[:, 384:512],
        wide(512, 2),
        sums[:, 768:1024],
        sums[:, 1030:1032].reshape(2, 256),
        sums[:, 1024:1026],
        sums[:, 1026:1030],
    )


def solution(mesh):
    rows = P(("strip", "sub"), None)
    flat = P(("strip", "sub"))
    placed = (rows, P(None, ("strip", "sub"), None), rows) + (P(),) * 7 + (flat,) * 5
    return jax.shard_map(
        local,
        mesh=mesh,
        in_specs=placed,
        out_specs=(rows, rows) + (P(),) * 7,
        check_vma=False,
    )
```

```python
import functools
import types

import jax
import jax.numpy as jnp
from jax import lax
from jax.experimental import pallas as pl
from jax.experimental.pallas import tpu as pltpu
from jax.sharding import PartitionSpec as P

HEADS = 8
EPS = 1e-05
NEGATIVE = -1e30
BLK = 128
BPC = 4
CH = BPC * BLK
WINDOWS = 64
BINS = 4
VMEM = 60 * 1024 * 1024
F32, BF16, I32 = jnp.float32, jnp.bfloat16, jnp.int32
GRAD_ROWS = 1040
GELU_A = 0.7978845608028654
GELU_B = 0.044715


def dot(a, b):
    return lax.dot_general(a, b, (((1,), (0,)), ((), ())), preferred_element_type=F32)


def dot_nt(a, b):
    return lax.dot_general(a, b, (((1,), (1,)), ((), ())), preferred_element_type=F32)


def flip(x):
    return jnp.transpose(x.astype(F32)).astype(BF16)


def iota(shape, dim):
    return lax.broadcasted_iota(I32, shape, dim)


def as_hot(mask):
    return mask.astype(F32).astype(BF16)


def column(row):
    return jnp.transpose(jnp.broadcast_to(row, (BLK, BLK)))


def spread(x):
    return jnp.concatenate([x] * BPC, axis=1)


def block(b):
    return slice(b * BLK, (b + 1) * BLK)


def counted(hot, groups):
    blocks = hot.shape[1] // BLK
    low = hot.astype(BF16)
    stacked = jnp.concatenate([low[:, block(b)] for b in range(blocks)], axis=0)
    row_at, col_at = iota((BLK, 2 * BLK), 0), iota((BLK, 2 * BLK), 1)
    sums = dot(stacked, as_hot((row_at < col_at) | (col_at >= BLK)))
    carry = jnp.zeros((groups, BLK), F32)
    before = []
    for b in range(blocks):
        part = sums[b * groups : (b + 1) * groups]
        before.append(part[:, :BLK] + carry)
        carry = carry + part[:, BLK:]
    return before, carry


def take_seats(win, live, scal_ref, cnt_ref, start_ref, seat_ref, pcol_ref):
    total = win.shape[1]
    hot = (iota((WINDOWS, total), 0) == jnp.where(live, win, -1)).astype(F32)
    before, carry = counted(hot, WINDOWS)
    counts = carry.astype(I32)
    cnt_ref[...] = counts
    zero = jnp.zeros((8, BLK), I32)
    rooms, ends = [zero] * BINS, [zero] * BINS
    fresh, largest = zero, zero
    sub = iota((8, BLK), 0)
    for g in range(WINDOWS // 8):
        tile = zero
        for i in range(8):
            w = 8 * g + i
            count = jnp.broadcast_to(counts[w : w + 1, :], (8, BLK))
            fits = [count <= r for r in rooms]
            start, free = fresh, None
            for k in reversed(range(BINS)):
                start = jnp.where(fits[k], ends[k], start)
            tile = jnp.where(sub == i, start, tile)
            taken = jnp.zeros((8, BLK), jnp.bool_)
            next_rooms, next_ends = [], []
            for k in range(BINS):
                here = fits[k] & jnp.logical_not(taken)
                taken = taken | fits[k]
                gone = jnp.where(here, count, 0)
                next_rooms.append(rooms[k] - gone)
                next_ends.append(ends[k] + gone)
            room_new = (-count) & (BLK - 1)
            end_new = fresh + count
            shifted_rooms = rooms[1:] + [room_new]
            shifted_ends = ends[1:] + [end_new]
            rooms = [jnp.where(taken, a, b) for a, b in zip(next_rooms, shifted_rooms)]
            ends = [jnp.where(taken, a, b) for a, b in zip(next_ends, shifted_ends)]
            fresh = jnp.where(taken, fresh, end_new + room_new)
            largest = jnp.maximum(largest, count)
        start_ref[8 * g : 8 * g + 8, :] = tile
    starts = start_ref[...].astype(F32)
    for b in range(total // BLK):
        seat = jnp.sum(hot[:, block(b)] * (before[b] + starts), axis=0, keepdims=True)
        seat = jnp.where(live[:, block(b)], seat, -1.0)
        seat_ref[:, block(b)] = jnp.broadcast_to(seat, (8, BLK)).astype(I32)
        pcol_ref[block(b), :] = column(seat).astype(I32)
    several = jnp.max(largest) > BLK
    scal_ref[0] = (jnp.max(fresh) + (CH - 1)) // CH
    scal_ref[1] = several.astype(I32)

    @pl.when(several)
    def _():
        at = iota((WINDOWS, BLK), 1)
        count, start = cnt_ref[...], start_ref[...]
        first = lax.shift_right_logical(start, 7)
        final = lax.shift_right_logical(start + jnp.maximum(count, 1) - 1, 7)
        touch = (count > 0) & (first <= at) & (at <= final)
        low_at = jnp.min(jnp.where(touch, first, at), axis=0, keepdims=True)
        high_at = jnp.max(jnp.where(touch, final, at), axis=0, keepdims=True)
        for b in range((scal_ref.shape[0] - 2) // 2):
            scal_ref[2 + 2 * b] = jnp.max(jnp.where(at[0:1] == b, low_at, 0))
            scal_ref[3 + 2 * b] = jnp.max(jnp.where(at[0:1] == b, high_at, 0))


def picked(pcol_ref, c):
    seat = iota((BLK, BLK), 1) + c * CH
    total = pcol_ref.shape[0]
    return jnp.concatenate(
        [
            jnp.concatenate([as_hot(pcol_ref[block(b), :] == seat + t * BLK) for t in range(BPC)], axis=1)
            for b in range(total // BLK)
        ],
        axis=0,
    )


def norm_forward(hidden, gain, shift):
    size = hidden.shape[0]
    average = jnp.sum(hidden, axis=0, keepdims=True) * (1.0 / size)
    centered = hidden - average
    inverse = lax.rsqrt(jnp.sum(centered * centered, axis=0, keepdims=True) * (1.0 / size) + EPS)
    normed = centered * inverse
    return normed * gain + shift, normed, inverse


def norm_backward(upstream, normed, inverse, gain):
    size = upstream.shape[0]
    scaled = upstream * gain
    center = jnp.sum(scaled, axis=0, keepdims=True) * (1.0 / size)
    along = jnp.sum(scaled * normed, axis=0, keepdims=True) * (1.0 / size)
    return inverse * (scaled - center - normed * along)


def tiles(x):
    return x.reshape(x.shape[0] // 8, 8, x.shape[1])


def own_heads(x):
    size = x.shape[0] // HEADS
    return jnp.concatenate([x[h * size : (h + 1) * size, block(h)] for h in range(HEADS)], axis=0)


def whole_rows(x):
    return jnp.broadcast_to(x, (8, x.shape[1]))


def put_heads(ref, t, at, x):
    size = x.shape[0] // HEADS
    for h in range(HEADS):
        ref[t, at + h * size : at + (h + 1) * size, block(h)] = x[h * size : (h + 1) * size]


def setup_weights(s, level):
    s.stack[...] = jnp.zeros(s.stack.shape, BF16)
    for b in range(3):
        s.wqkvt[block(b), :] = flip(s.w_qkv[level, :, block(b)])
    s.woutt[...] = flip(s.w_out[level])
    for b in range(2):
        s.wupt[block(b), :] = flip(s.w_up[level, :, block(b)])
        s.wdownt[:, block(b)] = flip(s.w_down[level, block(b), :])
        s.cols[6 + b] = column(s.b_up[level : level + 1, block(b)])
        s.cols[b] = column(s.gains[level, b : b + 1, :])
    for b in range(4):
        s.cols[2 + b] = column(s.shifts[level, b : b + 1, :])


def project(s, c, low, placing, ids):
    width = low.shape[0]
    head = width // HEADS
    joined = (low.astype(F32) + placing).astype(BF16)
    s.xt[c] = low
    s.ut[c] = joined
    qk = dot(s.wqkvt[: 2 * width], joined).astype(BF16).astype(F32)
    vt = dot(s.wqkvt[2 * width :], low).astype(BF16).astype(F32)
    s.qt[c] = (qk[:width] * (head ** (-0.5))).astype(BF16)
    kt = qk[width:]
    same = iota((BLK, CH), 0) == ids.astype(I32)
    s.mt[c] = jnp.where(same, 0.0, NEGATIVE).astype(BF16)
    hot = same.astype(F32)
    ones = jnp.ones((head, BLK), BF16)
    unit = as_hot(iota((BLK, BLK), 1) < 2)
    for t in range(BPC):
        b = BPC * c + t
        s.kt[b] = kt[:, block(t)].astype(BF16)
        for h in range(HEADS):
            s.vt[b, 2 * h * head : (2 * h + 1) * head, :] = vt[h * head : (h + 1) * head, block(t)].astype(BF16)
            s.vt[b, (2 * h + 1) * head : (2 * h + 2) * head, :] = ones
        s.k[b, :, :width] = jnp.transpose(kt[:, block(t)]).astype(BF16)
        s.k[b, :, width:] = jnp.transpose(hot[:, block(t)]).astype(BF16)
        if s.backward:
            s.v[b, :, :width] = jnp.transpose(vt[:, block(t)]).astype(BF16)
            s.v[b, :, width:] = unit
            s.dk[b] = jnp.zeros((BLK, width), F32)
            s.dv[b] = jnp.zeros((BLK, width), F32)


def attend(s, c, single):
    qt, mt = s.qt[c], s.mt[c]
    width = qt.shape[0]
    head = width // HEADS
    mixed, inverses = [], []
    for t in range(BPC):
        b = BPC * c + t
        put_heads(s.stack, t, 0, qt[:, block(t)])
        for h in range(HEADS):
            s.stack[t, width : 2 * width, block(h)] = mt[:, block(t)]
        if single:
            scores = dot(s.k[b], s.stack[t, : 2 * width])
            sums = []
            for h in range(HEADS):
                part = scores[:, block(h)]
                top = jnp.max(part, axis=0, keepdims=True)
                e = jnp.exp(part - top).astype(BF16)
                if s.backward:
                    s.e[t, :, block(h)] = e
                sums.append(dot(s.vt[b, 2 * h * head : (2 * h + 2) * head, :], e))
        else:
            lo, hi = s.scal[2 + 2 * b], s.scal[3 + 2 * b] + 1

            def step_top(j, top, t=t):
                return jnp.maximum(top, jnp.max(tiles(dot(s.k[j], s.stack[t, : 2 * width])), axis=0))

            top = lax.fori_loop(lo, hi, step_top, jnp.full((8, HEADS * BLK), 2 * NEGATIVE, F32))
            s.stat[t] = whole_rows(jnp.max(top, axis=0, keepdims=True))

            def step_mix(j, out, t=t):
                e = weights_of(s, j, t)
                return out + own_heads(dot(s.vt[j], e))

            out = lax.fori_loop(lo, hi, step_mix, jnp.zeros((2 * width, BLK), F32))
            sums = [out[2 * h * head : (2 * h + 2) * head] for h in range(HEADS)]
        inverse = [1.0 / x[head : head + 1] for x in sums]
        mixed.append(jnp.concatenate([x[:head] * i for x, i in zip(sums, inverse)], axis=0))
        inverses.append(inverse)
    return jnp.concatenate(mixed, axis=1), inverses


def weights_of(s, j, t):
    scores = dot(s.k[j], s.stack[t, : s.k.shape[2]])
    return jnp.exp(tiles(scores) - s.stat[t][None]).reshape(BLK, HEADS * BLK).astype(BF16)


def attend_back(s, c, single, mixed, inverses, mixed_grad):
    width = mixed.shape[0]
    head = width // HEADS
    at = iota((head, BLK), 0)
    for t in range(BPC):
        b = BPC * c + t
        base = 2 * width
        for h in range(HEADS):
            rows = slice(h * head, (h + 1) * head)
            pull = (mixed_grad[rows, block(t)] * inverses[t][h]).astype(BF16)
            level = -jnp.sum(pull.astype(F32) * mixed[rows, block(t)], axis=0, keepdims=True)
            high = level.astype(BF16).astype(F32)
            tail = jnp.where(at == 0, high, jnp.where(at == 1, level - high, 0.0)).astype(BF16)
            s.stack[t, base + h * head : base + (h + 1) * head, block(h)] = pull
            s.stack[t, base + width : base + width + head, block(h)] = tail
        if single:
            slopes = dot(s.v[b], s.stack[t, base:])
            grads, parts = [], []
            for h in range(HEADS):
                g = (s.e[t, :, block(h)].astype(F32) * slopes[:, block(h)]).astype(BF16)
                grads.append(g)
                parts.append(dot(s.kt[b, h * head : (h + 1) * head, :], g))
            s.dv[b] = dot_nt(s.e[t], s.stack[t, base : base + width])
            s.dk[b] = dot_nt(jnp.concatenate(grads, axis=1), s.stack[t, :width])
            dq = jnp.concatenate(parts, axis=0)
        else:
            lo, hi = s.scal[2 + 2 * b], s.scal[3 + 2 * b] + 1

            def step(j, dq, t=t):
                e = weights_of(s, j, t)
                slopes = dot(s.v[j], s.stack[t, base:])
                g = (e.astype(F32) * slopes).astype(BF16)
                s.dv[j] += dot_nt(e, s.stack[t, base : base + width])
                s.dk[j] += dot_nt(g, s.stack[t, :width])
                return dq + own_heads(dot(s.kt[j], g))

            dq = lax.fori_loop(lo, hi, step, jnp.zeros((width, BLK), F32))
        s.dq[c, :, block(t)] = (dq * (head ** (-0.5))).astype(BF16)


def fold(x):
    return sum(x[:, block(t)] for t in range(BPC))


def layer_chunk(s, level, c, single, upstream_of):
    mixed, inverses = attend(s, c, single)
    mixed_low = mixed.astype(BF16)
    gain_one, gain_two = spread(s.cols[0]), spread(s.cols[1])
    attended = dot(s.woutt[...], mixed_low) + spread(s.cols[2])
    first_out, normed_one, inverse_one = norm_forward(
        s.xt[c].astype(F32) + attended, gain_one, spread(s.cols[3])
    )
    first_low = first_out.astype(BF16)
    bias_up = jnp.concatenate([spread(s.cols[6]), spread(s.cols[7])], axis=0)
    before = dot(s.wupt[...], first_low) + bias_up
    square = before * before
    bend = jnp.tanh(before * (GELU_A + (GELU_A * GELU_B) * square))
    half = 0.5 + 0.5 * bend
    activated = (before * half).astype(BF16)
    branch = dot(s.wdownt[...], activated) + spread(s.cols[4])
    result, normed_two, inverse_two = norm_forward(first_out + branch, gain_two, spread(s.cols[5]))
    if upstream_of is None:
        return result.astype(BF16)
    upstream = upstream_of(c)
    ones = jnp.ones((16, CH), BF16)
    s.gg[0] += fold(upstream * normed_two)
    s.gg[1] += fold(upstream)
    second = norm_backward(upstream, normed_two, inverse_two, gain_two)
    branch_low = second.astype(BF16)
    s.gd[...] += dot_nt(jnp.concatenate([activated, ones], axis=0), branch_low)
    slope = half + half * (1.0 - bend) * before * (GELU_A + (3.0 * GELU_A * GELU_B) * square)
    before_low = (dot(s.w_down[level], branch_low) * slope).astype(BF16)
    s.gu[...] += dot_nt(jnp.concatenate([first_low, ones], axis=0), before_low)
    first_grad = second + dot(s.w_up[level], before_low)
    s.gg[2] += fold(first_grad * normed_one)
    s.gg[3] += fold(first_grad)
    residual = norm_backward(first_grad, normed_one, inverse_one, gain_one)
    s.dh[c] = residual
    attended_low = residual.astype(BF16)
    s.go[...] += dot_nt(jnp.concatenate([mixed_low, ones], axis=0), attended_low)
    attend_back(s, c, single, mixed, inverses, dot(s.w_out[level], attended_low))
    return result.astype(BF16)


def finish_chunk(s, level, c):
    width = s.xt.shape[1]
    dq = s.dq[c]
    dk = jnp.concatenate([s.dk[BPC * c + t] for t in range(BPC)], axis=0).astype(BF16)
    dv = jnp.concatenate([s.dv[BPC * c + t] for t in range(BPC)], axis=0).astype(BF16)
    dx = (
        s.dh[c]
        + dot(s.w_qkv[level, :, :width], dq)
        + dot_nt(s.w_qkv[level, :, width : 2 * width], dk)
        + dot_nt(s.w_qkv[level, :, 2 * width :], dv)
    )
    joined = s.ut[c]
    s.gq[0] += dot_nt(joined, dq)
    s.gq[1] += dot(joined, dk)
    s.gq[2] += dot(s.xt[c], dv)
    return dx


def write_sums(s, wg_ref):
    width = s.xt.shape[1]
    for b in range(3):
        wg_ref[block(b), :] = s.gq[b].astype(BF16)
    wg_ref[384:512, :] = s.go[:width].astype(BF16)
    for b in range(2):
        wg_ref[512 + b * BLK : 640 + b * BLK, :] = s.gu[:width, block(b)].astype(BF16)
    wg_ref[768:1024, :] = s.gd[:256].astype(BF16)
    sums = [jnp.sum(jnp.transpose(s.gg[i]), axis=0, keepdims=True) for i in range(4)]
    out_bias, down_bias = s.go[width : width + 1], s.gd[256:257]
    up_bias = s.gu[width : width + 1]
    small = [
        sums[2], sums[0], out_bias, sums[3], down_bias, sums[1], up_bias[:, :BLK], up_bias[:, BLK:],
        jnp.zeros((8, BLK), F32),
    ]
    wg_ref[1024:GRAD_ROWS, :] = jnp.concatenate(small, axis=0).astype(BF16)


def zero_sums(s):
    for ref in (s.gq, s.go, s.gu, s.gd, s.gg):
        ref[...] = jnp.zeros(ref.shape, F32)


WEIGHTS = ("w_qkv", "w_out", "w_up", "w_down", "b_up", "gains", "shifts")


def layer_scratch(nc, backward):
    vm = pltpu.VMEM
    nb, width = nc * BPC, 128
    out = dict(
        wqkvt=vm((384, width), BF16), woutt=vm((width, width), BF16), wupt=vm((256, width), BF16),
        wdownt=vm((width, 256), BF16), cols=vm((8, BLK, BLK), F32),
        xt=vm((nc, width, CH), BF16), ut=vm((nc, width, CH), BF16), qt=vm((nc, width, CH), BF16),
        mt=vm((nc, BLK, CH), BF16), kt=vm((nb, width, BLK), BF16), vt=vm((nb, 2 * width, BLK), BF16),
        k=vm((nb, BLK, 2 * width), BF16),
        stat=vm((BPC, 8, HEADS * BLK), F32), stack=vm((BPC, 4 * width, HEADS * BLK), BF16),
    )
    if backward:
        out.update(
            v=vm((nb, BLK, 2 * width), BF16), e=vm((BPC, BLK, HEADS * BLK), BF16),
            dh=vm((nc, width, CH), F32), dq=vm((nc, width, CH), BF16),
            dk=vm((nb, BLK, width), F32), dv=vm((nb, BLK, width), F32),
            gq=vm((3, width, width), F32), go=vm((width + 16, width), F32), gu=vm((width + 16, 256), F32),
            gd=vm((256 + 16, width), F32), gg=vm((4, width, BLK), F32),
        )
    return out


def seat_scratch(total):
    return dict(
        cnt=pltpu.VMEM((WINDOWS, BLK), I32), start=pltpu.VMEM((WINDOWS, BLK), I32)
    )


def call(body, name, ins, outs, scratch):
    names = list(ins) + list(outs) + list(scratch)

    def kernel(*refs):
        body(types.SimpleNamespace(**dict(zip(names, refs))))

    vmem, smem = pl.BlockSpec(memory_space=pltpu.VMEM), pl.BlockSpec(memory_space=pltpu.SMEM)
    result = pl.pallas_call(
        kernel,
        out_shape=tuple(outs.values()),
        in_specs=[smem if n == "scal" else vmem for n in ins],
        out_specs=tuple(smem if n == "scal" else vmem for n in outs),
        scratch_shapes=list(scratch.values()),
        compiler_params=pltpu.CompilerParams(vmem_limit_bytes=VMEM),
        name=name,
    )(*ins.values())
    return dict(zip(outs, result))


def sds(shape, dtype):
    return jax.ShapeDtypeStruct(shape, dtype)


def chunks_of(total):
    return -(-total // (64 * BPC))


def for_chunks(s, body):
    @pl.loop(0, s.scal[0])
    def _(c):
        @pl.when(s.scal[1] == 0)
        def _():
            body(c, True)

        @pl.when(s.scal[1] != 0)
        def _():
            body(c, False)


def forward_zero(meta, features, position, weights, buffer_rows):
    total, width = features.shape
    nc = chunks_of(total)

    def body(s):
        s.backward = False
        meta = s.meta[...]
        live = meta[1:2] > 0
        take_seats(meta[0:1], live, s.scal, s.cnt, s.start, s.seat, s.pcol)
        for b in range(total // BLK):
            s.srct[:width, block(b)] = flip(s.features[block(b), :])
            s.srct[width : 2 * width, block(b)] = flip(s.position[0, block(b), :])
        at = iota((16, total), 0)
        place = meta[2:3]
        rows = jnp.where(at == 0, meta[0:1] + 1, jnp.where(at == 1, 1, 0))
        rows = jnp.where(at == 2, place >> 8, jnp.where(at == 3, place & 255, rows))
        s.srct[2 * width :, :] = rows.astype(F32).astype(BF16)
        setup_weights(s, 0)
        s.acc[...] = jnp.zeros(s.acc.shape, F32)

        @pl.loop(0, s.scal[0])
        def _(c):
            moved = dot(s.srct[...], picked(s.pcol, c))
            tags = moved[2 * width :]
            low = moved[:width].astype(BF16)
            s.xs[c] = low
            s.ps[c] = moved[width : 2 * width].astype(BF16)
            s.ids[c] = jnp.broadcast_to(tags[0:1], (8, CH))
            spot = jnp.where(tags[1:2] > 0.5, tags[2:3] * 256 + tags[3:4], -1.0)
            s.spot[c] = jnp.broadcast_to(spot, (8, CH)).astype(I32)
            for t in range(BPC):
                s.spotcol[BPC * c + t] = column(spot[:, block(t)]).astype(I32)
            project(s, c, low, moved[width : 2 * width], tags[0:1])

        def run(c, single):
            out = layer_chunk(s, 0, c, single, None)
            for r in range(buffer_rows // CH):
                lanes = slice(r * CH, (r + 1) * CH)
                at = iota((BLK, CH), 1) + r * CH
                hot = jnp.concatenate(
                    [as_hot(jnp.concatenate([s.spotcol[BPC * c + t]] * BPC, axis=1) == at) for t in range(BPC)],
                    axis=0,
                )
                s.acc[:, lanes] += dot(out, hot)

        for_chunks(s, run)
        for r in range(buffer_rows // BLK):
            s.message[block(r), :] = jnp.transpose(s.acc[:, block(r)]).astype(BF16)

    ins = dict(meta=meta, features=features, position=position, **dict(zip(WEIGHTS, weights)))
    outs = dict(
        message=sds((buffer_rows, width), BF16),
        xs=sds((nc, width, CH), BF16), ps=sds((nc, width, CH), BF16),
        ids=sds((nc, 8, CH), F32), spot=sds((nc, 8, CH), I32), seat=sds((8, total), I32),
        scal=sds((2 + 2 * nc * BPC,), I32),
    )
    scratch = dict(
        pcol=pltpu.VMEM((total, BLK), I32), srct=pltpu.VMEM((2 * width + 16, total), BF16),
        acc=pltpu.VMEM((width, buffer_rows), F32), spotcol=pltpu.VMEM((nc * BPC, BLK, BLK), I32),
        **seat_scratch(total), **layer_scratch(nc, False),
    )
    return call(body, "forward_zero", ins, outs, scratch)


def prepare_one(meta, rest):
    total, width = rest.shape[0], rest.shape[1] // 2
    nc = chunks_of(total)

    def body(s):
        meta = s.meta[...].astype(I32)
        live = meta[1:2] > 0
        take_seats(meta[0:1], live, s.scal, s.cnt, s.start, s.seat, s.pcol)
        for b in range(total // BLK):
            s.srct[: 2 * width, block(b)] = flip(s.rest[block(b), :])
        rows = jnp.where(iota((16, total), 0) == 0, meta[0:1] + 1, 0)
        s.srct[2 * width :, :] = rows.astype(F32).astype(BF16)

        @pl.loop(0, s.scal[0])
        def _(c):
            moved = dot(s.srct[...], picked(s.pcol, c))
            s.ps[c] = moved[:width].astype(BF16)
            s.dy[c] = moved[width : 2 * width].astype(BF16)
            s.ids[c] = jnp.broadcast_to(moved[2 * width : 2 * width + 1], (8, CH))

    outs = dict(
        ps=sds((nc, width, CH), BF16), dy=sds((nc, width, CH), BF16), ids=sds((nc, 8, CH), F32),
        seat=sds((8, total), I32), pcol=sds((total, BLK), I32), scal=sds((2 + 2 * nc * BPC,), I32),
    )
    scratch = dict(srct=pltpu.VMEM((2 * width + 16, total), BF16), **seat_scratch(total))
    return call(body, "prepare_one", dict(meta=meta, rest=rest), outs, scratch)


def scatter(s, c, pair):
    total = s.seat.shape[1]
    step = 256
    for r in range(total // step):
        lanes = slice(r * step, (r + 1) * step)
        seat = s.seat[0:1, lanes] - c * CH
        hot = as_hot(iota((CH, step), 0) == seat)
        s.acc[:, lanes] += dot(pair, hot)


def layer_one(ready, arrived, weights):
    total, width = arrived.shape
    nc = chunks_of(total)

    def body(s):
        s.backward = True
        for b in range(total // BLK):
            s.srct[:, block(b)] = flip(s.arrived[block(b), :])
        setup_weights(s, 1)
        zero_sums(s)
        s.acc[...] = jnp.zeros(s.acc.shape, F32)

        @pl.loop(0, s.scal[0])
        def _(c):
            low = dot(s.srct[...], picked(s.pcol, c)).astype(BF16)
            project(s, c, low, s.ps[c].astype(F32), s.ids[c][0:1])

        def run(c, single):
            s.yt[c] = layer_chunk(s, 1, c, single, lambda c: s.dy[c].astype(F32))

        for_chunks(s, run)

        @pl.loop(0, s.scal[0])
        def _(c):
            dx = finish_chunk(s, 1, c)
            scatter(s, c, jnp.concatenate([s.yt[c], dx.astype(BF16)], axis=0))

        for r in range(total // BLK):
            s.out[block(r), :] = jnp.transpose(s.acc[:width, block(r)]).astype(BF16)
            s.dx[block(r), :] = jnp.transpose(s.acc[width:, block(r)]).astype(BF16)
        write_sums(s, s.wg)

    ins = dict(
        {k: ready[k] for k in ("scal", "ps", "dy", "ids", "seat", "pcol")}, arrived=arrived,
        **dict(zip(WEIGHTS, weights)),
    )
    outs = dict(
        dx=sds((total, width), BF16), out=sds((total, width), BF16), wg=sds((GRAD_ROWS, width), BF16)
    )
    scratch = dict(
        srct=pltpu.VMEM((width, total), BF16), acc=pltpu.VMEM((2 * width, total), F32),
        yt=pltpu.VMEM((nc, width, CH), BF16), **layer_scratch(nc, True),
    )
    return call(body, "layer_one", ins, outs, scratch)


def layer_zero(ready, returned, weights):
    total, width = ready["seat"].shape[1], returned.shape[1]
    nc = chunks_of(total)
    buffer_rows = returned.shape[0]

    def body(s):
        s.backward = True
        for b in range(buffer_rows // BLK):
            s.srct[:, block(b)] = flip(s.returned[block(b), :])
        setup_weights(s, 0)
        zero_sums(s)
        s.acc[...] = jnp.zeros(s.acc.shape, F32)

        @pl.loop(0, s.scal[0])
        def _(c):
            project(s, c, s.xs[c], s.ps[c].astype(F32), s.ids[c][0:1])

        def upstream_of(c):
            return dot(s.srct[...], as_hot(iota((buffer_rows, CH), 0) == s.spot[c][0:1]))

        for_chunks(s, lambda c, single: layer_chunk(s, 0, c, single, upstream_of))

        @pl.loop(0, s.scal[0])
        def _(c):
            dx = finish_chunk(s, 0, c)
            high = dx.astype(BF16)
            scatter(s, c, jnp.concatenate([high, (dx - high.astype(F32)).astype(BF16)], axis=0))

        for r in range(total // BLK):
            s.grad[block(r), :] = jnp.transpose(s.acc[:width, block(r)] + s.acc[width:, block(r)])
        write_sums(s, s.wg)

    ins = dict(
        {k: ready[k] for k in ("scal", "xs", "ps", "ids", "spot", "seat")}, returned=returned,
        **dict(zip(WEIGHTS, weights)),
    )
    outs = dict(grad=sds((total, width), F32), wg=sds((GRAD_ROWS, width), BF16))
    scratch = dict(
        srct=pltpu.VMEM((width, buffer_rows), BF16), acc=pltpu.VMEM((2 * width, total), F32),
        **layer_scratch(nc, True),
    )
    return call(body, "layer_zero", ins, outs, scratch)


def send_rows(ints, position, cotangent, strips, cap):
    total, width = cotangent.shape

    def body(s):
        ints = s.ints[...]
        live = ints[1:2] > 0
        place = jnp.where(live, ints[2:3] * cap + ints[3:4], -1)
        s.meta[...] = jnp.concatenate([ints[0:2], place, jnp.zeros((5, total), I32)], axis=0)
        source = jnp.concatenate([s.position[1], s.cotangent[...]], axis=1)
        at = iota((16, total), 0)
        rows = jnp.where(at == 0, ints[4:5], jnp.where(at == 1, ints[1:2], 0)).astype(F32).astype(BF16)
        spot = iota((cap, total), 0)
        for d in range(strips):
            hot = as_hot(spot + d * cap == place)
            s.send[d, :cap, :] = dot(hot, source).astype(BF16)
            s.send[d, cap:, :] = jnp.zeros((16, 2 * width), BF16)
            s.send[d, cap:, :cap] = dot_nt(rows, hot).astype(BF16)

    ins = dict(ints=ints, position=position, cotangent=cotangent)
    outs = dict(send=sds((strips, cap + 16, 2 * width), BF16), meta=sds((8, total), I32))
    return call(body, "send_rows", ins, outs, {})


def fetch_rows(meta, rows):
    total = meta.shape[1]
    buffer_rows, width = rows.shape

    def body(s):
        at = iota((BLK, buffer_rows), 1)
        for b in range(total // BLK):
            col = column(s.meta[2:3, block(b)].astype(F32)).astype(I32)
            hot = as_hot(jnp.concatenate([col] * (buffer_rows // BLK), axis=1) == at)
            s.out[block(b), :] = dot(hot, s.rows[...]).astype(BF16)

    return call(body, "fetch_rows", dict(meta=meta, rows=rows), dict(out=sds((total, width), BF16)), {})["out"]


def local(
    features, position, cotangent, w_qkv, w_out, w_up, w_down, b_up, gains, shifts,
    window, shifted_window, dest, slot, valid,
):
    strips = lax.axis_size("strip")
    devices = strips * lax.axis_size("sub")
    rows, width = features.shape
    cap = 2 * rows // strips
    buffer_rows = strips * cap
    weights = (w_qkv, w_out, w_up, w_down, b_up, gains, shifts)

    def swap(x):
        return lax.all_to_all(x, "strip", split_axis=0, concat_axis=0, tiled=True)

    ints = jnp.stack([window, valid, dest, slot, shifted_window])
    sent = send_rows(ints, position, cotangent, strips, cap)
    arrived = swap(sent["send"])
    zero = forward_zero(sent["meta"], features, position, weights, buffer_rows)
    moved = swap(zero["message"])

    meta_one = arrived[:, cap : cap + 2, :cap].transpose(1, 0, 2).reshape(2, buffer_rows).astype(F32)
    ready = prepare_one(meta_one, arrived[:, :cap].reshape(buffer_rows, 2 * width))
    one = layer_one(ready, moved, weights)
    returned = swap(one["dx"])
    last = layer_zero(zero, returned, weights)
    output = fetch_rows(sent["meta"], swap(one["out"]))

    both = jnp.concatenate([last["wg"], one["wg"]], axis=0)
    share = -(-both.shape[0] // (8 * devices)) * 8
    both = jnp.pad(both, ((0, share * devices - both.shape[0]), (0, 0)))
    axes = ("strip", "sub")
    parts = lax.all_to_all(both, axes, split_axis=0, concat_axis=0, tiled=True)
    mine = jnp.sum(parts.reshape(devices, share, width).astype(F32), axis=0).astype(BF16)
    whole = lax.all_to_all(
        jnp.tile(mine, (devices, 1)), axes, split_axis=0, concat_axis=0, tiled=True
    ).astype(F32)
    sums = whole[: 2 * GRAD_ROWS].reshape(2, GRAD_ROWS, width)
    wide = lambda lo, n: jnp.concatenate(
        [sums[:, lo + i * BLK : lo + (i + 1) * BLK] for i in range(n)], axis=2
    )
    return (
        output,
        last["grad"],
        wide(0, 3),
        sums[:, 384:512],
        wide(512, 2),
        sums[:, 768:1024],
        sums[:, 1030:1032].reshape(2, 256),
        sums[:, 1024:1026],
        sums[:, 1026:1030],
    )


def solution(mesh):
    rows = P(("strip", "sub"), None)
    flat = P(("strip", "sub"))
    placed = (rows, P(None, ("strip", "sub"), None), rows) + (P(),) * 7 + (flat,) * 5
    return jax.shard_map(
        local,
        mesh=mesh,
        in_specs=placed,
        out_specs=(rows, rows) + (P(),) * 7,
        check_vma=False,
    )
```

```python
import functools
import types

import jax
import jax.numpy as jnp
from jax import lax
from jax.experimental import pallas as pl
from jax.experimental.pallas import tpu as pltpu
from jax.sharding import PartitionSpec as P

HEADS = 8
EPS = 1e-05
NEGATIVE = -1e30
BLK = 128
BPC = 4
CH = BPC * BLK
WINDOWS = 64
BINS = 4
VMEM = 60 * 1024 * 1024
F32, BF16, I32 = jnp.float32, jnp.bfloat16, jnp.int32
GRAD_ROWS = 1040
PART_ROWS = 272
HALF_ROWS = 4 * PART_ROWS
GELU_A = 0.7978845608028654
GELU_B = 0.044715


def dot(a, b):
    return lax.dot_general(a, b, (((1,), (0,)), ((), ())), preferred_element_type=F32)


def dot_nt(a, b):
    return lax.dot_general(a, b, (((1,), (1,)), ((), ())), preferred_element_type=F32)


def flip(x):
    return jnp.transpose(x.astype(F32)).astype(BF16)


def iota(shape, dim):
    return lax.broadcasted_iota(I32, shape, dim)


def as_hot(mask):
    return mask.astype(F32).astype(BF16)


def column(row):
    return jnp.transpose(jnp.broadcast_to(row, (BLK, BLK)))


def spread(x):
    return jnp.concatenate([x] * BPC, axis=1)


def block(b):
    return slice(b * BLK, (b + 1) * BLK)


def ranges(total, step):
    return [slice(at, min(at + step, total)) for at in range(0, total, step)]


def counted(hot, groups):
    blocks = hot.shape[1] // BLK
    low = hot.astype(BF16)
    stacked = jnp.concatenate([low[:, block(b)] for b in range(blocks)], axis=0)
    row_at, col_at = iota((BLK, 2 * BLK), 0), iota((BLK, 2 * BLK), 1)
    sums = dot(stacked, as_hot((row_at < col_at) | (col_at >= BLK)))
    carry = jnp.zeros((groups, BLK), F32)
    before = []
    for b in range(blocks):
        part = sums[b * groups : (b + 1) * groups]
        before.append(part[:, :BLK] + carry)
        carry = carry + part[:, BLK:]
    return before, carry


def take_seats(win, live, scal_ref, cnt_ref, start_ref, seat_ref, pcol_ref):
    total = win.shape[1]
    hot = (iota((WINDOWS, total), 0) == jnp.where(live, win, -1)).astype(F32)
    before, carry = counted(hot, WINDOWS)
    counts = carry.astype(I32)
    cnt_ref[...] = counts
    zero = jnp.zeros((8, BLK), I32)
    rooms, ends = [zero] * BINS, [zero] * BINS
    fresh, largest = zero, zero
    sub = iota((8, BLK), 0)
    for g in range(WINDOWS // 8):
        tile = zero
        for i in range(8):
            w = 8 * g + i
            count = jnp.broadcast_to(counts[w : w + 1, :], (8, BLK))
            fits = [count <= r for r in rooms]
            start, free = fresh, None
            for k in reversed(range(BINS)):
                start = jnp.where(fits[k], ends[k], start)
            tile = jnp.where(sub == i, start, tile)
            taken = jnp.zeros((8, BLK), jnp.bool_)
            next_rooms, next_ends = [], []
            for k in range(BINS):
                here = fits[k] & jnp.logical_not(taken)
                taken = taken | fits[k]
                gone = jnp.where(here, count, 0)
                next_rooms.append(rooms[k] - gone)
                next_ends.append(ends[k] + gone)
            room_new = (-count) & (BLK - 1)
            end_new = fresh + count
            shifted_rooms = rooms[1:] + [room_new]
            shifted_ends = ends[1:] + [end_new]
            rooms = [jnp.where(taken, a, b) for a, b in zip(next_rooms, shifted_rooms)]
            ends = [jnp.where(taken, a, b) for a, b in zip(next_ends, shifted_ends)]
            fresh = jnp.where(taken, fresh, end_new + room_new)
            largest = jnp.maximum(largest, count)
        start_ref[8 * g : 8 * g + 8, :] = tile
    starts = start_ref[...].astype(F32)
    for b in range(total // BLK):
        seat = jnp.sum(hot[:, block(b)] * (before[b] + starts), axis=0, keepdims=True)
        seat = jnp.where(live[:, block(b)], seat, -1.0)
        seat_ref[:, block(b)] = jnp.broadcast_to(seat, (8, BLK)).astype(I32)
        pcol_ref[block(b), :] = column(seat).astype(I32)
    several = jnp.max(largest) > BLK
    scal_ref[0] = (jnp.max(fresh) + (CH - 1)) // CH
    scal_ref[1] = several.astype(I32)

    @pl.when(several)
    def _():
        at = iota((WINDOWS, BLK), 1)
        count, start = cnt_ref[...], start_ref[...]
        first = lax.shift_right_logical(start, 7)
        final = lax.shift_right_logical(start + jnp.maximum(count, 1) - 1, 7)
        touch = (count > 0) & (first <= at) & (at <= final)
        low_at = jnp.min(jnp.where(touch, first, at), axis=0, keepdims=True)
        high_at = jnp.max(jnp.where(touch, final, at), axis=0, keepdims=True)
        for b in range((scal_ref.shape[0] - 3) // 2):
            scal_ref[2 + 2 * b] = jnp.max(jnp.where(at[0:1] == b, low_at, 0))
            scal_ref[3 + 2 * b] = jnp.max(jnp.where(at[0:1] == b, high_at, 0))


def picked(pcol_ref, c):
    seat = iota((BLK, BLK), 1) + c * CH
    total = pcol_ref.shape[0]
    return jnp.concatenate(
        [
            jnp.concatenate([as_hot(pcol_ref[block(b), :] == seat + t * BLK) for t in range(BPC)], axis=1)
            for b in range(total // BLK)
        ],
        axis=0,
    )


def norm_forward(hidden, gain, shift):
    size = hidden.shape[0]
    average = jnp.sum(hidden, axis=0, keepdims=True) * (1.0 / size)
    centered = hidden - average
    inverse = lax.rsqrt(jnp.sum(centered * centered, axis=0, keepdims=True) * (1.0 / size) + EPS)
    normed = centered * inverse
    return normed * gain + shift, normed, inverse


def norm_backward(upstream, normed, inverse, gain):
    size = upstream.shape[0]
    scaled = upstream * gain
    center = jnp.sum(scaled, axis=0, keepdims=True) * (1.0 / size)
    along = jnp.sum(scaled * normed, axis=0, keepdims=True) * (1.0 / size)
    return inverse * (scaled - center - normed * along)


def tiles(x):
    return x.reshape(x.shape[0] // 8, 8, x.shape[1])


def own_heads(x):
    size = x.shape[0] // HEADS
    return jnp.concatenate([x[h * size : (h + 1) * size, block(h)] for h in range(HEADS)], axis=0)


def whole_rows(x):
    return jnp.broadcast_to(x, (8, x.shape[1]))


def put_heads(ref, t, at, x):
    size = x.shape[0] // HEADS
    for h in range(HEADS):
        ref[t, at + h * size : at + (h + 1) * size, block(h)] = x[h * size : (h + 1) * size]


def setup_weights(s, level):
    s.stack[...] = jnp.zeros(s.stack.shape, BF16)
    for b in range(3):
        s.wqkvt[block(b), :] = flip(s.w_qkv[level, :, block(b)])
    s.woutt[...] = flip(s.w_out[level])
    for b in range(2):
        s.wupt[block(b), :] = flip(s.w_up[level, :, block(b)])
        s.wdownt[:, block(b)] = flip(s.w_down[level, block(b), :])
        s.cols[6 + b] = column(s.b_up[level : level + 1, block(b)])
        s.cols[b] = column(s.gains[level, b : b + 1, :])
    for b in range(4):
        s.cols[2 + b] = column(s.shifts[level, b : b + 1, :])


def project(s, c, low, placing, ids):
    width = low.shape[0]
    head = width // HEADS
    joined = (low.astype(F32) + placing).astype(BF16)
    s.xt[c] = low
    s.ut[c] = joined
    qk = dot(s.wqkvt[: 2 * width], joined).astype(BF16).astype(F32)
    vt = dot(s.wqkvt[2 * width :], low).astype(BF16).astype(F32)
    s.qt[c] = (qk[:width] * (head ** (-0.5))).astype(BF16)
    kt = qk[width:]
    same = iota((BLK, CH), 0) == ids.astype(I32)
    s.mt[c] = jnp.where(same, 0.0, NEGATIVE).astype(BF16)
    hot = same.astype(F32)
    ones = jnp.ones((head, BLK), BF16)
    unit = as_hot(iota((BLK, BLK), 1) < 2)
    for t in range(BPC):
        b = BPC * c + t
        s.kt[b] = kt[:, block(t)].astype(BF16)
        for h in range(HEADS):
            s.vt[b, 2 * h * head : (2 * h + 1) * head, :] = vt[h * head : (h + 1) * head, block(t)].astype(BF16)
            s.vt[b, (2 * h + 1) * head : (2 * h + 2) * head, :] = ones
        s.k[b, :, :width] = jnp.transpose(kt[:, block(t)]).astype(BF16)
        s.k[b, :, width:] = jnp.transpose(hot[:, block(t)]).astype(BF16)
        if s.backward:
            s.v[b, :, :width] = jnp.transpose(vt[:, block(t)]).astype(BF16)
            s.v[b, :, width:] = unit
            s.dk[b] = jnp.zeros((BLK, width), F32)
            s.dv[b] = jnp.zeros((BLK, width), F32)


def attend(s, c, single):
    qt, mt = s.qt[c], s.mt[c]
    width = qt.shape[0]
    head = width // HEADS
    mixed, inverses = [], []
    for t in range(BPC):
        b = BPC * c + t
        put_heads(s.stack, t, 0, qt[:, block(t)])
        for h in range(HEADS):
            s.stack[t, width : 2 * width, block(h)] = mt[:, block(t)]
        if single:
            scores = dot(s.k[b], s.stack[t, : 2 * width])
            sums = []
            for h in range(HEADS):
                part = scores[:, block(h)]
                top = jnp.max(part, axis=0, keepdims=True)
                e = jnp.exp(part - top).astype(BF16)
                if s.backward:
                    s.e[t, :, block(h)] = e
                sums.append(dot(s.vt[b, 2 * h * head : (2 * h + 2) * head, :], e))
        else:
            lo, hi = s.scal[2 + 2 * b], s.scal[3 + 2 * b] + 1

            def step_top(j, top, t=t):
                return jnp.maximum(top, jnp.max(tiles(dot(s.k[j], s.stack[t, : 2 * width])), axis=0))

            top = lax.fori_loop(lo, hi, step_top, jnp.full((8, HEADS * BLK), 2 * NEGATIVE, F32))
            s.stat[t] = whole_rows(jnp.max(top, axis=0, keepdims=True))

            def step_mix(j, out, t=t):
                e = weights_of(s, j, t)
                return out + own_heads(dot(s.vt[j], e))

            out = lax.fori_loop(lo, hi, step_mix, jnp.zeros((2 * width, BLK), F32))
            sums = [out[2 * h * head : (2 * h + 2) * head] for h in range(HEADS)]
        inverse = [1.0 / x[head : head + 1] for x in sums]
        mixed.append(jnp.concatenate([x[:head] * i for x, i in zip(sums, inverse)], axis=0))
        inverses.append(inverse)
    return jnp.concatenate(mixed, axis=1), inverses


def weights_of(s, j, t):
    scores = dot(s.k[j], s.stack[t, : s.k.shape[2]])
    return jnp.exp(tiles(scores) - s.stat[t][None]).reshape(BLK, HEADS * BLK).astype(BF16)


def attend_back(s, c, single, mixed, inverses, mixed_grad):
    width = mixed.shape[0]
    head = width // HEADS
    at = iota((head, BLK), 0)
    for t in range(BPC):
        b = BPC * c + t
        base = 2 * width
        for h in range(HEADS):
            rows = slice(h * head, (h + 1) * head)
            pull = (mixed_grad[rows, block(t)] * inverses[t][h]).astype(BF16)
            level = -jnp.sum(pull.astype(F32) * mixed[rows, block(t)], axis=0, keepdims=True)
            high = level.astype(BF16).astype(F32)
            tail = jnp.where(at == 0, high, jnp.where(at == 1, level - high, 0.0)).astype(BF16)
            s.stack[t, base + h * head : base + (h + 1) * head, block(h)] = pull
            s.stack[t, base + width : base + width + head, block(h)] = tail
        if single:
            slopes = dot(s.v[b], s.stack[t, base:])
            grads, parts = [], []
            for h in range(HEADS):
                g = (s.e[t, :, block(h)].astype(F32) * slopes[:, block(h)]).astype(BF16)
                grads.append(g)
                parts.append(dot(s.kt[b, h * head : (h + 1) * head, :], g))
            s.dv[b] = dot_nt(s.e[t], s.stack[t, base : base + width])
            s.dk[b] = dot_nt(jnp.concatenate(grads, axis=1), s.stack[t, :width])
            dq = jnp.concatenate(parts, axis=0)
        else:
            lo, hi = s.scal[2 + 2 * b], s.scal[3 + 2 * b] + 1

            def step(j, dq, t=t):
                e = weights_of(s, j, t)
                slopes = dot(s.v[j], s.stack[t, base:])
                g = (e.astype(F32) * slopes).astype(BF16)
                s.dv[j] += dot_nt(e, s.stack[t, base : base + width])
                s.dk[j] += dot_nt(g, s.stack[t, :width])
                return dq + own_heads(dot(s.kt[j], g))

            dq = lax.fori_loop(lo, hi, step, jnp.zeros((width, BLK), F32))
        s.dq[c, :, block(t)] = (dq * (head ** (-0.5))).astype(BF16)


def fold(x):
    return sum(x[:, block(t)] for t in range(BPC))


def layer_chunk(s, level, c, single, upstream_of):
    mixed, inverses = attend(s, c, single)
    mixed_low = mixed.astype(BF16)
    gain_one, gain_two = spread(s.cols[0]), spread(s.cols[1])
    attended = dot(s.woutt[...], mixed_low) + spread(s.cols[2])
    first_out, normed_one, inverse_one = norm_forward(
        s.xt[c].astype(F32) + attended, gain_one, spread(s.cols[3])
    )
    first_low = first_out.astype(BF16)
    bias_up = jnp.concatenate([spread(s.cols[6]), spread(s.cols[7])], axis=0)
    before = dot(s.wupt[...], first_low) + bias_up
    square = before * before
    bend = jnp.tanh(before * (GELU_A + (GELU_A * GELU_B) * square))
    half = 0.5 + 0.5 * bend
    activated = (before * half).astype(BF16)
    branch = dot(s.wdownt[...], activated) + spread(s.cols[4])
    result, normed_two, inverse_two = norm_forward(first_out + branch, gain_two, spread(s.cols[5]))
    if upstream_of is None:
        return result.astype(BF16)
    upstream = upstream_of(c)
    ones = jnp.ones((16, CH), BF16)
    s.gg[0] += fold(upstream * normed_two)
    s.gg[1] += fold(upstream)
    second = norm_backward(upstream, normed_two, inverse_two, gain_two)
    branch_low = second.astype(BF16)
    s.gd[...] += dot_nt(jnp.concatenate([activated, ones], axis=0), branch_low)
    slope = half + half * (1.0 - bend) * before * (GELU_A + (3.0 * GELU_A * GELU_B) * square)
    before_low = (dot(s.w_down[level], branch_low) * slope).astype(BF16)
    s.gu[...] += dot_nt(jnp.concatenate([first_low, ones], axis=0), before_low)
    first_grad = second + dot(s.w_up[level], before_low)
    s.gg[2] += fold(first_grad * normed_one)
    s.gg[3] += fold(first_grad)
    residual = norm_backward(first_grad, normed_one, inverse_one, gain_one)
    s.dh[c] = residual
    attended_low = residual.astype(BF16)
    s.go[...] += dot_nt(jnp.concatenate([mixed_low, ones], axis=0), attended_low)
    attend_back(s, c, single, mixed, inverses, dot(s.w_out[level], attended_low))
    return result.astype(BF16)


def finish_chunk(s, level, c):
    width = s.xt.shape[1]
    dq = s.dq[c]
    dk = jnp.concatenate([s.dk[BPC * c + t] for t in range(BPC)], axis=0).astype(BF16)
    dv = jnp.concatenate([s.dv[BPC * c + t] for t in range(BPC)], axis=0).astype(BF16)
    dx = (
        s.dh[c]
        + dot(s.w_qkv[level, :, :width], dq)
        + dot_nt(s.w_qkv[level, :, width : 2 * width], dk)
        + dot_nt(s.w_qkv[level, :, 2 * width :], dv)
    )
    joined = s.ut[c]
    s.gq[0] += dot_nt(joined, dq)
    s.gq[1] += dot(joined, dk)
    s.gq[2] += dot(s.xt[c], dv)
    return dx


def write_sums(s, wg_ref):
    width = s.xt.shape[1]
    for b in range(3):
        wg_ref[block(b), :] = s.gq[b].astype(BF16)
    wg_ref[384:512, :] = s.go[:width].astype(BF16)
    for b in range(2):
        wg_ref[512 + b * BLK : 640 + b * BLK, :] = s.gu[:width, block(b)].astype(BF16)
    wg_ref[768:1024, :] = s.gd[:256].astype(BF16)
    sums = [jnp.sum(jnp.transpose(s.gg[i]), axis=0, keepdims=True) for i in range(4)]
    out_bias, down_bias = s.go[width : width + 1], s.gd[256:257]
    up_bias = s.gu[width : width + 1]
    small = [
        sums[2], sums[0], out_bias, sums[3], down_bias, sums[1], up_bias[:, :BLK], up_bias[:, BLK:],
        jnp.zeros((8, BLK), F32),
    ]
    wg_ref[1024:GRAD_ROWS, :] = jnp.concatenate(small, axis=0).astype(BF16)


def zero_sums(s):
    for ref in (s.gq, s.go, s.gu, s.gd, s.gg):
        ref[...] = jnp.zeros(ref.shape, F32)


WEIGHTS = ("w_qkv", "w_out", "w_up", "w_down", "b_up", "gains", "shifts")


def layer_scratch(nc, backward):
    vm = pltpu.VMEM
    nb, width = nc * BPC, 128
    out = dict(
        wqkvt=vm((384, width), BF16), woutt=vm((width, width), BF16), wupt=vm((256, width), BF16),
        wdownt=vm((width, 256), BF16), cols=vm((8, BLK, BLK), F32),
        xt=vm((nc, width, CH), BF16), ut=vm((nc, width, CH), BF16), qt=vm((nc, width, CH), BF16),
        mt=vm((nc, BLK, CH), BF16), kt=vm((nb, width, BLK), BF16), vt=vm((nb, 2 * width, BLK), BF16),
        k=vm((nb, BLK, 2 * width), BF16),
        stat=vm((BPC, 8, HEADS * BLK), F32), stack=vm((BPC, 4 * width, HEADS * BLK), BF16),
    )
    if backward:
        out.update(
            v=vm((nb, BLK, 2 * width), BF16), e=vm((BPC, BLK, HEADS * BLK), BF16),
            dh=vm((nc, width, CH), F32), dq=vm((nc, width, CH), BF16),
            dk=vm((nb, BLK, width), F32), dv=vm((nb, BLK, width), F32),
            gq=vm((3, width, width), F32), go=vm((width + 16, width), F32), gu=vm((width + 16, 256), F32),
            gd=vm((256 + 16, width), F32), gg=vm((4, width, BLK), F32),
        )
    return out


def seat_scratch(total):
    return dict(
        cnt=pltpu.VMEM((WINDOWS, BLK), I32), start=pltpu.VMEM((WINDOWS, BLK), I32)
    )


def call(body, name, ins, outs, scratch):
    names = list(ins) + list(outs) + list(scratch)

    def kernel(*refs):
        body(types.SimpleNamespace(**dict(zip(names, refs))))

    vmem, smem = pl.BlockSpec(memory_space=pltpu.VMEM), pl.BlockSpec(memory_space=pltpu.SMEM)
    result = pl.pallas_call(
        kernel,
        out_shape=tuple(outs.values()),
        in_specs=[smem if n in ("scal", "who") else vmem for n in ins],
        out_specs=tuple(smem if n == "scal" else vmem for n in outs),
        scratch_shapes=list(scratch.values()),
        compiler_params=pltpu.CompilerParams(vmem_limit_bytes=VMEM),
        name=name,
    )(*ins.values())
    return dict(zip(outs, result))


def sds(shape, dtype):
    return jax.ShapeDtypeStruct(shape, dtype)


def chunks_of(total):
    return -(-total // (64 * BPC))


def for_chunks(s, body):
    @pl.loop(0, s.scal[0])
    def _(c):
        @pl.when(s.scal[1] == 0)
        def _():
            body(c, True)

        @pl.when(s.scal[1] != 0)
        def _():
            body(c, False)


def forward_zero(meta, features, position, weights, buffer_rows):
    total, width = features.shape
    nc = chunks_of(total)

    def body(s):
        s.backward = False
        meta = s.meta[...]
        live = meta[1:2] > 0
        take_seats(meta[0:1], live, s.scal, s.cnt, s.start, s.seat, s.pcol)
        for b in range(total // BLK):
            s.srct[:width, block(b)] = flip(s.features[block(b), :])
            s.srct[width : 2 * width, block(b)] = flip(s.position[0, block(b), :])
        at = iota((16, total), 0)
        place = meta[2:3]
        rows = jnp.where(at == 0, meta[0:1] + 1, jnp.where(at == 1, 1, 0))
        rows = jnp.where(at == 2, place >> 8, jnp.where(at == 3, place & 255, rows))
        s.srct[2 * width :, :] = rows.astype(F32).astype(BF16)
        setup_weights(s, 0)
        s.acc[...] = jnp.zeros(s.acc.shape, F32)

        @pl.loop(0, s.scal[0])
        def _(c):
            moved = dot(s.srct[...], picked(s.pcol, c))
            tags = moved[2 * width :]
            low = moved[:width].astype(BF16)
            s.xs[c] = low
            s.ps[c] = moved[width : 2 * width].astype(BF16)
            s.ids[c] = jnp.broadcast_to(tags[0:1], (8, CH))
            spot = jnp.where(tags[1:2] > 0.5, tags[2:3] * 256 + tags[3:4], -1.0)
            s.spot[c] = jnp.broadcast_to(spot, (8, CH)).astype(I32)
            for t in range(BPC):
                s.spotcol[BPC * c + t] = column(spot[:, block(t)]).astype(I32)
            project(s, c, low, moved[width : 2 * width], tags[0:1])

        def run(c, single):
            out = layer_chunk(s, 0, c, single, None)
            for lanes in ranges(buffer_rows, CH):
                copies = (lanes.stop - lanes.start) // BLK
                at = iota((BLK, copies * BLK), 1) + lanes.start
                hot = jnp.concatenate(
                    [
                        as_hot(jnp.concatenate([s.spotcol[BPC * c + t]] * copies, axis=1) == at)
                        for t in range(BPC)
                    ],
                    axis=0,
                )
                s.acc[:, lanes] += dot(out, hot)

        for_chunks(s, run)
        for r in range(buffer_rows // BLK):
            s.message[block(r), :] = jnp.transpose(s.acc[:, block(r)]).astype(BF16)

    ins = dict(meta=meta, features=features, position=position, **dict(zip(WEIGHTS, weights)))
    outs = dict(
        message=sds((buffer_rows, width), BF16),
        xs=sds((nc, width, CH), BF16), ps=sds((nc, width, CH), BF16),
        ids=sds((nc, 8, CH), F32), spot=sds((nc, 8, CH), I32), seat=sds((8, total), I32),
        scal=sds((3 + 2 * nc * BPC,), I32),
    )
    scratch = dict(
        pcol=pltpu.VMEM((total, BLK), I32), srct=pltpu.VMEM((2 * width + 16, total), BF16),
        acc=pltpu.VMEM((width, buffer_rows), F32), spotcol=pltpu.VMEM((nc * BPC, BLK, BLK), I32),
        **seat_scratch(total), **layer_scratch(nc, False),
    )
    return call(body, "forward_zero", ins, outs, scratch)


def prepare_one(meta, rest):
    total, width = rest.shape[0], rest.shape[1] // 2
    nc = chunks_of(total)

    def body(s):
        meta = s.meta[...].astype(I32)
        live = meta[1:2] > 0
        take_seats(meta[0:1], live, s.scal, s.cnt, s.start, s.seat, s.pcol)
        for b in range(total // BLK):
            s.srct[: 2 * width, block(b)] = flip(s.rest[block(b), :])
        s.scal[s.scal.shape[0] - 1] = jnp.max(meta[2:3])
        rows = jnp.where(iota((16, total), 0) == 0, meta[0:1] + 1, 0)
        s.srct[2 * width :, :] = rows.astype(F32).astype(BF16)

        @pl.loop(0, s.scal[0])
        def _(c):
            moved = dot(s.srct[...], picked(s.pcol, c))
            s.ps[c] = moved[:width].astype(BF16)
            s.dy[c] = moved[width : 2 * width].astype(BF16)
            s.ids[c] = jnp.broadcast_to(moved[2 * width : 2 * width + 1], (8, CH))

    outs = dict(
        ps=sds((nc, width, CH), BF16), dy=sds((nc, width, CH), BF16), ids=sds((nc, 8, CH), F32),
        seat=sds((8, total), I32), pcol=sds((total, BLK), I32), scal=sds((3 + 2 * nc * BPC,), I32),
    )
    scratch = dict(srct=pltpu.VMEM((2 * width + 16, total), BF16), **seat_scratch(total))
    return call(body, "prepare_one", dict(meta=meta, rest=rest), outs, scratch)


def scatter(s, c, pair):
    for lanes in ranges(s.seat.shape[1], 256):
        seat = s.seat[0:1, lanes] - c * CH
        hot = as_hot(iota((CH, lanes.stop - lanes.start), 0) == seat)
        s.acc[:, lanes] += dot(pair, hot)


def layer_one(ready, arrived, weights, strips, full):
    total, width = arrived.shape
    cap = total // strips
    nc = chunks_of(total)

    def body(s):
        s.backward = True
        for b in range(total // BLK):
            s.srct[:, block(b)] = flip(s.arrived[block(b), :])
        setup_weights(s, 1)
        zero_sums(s)
        s.acc[...] = jnp.zeros(s.acc.shape, F32)

        @pl.loop(0, s.scal[0])
        def _(c):
            low = dot(s.srct[...], picked(s.pcol, c)).astype(BF16)
            project(s, c, low, s.ps[c].astype(F32), s.ids[c][0:1])

        def run(c, single):
            s.yt[c] = layer_chunk(s, 1, c, single, lambda c: s.dy[c].astype(F32))

        for_chunks(s, run)

        @pl.loop(0, s.scal[0])
        def _(c):
            dx = finish_chunk(s, 1, c)
            scatter(s, c, jnp.concatenate([s.yt[c], dx.astype(BF16)], axis=0))

        for r in range(total // BLK):
            s.flat[block(r), :] = jnp.transpose(s.acc[:width, block(r)]).astype(BF16)
            s.dx[block(r), :] = jnp.transpose(s.acc[width:, block(r)]).astype(BF16)
        for d in range(strips):
            s.out[d, :cap, :] = s.flat[d * cap : (d + 1) * cap, :]
            if cap < full:
                s.out[d, cap:, :] = jnp.zeros((full - cap, width), BF16)
        write_sums(s, s.wg)

    ins = dict(
        {k: ready[k] for k in ("scal", "ps", "dy", "ids", "seat", "pcol")}, arrived=arrived,
        **dict(zip(WEIGHTS, weights)),
    )
    outs = dict(
        dx=sds((total, width), BF16), out=sds((strips, full, width), BF16), wg=sds((GRAD_ROWS, width), BF16)
    )
    scratch = dict(
        flat=pltpu.VMEM((total, width), BF16),
        srct=pltpu.VMEM((width, total), BF16), acc=pltpu.VMEM((2 * width, total), F32),
        yt=pltpu.VMEM((nc, width, CH), BF16), **layer_scratch(nc, True),
    )
    return call(body, "layer_one", ins, outs, scratch)


def layer_zero(ready, returned, weights, sums_one, who):
    total, width = ready["seat"].shape[1], returned.shape[1]
    nc = chunks_of(total)
    buffer_rows = returned.shape[0]

    def body(s):
        s.backward = True
        for b in range(buffer_rows // BLK):
            s.srct[:, block(b)] = flip(s.returned[block(b), :])
        setup_weights(s, 0)
        zero_sums(s)
        s.acc[...] = jnp.zeros(s.acc.shape, F32)

        @pl.loop(0, s.scal[0])
        def _(c):
            project(s, c, s.xs[c], s.ps[c].astype(F32), s.ids[c][0:1])

        def upstream_of(c):
            return dot(s.srct[...], as_hot(iota((buffer_rows, CH), 0) == s.spot[c][0:1]))

        for_chunks(s, lambda c, single: layer_chunk(s, 0, c, single, upstream_of))

        @pl.loop(0, s.scal[0])
        def _(c):
            dx = finish_chunk(s, 0, c)
            high = dx.astype(BF16)
            scatter(s, c, jnp.concatenate([high, (dx - high.astype(F32)).astype(BF16)], axis=0))

        for r in range(total // BLK):
            s.grad[block(r), :] = jnp.transpose(s.acc[:width, block(r)] + s.acc[width:, block(r)])
        write_sums(s, s.both)
        s.both[GRAD_ROWS : 2 * GRAD_ROWS, :] = s.sums_one[...]
        s.both[2 * GRAD_ROWS :, :] = jnp.zeros((2 * HALF_ROWS - 2 * GRAD_ROWS, width), BF16)
        start = pl.multiple_of(s.who[0] * HALF_ROWS, 16)
        s.keep[...] = s.both[pl.ds(start, HALF_ROWS), :]
        s.give[...] = s.both[pl.ds(pl.multiple_of(HALF_ROWS - start, 16), HALF_ROWS), :]

    ins = dict(
        {k: ready[k] for k in ("scal", "xs", "ps", "ids", "spot", "seat")}, returned=returned,
        sums_one=sums_one, who=who, **dict(zip(WEIGHTS, weights)),
    )
    half = sds((HALF_ROWS, width), BF16)
    outs = dict(grad=sds((total, width), F32), keep=half, give=half)
    scratch = dict(
        both=pltpu.VMEM((2 * HALF_ROWS, width), BF16),
        srct=pltpu.VMEM((width, buffer_rows), BF16), acc=pltpu.VMEM((2 * width, total), F32),
        **layer_scratch(nc, True),
    )
    return call(body, "layer_zero", ins, outs, scratch)


def send_rows(ints, position, cotangent, strips, cap, full, balanced):
    total, width = cotangent.shape

    def body(s):
        ints = s.ints[...]
        live, dest, slot, shifted = ints[1:2] > 0, ints[2:3], ints[3:4], ints[4:5]
        owner, key = dest, shifted
        if balanced:
            owner = (shifted + dest) & (strips - 1)
            key = dest * (WINDOWS // strips) + shifted // strips
            groups = max(strips, 16)
            hot = (iota((groups, total), 0) == jnp.where(live, owner, -1)).astype(F32)
            before, _ = counted(hot, groups)
            slot = jnp.concatenate(
                [
                    jnp.sum(hot[:, block(b)] * before[b], axis=0, keepdims=True)
                    for b in range(total // BLK)
                ],
                axis=1,
            ).astype(I32)
        fits = live & (slot < cap)
        over = jnp.max(jnp.where(live & (slot >= cap), 1, 0))
        place = jnp.where(fits, owner * cap + slot, -1)
        wide = jnp.where(fits, owner * full + slot, -1)
        s.meta[...] = jnp.concatenate([ints[0:2], place, wide, jnp.zeros((4, total), I32)], axis=0)
        source = jnp.concatenate([s.position[1], s.cotangent[...]], axis=1)
        at = iota((16, total), 0)
        rows = jnp.where(at == 0, key, jnp.where(at == 1, ints[1:2], 0)).astype(F32).astype(BF16)
        spot = iota((cap, total), 0)
        third = as_hot((iota((16, 2 * width), 0) == 2) & (over > 0))
        for d in range(strips):
            hot = as_hot(spot + d * cap == place)
            s.send[d, :cap, :] = dot(hot, source).astype(BF16)
            tags = dot_nt(rows, hot)
            if cap < 2 * width:
                tags = jnp.concatenate([tags, jnp.zeros((16, 2 * width - cap), F32)], axis=1)
            s.send[d, cap:, :] = tags.astype(BF16) + third

    ins = dict(ints=ints, position=position, cotangent=cotangent)
    outs = dict(send=sds((strips, cap + 16, 2 * width), BF16), meta=sds((8, total), I32))
    return call(body, "send_rows", ins, outs, {})


def fetch_rows(meta, rows):
    total = meta.shape[1]
    buffer_rows, width = rows.shape

    def body(s):
        at = iota((BLK, buffer_rows), 1)
        for b in range(total // BLK):
            col = column(s.meta[3:4, block(b)].astype(F32)).astype(I32)
            hot = as_hot(jnp.concatenate([col] * (buffer_rows // BLK), axis=1) == at)
            s.out[block(b), :] = dot(hot, s.rows[...]).astype(BF16)

    return call(body, "fetch_rows", dict(meta=meta, rows=rows), dict(out=sds((total, width), BF16)), {})["out"]


def cut_half(keep, got, who):
    def body(s):
        total = s.keep[...].astype(F32) + s.got[...].astype(F32)
        s.sums[...] = total.astype(BF16)
        for m, ref in enumerate((s.own, s.one, s.two, s.three)):
            start = pl.multiple_of((s.who[1] ^ m) * PART_ROWS, 16)
            ref[...] = s.sums[pl.ds(start, PART_ROWS), :]

    part = sds((PART_ROWS, keep.shape[1]), BF16)
    return call(
        body, "cut_half", dict(keep=keep, got=got, who=who), dict(own=part, one=part, two=part, three=part),
        dict(sums=pltpu.VMEM(keep.shape, BF16)),
    )


def unpack_sums(mine, other, who):
    width = mine.shape[1]

    def body(s):
        for a, ref in enumerate((s.mine, s.other)):
            for m in range(4):
                row = (s.who[0] ^ a) * HALF_ROWS + (s.who[1] ^ m) * PART_ROWS
                s.both[pl.ds(pl.multiple_of(row, 16), PART_ROWS), :] = ref[
                    m * PART_ROWS : (m + 1) * PART_ROWS, :
                ].astype(F32)
        for level in range(2):
            at = level * GRAD_ROWS
            for b in range(3):
                s.w_qkv[level, :, block(b)] = s.both[at + b * BLK : at + (b + 1) * BLK, :]
            s.w_out[level] = s.both[at + 384 : at + 512, :]
            for b in range(2):
                s.w_up[level, :, block(b)] = s.both[at + 512 + b * BLK : at + 640 + b * BLK, :]
                s.b_up[level : level + 1, block(b)] = s.both[at + 1030 + b : at + 1031 + b, :]
            s.w_down[level] = s.both[at + 768 : at + 1024, :]
            s.gains[level] = s.both[at + 1024 : at + 1026, :]
            s.shifts[level] = s.both[at + 1026 : at + 1030, :]

    outs = dict(
        w_qkv=sds((2, width, 384), F32), w_out=sds((2, width, width), F32), w_up=sds((2, width, 256), F32),
        w_down=sds((2, 256, width), F32), b_up=sds((2, 256), F32), gains=sds((2, 2, width), F32),
        shifts=sds((2, 4, width), F32),
    )
    done = call(
        body, "unpack_sums", dict(mine=mine, other=other, who=who), outs,
        dict(both=pltpu.VMEM((2 * HALF_ROWS, width), F32)),
    )
    return tuple(done[n] for n in WEIGHTS)


def paired_sum(parts):
    while len(parts) > 1:
        parts = [parts[i] + parts[i + 1] for i in range(0, len(parts), 2)]
    return parts[0]


def local(
    features, position, cotangent, w_qkv, w_out, w_up, w_down, b_up, gains, shifts,
    window, shifted_window, dest, slot, valid,
):
    strips, subs = lax.axis_size("strip"), lax.axis_size("sub")
    rows, width = features.shape
    full = 2 * rows // strips
    short = -(-(11 * full) // 256) * 16
    weights = (w_qkv, w_out, w_up, w_down, b_up, gains, shifts)

    def swap(x):
        return lax.all_to_all(x, "strip", split_axis=0, concat_axis=0, tiled=True)

    def trade(x, strip_mask, sub_mask):
        pairs = [
            (t * subs + u, (t ^ strip_mask) * subs + (u ^ sub_mask)) for t in range(strips) for u in range(subs)
        ]
        return lax.ppermute(x, ("strip", "sub"), pairs)

    at_strip, at_sub = lax.axis_index("strip"), lax.axis_index("sub")
    who = jnp.stack([at_sub & 1, ((at_sub >> 1) & 1) + 2 * (at_strip & 1)]).astype(I32)

    ints = jnp.stack([window, valid, dest, slot, shifted_window])

    def there(cap, balanced):
        sent = send_rows(ints, position, cotangent, strips, cap, full, balanced)
        arrived = swap(sent["send"])
        zero = forward_zero(sent["meta"], features, position, weights, strips * cap)
        moved = swap(zero["message"])
        tags = arrived[:, cap : cap + 3, :cap].transpose(1, 0, 2).reshape(3, strips * cap).astype(F32)
        ready = prepare_one(tags, arrived[:, :cap].reshape(strips * cap, 2 * width))
        return sent["meta"], zero, moved, ready

    def back(meta, zero, moved, ready):
        one = layer_one(ready, moved, weights, strips, full)
        returned = swap(one["dx"])
        out, sums_one, returned = lax.optimization_barrier((one["out"], one["wg"], returned))
        out = swap(out)
        last = layer_zero(zero, returned, weights, sums_one, who)
        return lax.optimization_barrier((last["keep"], last["give"], last["grad"], out, meta))

    first = there(short, True)
    over = first[3]["scal"][-1] > 0
    _, keep, give, grad, out, meta = lax.while_loop(
        lambda state: state[0], lambda _: (False, *back(*there(full, False))), (over, *back(*first))
    )

    square = ((0, 2), (1, 0), (1, 2))
    cut = cut_half(keep, trade(give, 0, 1), who)
    got = [trade(cut[n], *mask) for n, mask in zip(("one", "two", "three"), square)]
    part = paired_sum([x.astype(F32) for x in (cut["own"], *got)]).astype(BF16)
    got = [trade(part, m, 0) for m in range(2, strips, 2)]
    part = paired_sum([x.astype(F32) for x in (part, *got)]).astype(BF16)
    part, output = lax.optimization_barrier((part, fetch_rows(meta, out.reshape(strips * full, width))))
    mine = jnp.concatenate([part] + [trade(part, *mask) for mask in square], axis=0)
    return (output, grad) + unpack_sums(mine, trade(mine, 0, 1), who)


def solution(mesh):
    rows = P(("strip", "sub"), None)
    flat = P(("strip", "sub"))
    placed = (rows, P(None, ("strip", "sub"), None), rows) + (P(),) * 7 + (flat,) * 5
    return jax.shard_map(
        local,
        mesh=mesh,
        in_specs=placed,
        out_specs=(rows, rows) + (P(),) * 7,
        check_vma=False,
    )
```

```python
import functools
import types

import jax
import jax.numpy as jnp
from jax import lax
from jax.experimental import pallas as pl
from jax.experimental.pallas import tpu as pltpu
from jax.sharding import PartitionSpec as P

HEADS = 8
EPS = 1e-05
NEGATIVE = -1e30
BLK = 128
UNIT = 2
WIDE = 4
UL = UNIT * BLK
WINDOWS = 64
BINS = 4
PAIR = 2
VMEM = 60 * 1024 * 1024
F32, BF16, I32 = jnp.float32, jnp.bfloat16, jnp.int32
GRAD_ROWS = 1040
PART_ROWS = 272
HALF_ROWS = 4 * PART_ROWS
MICROS = dict(
    send_rows=4, forward_zero=9, layer_one=17, layer_zero=14, fetch_rows=3, cut_half=2, unpack_sums=2
)
GELU_A = 0.7978845608028654
GELU_B = 0.044715


def dot(a, b):
    return lax.dot_general(a, b, (((1,), (0,)), ((), ())), preferred_element_type=F32)


def dot_nt(a, b):
    return lax.dot_general(a, b, (((1,), (1,)), ((), ())), preferred_element_type=F32)


def flip(x):
    return jnp.transpose(x.astype(F32)).astype(BF16)


def iota(shape, dim):
    return lax.broadcasted_iota(I32, shape, dim)


def as_hot(mask):
    return mask.astype(F32).astype(BF16)


def column(row):
    return jnp.transpose(jnp.broadcast_to(row, (BLK, BLK)))


def spread(x, n):
    return jnp.concatenate([x] * (n * UNIT), axis=1)


def get(ref, u, n):
    return jnp.concatenate([ref[u + i] for i in range(n)], axis=1)


def put(ref, u, n, x):
    for i in range(n):
        ref[u + i] = x[:, i * UL : (i + 1) * UL]


def flat_row(x):
    return jnp.concatenate([x[i : i + 1] for i in range(x.shape[0])], axis=1)


def block(b):
    return slice(b * BLK, (b + 1) * BLK)


def ranges(total, step):
    return [slice(at, min(at + step, total)) for at in range(0, total, step)]


def counted(hot, groups):
    blocks = hot.shape[1] // BLK
    low = hot.astype(BF16)
    stacked = jnp.concatenate([low[:, block(b)] for b in range(blocks)], axis=0)
    row_at, col_at = iota((BLK, 2 * BLK), 0), iota((BLK, 2 * BLK), 1)
    sums = dot(stacked, as_hot((row_at < col_at) | (col_at >= BLK)))
    carry = jnp.zeros((groups, BLK), F32)
    before = []
    for b in range(blocks):
        part = sums[b * groups : (b + 1) * groups]
        before.append(part[:, :BLK] + carry)
        carry = carry + part[:, BLK:]
    return before, carry


def take_seats(win, live, windows, scal_ref, cnt_ref, start_ref, seat_ref, pcol_ref):
    total = win.shape[1]
    hot = (iota((windows, total), 0) == jnp.where(live, win, -1)).astype(F32)
    before, carry = counted(hot, windows)
    counts = carry.astype(I32)
    cnt_ref[...] = counts
    zero = jnp.zeros((8, BLK), I32)
    rooms, ends = [zero] * BINS, [zero] * BINS
    fresh, largest = zero, zero
    sub = iota((8, BLK), 0)
    for g in range(windows // 8):
        tile = zero
        for i in range(8):
            w = 8 * g + i
            count = jnp.broadcast_to(counts[w : w + 1, :], (8, BLK))
            fits = [count <= r for r in rooms]
            start, free = fresh, None
            for k in reversed(range(BINS)):
                start = jnp.where(fits[k], ends[k], start)
            tile = jnp.where(sub == i, start, tile)
            taken = jnp.zeros((8, BLK), jnp.bool_)
            next_rooms, next_ends = [], []
            for k in range(BINS):
                here = fits[k] & jnp.logical_not(taken)
                taken = taken | fits[k]
                gone = jnp.where(here, count, 0)
                next_rooms.append(rooms[k] - gone)
                next_ends.append(ends[k] + gone)
            room_new = (-count) & (BLK - 1)
            end_new = fresh + count
            shifted_rooms = rooms[1:] + [room_new]
            shifted_ends = ends[1:] + [end_new]
            rooms = [jnp.where(taken, a, b) for a, b in zip(next_rooms, shifted_rooms)]
            ends = [jnp.where(taken, a, b) for a, b in zip(next_ends, shifted_ends)]
            fresh = jnp.where(taken, fresh, end_new + room_new)
            largest = jnp.maximum(largest, count)
        start_ref[8 * g : 8 * g + 8, :] = tile
    starts = start_ref[...].astype(F32)
    for b in range(total // BLK):
        seat = jnp.sum(hot[:, block(b)] * (before[b] + starts), axis=0, keepdims=True)
        seat = jnp.where(live[:, block(b)], seat, -1.0)
        seat_ref[:, block(b)] = jnp.broadcast_to(seat, (8, BLK)).astype(I32)
        pcol_ref[block(b), :] = column(seat).astype(I32)
    several = jnp.max(largest) > BLK
    scal_ref[0] = (jnp.max(fresh) + (UL - 1)) // UL
    scal_ref[1] = several.astype(I32)

    @pl.when(several)
    def _():
        at = iota((windows, BLK), 1)
        count, start = cnt_ref[...], start_ref[...]
        first = lax.shift_right_logical(start, 7)
        final = lax.shift_right_logical(start + jnp.maximum(count, 1) - 1, 7)
        touch = (count > 0) & (first <= at) & (at <= final)
        low_at = jnp.min(jnp.where(touch, first, at), axis=0, keepdims=True)
        high_at = jnp.max(jnp.where(touch, final, at), axis=0, keepdims=True)
        for b in range((scal_ref.shape[0] - 3) // 2):
            scal_ref[2 + 2 * b] = jnp.max(jnp.where(at[0:1] == b, low_at, 0))
            scal_ref[3 + 2 * b] = jnp.max(jnp.where(at[0:1] == b, high_at, 0))


def picked(pcol_ref, u, n):
    seat = iota((BLK, BLK), 1) + u * UL
    return jnp.concatenate(
        [
            jnp.concatenate(
                [as_hot(pcol_ref[block(b), :] == seat + t * BLK) for t in range(n * UNIT)], axis=1
            )
            for b in range(pcol_ref.shape[0] // BLK)
        ],
        axis=0,
    )


def norm_forward(hidden, gain, shift):
    size = hidden.shape[0]
    average = jnp.sum(hidden, axis=0, keepdims=True) * (1.0 / size)
    centered = hidden - average
    inverse = lax.rsqrt(jnp.sum(centered * centered, axis=0, keepdims=True) * (1.0 / size) + EPS)
    normed = centered * inverse
    return normed * gain + shift, normed, inverse


def norm_backward(upstream, normed, inverse, gain):
    size = upstream.shape[0]
    scaled = upstream * gain
    center = jnp.sum(scaled, axis=0, keepdims=True) * (1.0 / size)
    along = jnp.sum(scaled * normed, axis=0, keepdims=True) * (1.0 / size)
    return inverse * (scaled - center - normed * along)


def tiles(x):
    return x.reshape(x.shape[0] // 8, 8, x.shape[1])


def own_heads(x):
    size = x.shape[0] // HEADS
    return jnp.concatenate([x[h * size : (h + 1) * size, block(h)] for h in range(HEADS)], axis=0)


def whole_rows(x):
    return jnp.broadcast_to(x, (8, x.shape[1]))


def put_heads(ref, t, at, x):
    size = x.shape[0] // HEADS
    for h in range(HEADS):
        ref[t, at + h * size : at + (h + 1) * size, block(h)] = x[h * size : (h + 1) * size]


BIG_WEIGHTS = ("w_qkv", "w_out", "w_up", "w_down")


def weight_copies(s, level):
    pairs = zip(BIG_WEIGHTS, (s.wqkv, s.wout, s.wup, s.wdown))
    return [
        pltpu.make_async_copy(getattr(s, name).at[level], ref, s.wsem.at[i])
        for i, (name, ref) in enumerate(pairs)
    ]


def setup_weights(s, level, copies):
    s.stack[...] = jnp.zeros(s.stack.shape, BF16)
    for b in range(2):
        s.cols[6 + b] = column(s.b_up[level : level + 1, block(b)])
        s.cols[b] = column(s.gains[level, b : b + 1, :])
    for b in range(4):
        s.cols[2 + b] = column(s.shifts[level, b : b + 1, :])
    for copy in copies:
        copy.wait()
    for b in range(3):
        s.wqkvt[block(b), :] = flip(s.wqkv[:, block(b)])
    s.woutt[...] = flip(s.wout[...])
    for b in range(2):
        s.wupt[block(b), :] = flip(s.wup[:, block(b)])
        s.wdownt[:, block(b)] = flip(s.wdown[block(b), :])


def project(s, u, n, low, placing, ids):
    width = low.shape[0]
    head = width // HEADS
    joined = (low.astype(F32) + placing).astype(BF16)
    put(s.xt, u, n, low)
    put(s.ut, u, n, joined)
    qk = dot(s.wqkvt[: 2 * width], joined).astype(BF16).astype(F32)
    vt = dot(s.wqkvt[2 * width :], low).astype(BF16).astype(F32)
    put(s.qt, u, n, (qk[:width] * (head ** (-0.5))).astype(BF16))
    kt = qk[width:]
    ones = jnp.ones((head, BLK), BF16)
    for t in range(n * UNIT):
        b = UNIT * u + t
        s.kt[b] = kt[:, block(t)].astype(BF16)
        for h in range(HEADS):
            s.vt[b, 2 * h * head : (2 * h + 1) * head, :] = vt[h * head : (h + 1) * head, block(t)].astype(BF16)
            s.vt[b, (2 * h + 1) * head : (2 * h + 2) * head, :] = ones
        s.k[b] = jnp.transpose(kt[:, block(t)]).astype(BF16)
        s.idcol[b] = column(ids[:, block(t)])
        s.idrow[b] = jnp.broadcast_to(ids[:, block(t)], (8, BLK))
        if s.backward:
            s.v[b] = jnp.transpose(vt[:, block(t)]).astype(BF16)
            s.dk[b] = jnp.zeros((BLK, width), F32)
            s.dv[b] = jnp.zeros((BLK, width), F32)


def other_window(s, keys, queries):
    return jnp.where(s.idcol[keys] == s.idrow[queries][0:1], 0.0, NEGATIVE)


def attend(s, u, n, single):
    qt = get(s.qt, u, n)
    width = qt.shape[0]
    head = width // HEADS
    mixed, inverses = [], []
    for t in range(n * UNIT):
        b = UNIT * u + t
        put_heads(s.stack, t, 0, qt[:, block(t)])
        if single:
            scores = dot(s.k[b], s.stack[t, :width])
            bias = other_window(s, b, b)
            sums = []
            for p in range(0, HEADS, PAIR):
                es = []
                for h in range(p, p + PAIR):
                    part = scores[:, block(h)] + bias
                    top = jnp.max(part, axis=0, keepdims=True)
                    es.append(jnp.exp(part - top).astype(BF16))
                es = jnp.concatenate(es, axis=1)
                if s.backward:
                    s.e[t, :BLK, p * BLK : (p + PAIR) * BLK] = es
                got = dot(s.vt[b, 2 * p * head : 2 * (p + PAIR) * head, :], es)
                sums += [got[2 * i * head : (2 * i + 2) * head, block(i)] for i in range(PAIR)]
        else:
            lo, hi = s.scal[2 + 2 * b], s.scal[3 + 2 * b] + 1

            def step_top(j, top, t=t, b=b):
                return jnp.maximum(top, jnp.max(tiles(masked_scores(s, j, t, b)), axis=0))

            top = lax.fori_loop(lo, hi, step_top, jnp.full((8, HEADS * BLK), 2 * NEGATIVE, F32))
            s.stat[t] = whole_rows(jnp.max(top, axis=0, keepdims=True))

            def step_mix(j, out, t=t, b=b):
                e = weights_of(s, j, t, b)
                return out + own_heads(dot(s.vt[j], e))

            out = lax.fori_loop(lo, hi, step_mix, jnp.zeros((2 * width, BLK), F32))
            sums = [out[2 * h * head : (2 * h + 2) * head] for h in range(HEADS)]
        inverse = [1.0 / x[head : head + 1] for x in sums]
        mixed.append(jnp.concatenate([x[:head] * i for x, i in zip(sums, inverse)], axis=0))
        inverses.append(inverse)
    return jnp.concatenate(mixed, axis=1), inverses


def masked_scores(s, j, t, b):
    bias = jnp.concatenate([other_window(s, j, b)] * HEADS, axis=1)
    return dot(s.k[j], s.stack[t, : s.k.shape[2]]) + bias


def weights_of(s, j, t, b):
    scores = masked_scores(s, j, t, b)
    return jnp.exp(tiles(scores) - s.stat[t][None]).reshape(BLK, HEADS * BLK).astype(BF16)


def attend_back(s, u, n, single, mixed, inverses, mixed_grad):
    width = mixed.shape[0]
    head = width // HEADS
    dqs = []
    for t in range(n * UNIT):
        b = UNIT * u + t
        levels = []
        for h in range(HEADS):
            rows = slice(h * head, (h + 1) * head)
            pull = (mixed_grad[rows, block(t)] * inverses[t][h]).astype(BF16)
            levels.append(jnp.sum(pull.astype(F32) * mixed[rows, block(t)], axis=0, keepdims=True))
            s.stack[t, width + h * head : width + (h + 1) * head, block(h)] = pull
        if single:
            slopes = dot(s.v[b], s.stack[t, width:])
            parts = []
            for p in range(0, HEADS, PAIR):
                gs = []
                for h in range(p, p + PAIR):
                    e = s.e[t, :BLK, block(h)].astype(F32)
                    gs.append((e * (slopes[:, block(h)] - levels[h])).astype(BF16))
                gs = jnp.concatenate(gs, axis=1)
                s.e[t, BLK:, p * BLK : (p + PAIR) * BLK] = gs
                got = dot(s.kt[b, p * head : (p + PAIR) * head, :], gs)
                parts += [got[i * head : (i + 1) * head, block(i)] for i in range(PAIR)]
            both = dot_nt(s.e[t], s.stack[t])
            s.dv[b] = both[:BLK, width:]
            s.dk[b] = both[BLK:, :width]
            dq = jnp.concatenate(parts, axis=0)
        else:
            lo, hi = s.scal[2 + 2 * b], s.scal[3 + 2 * b] + 1
            s.level[t] = whole_rows(jnp.concatenate(levels, axis=1))

            def step(j, dq, t=t, b=b):
                e = weights_of(s, j, t, b)
                slopes = tiles(dot(s.v[j], s.stack[t, width:])) - s.level[t][None]
                g = (e.astype(F32) * slopes.reshape(BLK, HEADS * BLK)).astype(BF16)
                s.dv[j] += dot_nt(e, s.stack[t, width:])
                s.dk[j] += dot_nt(g, s.stack[t, :width])
                return dq + own_heads(dot(s.kt[j], g))

            dq = lax.fori_loop(lo, hi, step, jnp.zeros((width, BLK), F32))
        dqs.append((dq * (head ** (-0.5))).astype(BF16))
    put(s.dq, u, n, jnp.concatenate(dqs, axis=1))


def fold(x):
    return sum(x[:, block(t)] for t in range(x.shape[1] // BLK))


def layer_units(s, u, n, single, upstream_of):
    mixed, inverses = attend(s, u, n, single)
    mixed_low = mixed.astype(BF16)
    spread_n = functools.partial(spread, n=n)
    gain_one, gain_two = spread_n(s.cols[0]), spread_n(s.cols[1])
    attended = dot(s.woutt[...], mixed_low) + spread_n(s.cols[2])
    first_out, normed_one, inverse_one = norm_forward(
        get(s.xt, u, n).astype(F32) + attended, gain_one, spread_n(s.cols[3])
    )
    first_low = first_out.astype(BF16)
    bias_up = jnp.concatenate([spread_n(s.cols[6]), spread_n(s.cols[7])], axis=0)
    before = dot(s.wupt[...], first_low) + bias_up
    square = before * before
    bend = jnp.tanh(before * (GELU_A + (GELU_A * GELU_B) * square))
    half = 0.5 + 0.5 * bend
    activated = (before * half).astype(BF16)
    branch = dot(s.wdownt[...], activated) + spread_n(s.cols[4])
    result, normed_two, inverse_two = norm_forward(first_out + branch, gain_two, spread_n(s.cols[5]))
    if upstream_of is None:
        return result.astype(BF16)
    upstream = upstream_of(u, n)
    ones = jnp.ones((16, n * UL), BF16)
    s.gg[0] += fold(upstream * normed_two)
    s.gg[1] += fold(upstream)
    second = norm_backward(upstream, normed_two, inverse_two, gain_two)
    branch_low = second.astype(BF16)
    s.gd[...] += dot_nt(jnp.concatenate([activated, ones], axis=0), branch_low)
    slope = half + half * (1.0 - bend) * before * (GELU_A + (3.0 * GELU_A * GELU_B) * square)
    before_low = (dot(s.wdown[...], branch_low) * slope).astype(BF16)
    s.gu[...] += dot_nt(jnp.concatenate([first_low, ones], axis=0), before_low)
    first_grad = second + dot(s.wup[...], before_low)
    s.gg[2] += fold(first_grad * normed_one)
    s.gg[3] += fold(first_grad)
    residual = norm_backward(first_grad, normed_one, inverse_one, gain_one)
    put(s.dh, u, n, residual)
    attended_low = residual.astype(BF16)
    s.go[...] += dot_nt(jnp.concatenate([mixed_low, ones], axis=0), attended_low)
    attend_back(s, u, n, single, mixed, inverses, dot(s.wout[...], attended_low))
    return result.astype(BF16)


def finish_units(s, u, n):
    width = s.xt.shape[1]
    dq = get(s.dq, u, n)
    blocks = [UNIT * u + t for t in range(n * UNIT)]
    dk = jnp.concatenate([s.dk[b] for b in blocks], axis=0).astype(BF16)
    dv = jnp.concatenate([s.dv[b] for b in blocks], axis=0).astype(BF16)
    dx = (
        get(s.dh, u, n)
        + dot(s.wqkv[:, :width], dq)
        + dot_nt(s.wqkv[:, width : 2 * width], dk)
        + dot_nt(s.wqkv[:, 2 * width :], dv)
    )
    joined = get(s.ut, u, n)
    s.gq[0] += dot_nt(joined, dq)
    s.gq[1] += dot(joined, dk)
    s.gq[2] += dot(get(s.xt, u, n), dv)
    return dx


def write_sums(s, wg_ref):
    width = s.xt.shape[1]
    for b in range(3):
        wg_ref[block(b), :] = s.gq[b].astype(BF16)
    wg_ref[384:512, :] = s.go[:width].astype(BF16)
    for b in range(2):
        wg_ref[512 + b * BLK : 640 + b * BLK, :] = s.gu[:width, block(b)].astype(BF16)
    wg_ref[768:1024, :] = s.gd[:256].astype(BF16)
    sums = [jnp.sum(jnp.transpose(s.gg[i]), axis=0, keepdims=True) for i in range(4)]
    out_bias, down_bias = s.go[width : width + 1], s.gd[256:257]
    up_bias = s.gu[width : width + 1]
    small = [
        sums[2], sums[0], out_bias, sums[3], down_bias, sums[1], up_bias[:, :BLK], up_bias[:, BLK:],
        jnp.zeros((8, BLK), F32),
    ]
    wg_ref[1024:GRAD_ROWS, :] = jnp.concatenate(small, axis=0).astype(BF16)


def zero_sums(s):
    for ref in (s.gq, s.go, s.gu, s.gd, s.gg):
        ref[...] = jnp.zeros(ref.shape, F32)


WEIGHTS = ("w_qkv", "w_out", "w_up", "w_down", "b_up", "gains", "shifts")


def layer_scratch(units, backward):
    vm = pltpu.VMEM
    width, blocks, most = 128, units * UNIT, WIDE * UNIT
    lanes = lambda dtype: vm((units, width, UL), dtype)
    out = dict(
        wqkv=vm((width, 384), BF16), wout=vm((width, width), BF16), wup=vm((width, 256), BF16),
        wdown=vm((256, width), BF16), wsem=pltpu.SemaphoreType.DMA((4,)),
        wqkvt=vm((384, width), BF16), woutt=vm((width, width), BF16), wupt=vm((256, width), BF16),
        wdownt=vm((width, 256), BF16), cols=vm((8, BLK, BLK), F32),
        xt=lanes(BF16), ut=lanes(BF16), qt=lanes(BF16),
        kt=vm((blocks, width, BLK), BF16), vt=vm((blocks, 2 * width, BLK), BF16),
        k=vm((blocks, BLK, width), BF16),
        idcol=vm((blocks, BLK, BLK), F32), idrow=vm((blocks, 8, BLK), F32),
        stat=vm((UNIT, 8, HEADS * BLK), F32), level=vm((UNIT, 8, HEADS * BLK), F32),
        stack=vm((most, 2 * width, HEADS * BLK), BF16),
    )
    if backward:
        out.update(
            v=vm((blocks, BLK, width), BF16), e=vm((most, 2 * BLK, HEADS * BLK), BF16),
            dh=lanes(F32), dq=lanes(BF16),
            dk=vm((blocks, BLK, width), F32), dv=vm((blocks, BLK, width), F32),
            gq=vm((3, width, width), F32), go=vm((width + 16, width), F32), gu=vm((width + 16, 256), F32),
            gd=vm((256 + 16, width), F32), gg=vm((4, width, BLK), F32),
        )
    return out


def seat_scratch(windows):
    return dict(cnt=pltpu.VMEM((windows, BLK), I32), start=pltpu.VMEM((windows, BLK), I32))


def call(body, name, ins, outs, scratch, far=()):
    names = list(ins) + list(outs) + list(scratch)

    def kernel(*refs):
        body(types.SimpleNamespace(**dict(zip(names, refs))))

    def spec(n):
        space = pltpu.SMEM if n in ("scal", "who", "over") else pl.ANY if n in far else pltpu.VMEM
        return pl.BlockSpec(memory_space=space)

    result = pl.pallas_call(
        kernel,
        out_shape=tuple(outs.values()),
        in_specs=[spec(n) for n in ins],
        out_specs=tuple(spec(n) for n in outs),
        scratch_shapes=list(scratch.values()),
        compiler_params=pltpu.CompilerParams(vmem_limit_bytes=VMEM),
        cost_estimate=pl.CostEstimate(flops=MICROS[name] * 10**9, bytes_accessed=2**20, transcendentals=0),
        name=name,
    )(*ins.values())
    return dict(zip(outs, result))


def sds(shape, dtype):
    return jax.ShapeDtypeStruct(shape, dtype)


def units_of(total):
    return -(-total // (64 * UNIT * WIDE)) * WIDE


def wide_steps(s):
    return (s.scal[0] + 1) // WIDE


def for_units(s, body, by_window=False):
    wide, last = wide_steps(s), s.scal[0]
    if by_window:
        last = jnp.where(s.scal[1] == 0, last, covered(s))
        wide = jnp.where(s.scal[1] == 0, wide, 0)

    @pl.loop(0, wide)
    def _(c):
        body(c * WIDE, WIDE, *([True] if by_window else []))

    @pl.loop(wide * WIDE, last)
    def _(u):
        if not by_window:
            body(u, 1)
            return

        @pl.when(s.scal[1] == 0)
        def _():
            body(u, 1, True)

        @pl.when(s.scal[1] != 0)
        def _():
            body(u, 1, False)


def covered(s):
    return jnp.maximum(s.scal[0], wide_steps(s) * WIDE)


def unit_copies(s, pairs):
    def copy(i, u):
        source, target = pairs[i]
        return pltpu.make_async_copy(source.at[u], target.at[u], s.usem.at[i, u])

    def start():
        @pl.loop(0, covered(s))
        def _(u):
            for i in range(len(pairs)):
                copy(i, u).start()

    def wait():
        @pl.loop(0, covered(s))
        def _(u):
            for i in range(len(pairs)):
                copy(i, u).wait()

    return start, wait


def forward_zero(meta, features, position, weights, strips, cap, who):
    total, width = features.shape
    units = units_of(total)
    buffer_rows = strips * cap

    def body(s):
        s.backward = False
        near = [
            pltpu.make_async_copy(s.features, s.x, s.sem.at[0]),
            pltpu.make_async_copy(s.position.at[0], s.p, s.sem.at[1]),
        ]
        copies = weight_copies(s, 0)
        for copy in near + copies:
            copy.start()
        meta = s.meta[...]
        live = meta[1:2] > 0
        take_seats(meta[0:1], live, WINDOWS // 2, s.scal, s.cnt, s.start, s.seat, s.pcol)
        setup_weights(s, 0, copies)
        for copy in near:
            copy.wait()
        for b in range(total // BLK):
            s.srct[:width, block(b)] = flip(s.x[block(b), :])
            s.srct[width : 2 * width, block(b)] = flip(s.p[block(b), :])
        at = iota((16, total), 0)
        place = meta[2:3]
        rows = jnp.where(at == 0, meta[0:1] + 1, jnp.where(at == 1, 1, 0))
        rows = jnp.where(at == 2, place >> 8, jnp.where(at == 3, place & 255, rows))
        s.srct[2 * width :, :] = rows.astype(F32).astype(BF16)
        s.acc[...] = jnp.zeros(s.acc.shape, F32)

        def begin(u, n):
            moved = dot(s.srct[...], picked(s.pcol, u, n))
            tags = moved[2 * width :]
            low = moved[:width].astype(BF16)
            put(s.pt, u, n, moved[width : 2 * width].astype(BF16))
            put(s.ids, u, n, whole_rows(tags[0:1]))
            spot = jnp.where(tags[1:2] > 0.5, tags[2:3] * 256 + tags[3:4], -1.0)
            put(s.spot, u, n, whole_rows(spot).astype(I32))
            for t in range(n * UNIT):
                s.spotcol[UNIT * u + t] = column(spot[:, block(t)]).astype(I32)
            project(s, u, n, low, moved[width : 2 * width], tags[0:1])

        for_units(s, begin)
        start, wait = unit_copies(s, [(s.xt, s.xs), (s.pt, s.ps)])
        start()

        def run(u, n, single):
            out = layer_units(s, u, n, single, None)
            for lanes in ranges(buffer_rows, 512):
                copies = (lanes.stop - lanes.start) // BLK
                at = iota((BLK, copies * BLK), 1) + lanes.start
                hot = jnp.concatenate(
                    [
                        as_hot(jnp.concatenate([s.spotcol[UNIT * u + t]] * copies, axis=1) == at)
                        for t in range(n * UNIT)
                    ],
                    axis=0,
                )
                s.acc[:, lanes] += dot(out, hot)

        for_units(s, run, True)
        for r in range(buffer_rows // BLK):
            s.flat[block(r), :] = jnp.transpose(s.acc[:, block(r)]).astype(BF16)
        for h in range(strips // 2):
            strip = (s.who[2] + 2 * h) & (strips - 1)
            getattr(s, f"own{h}")[...] = s.flat[pl.ds(pl.multiple_of(strip * cap, 16), cap), :]
            row = pl.multiple_of((strip ^ 1) * cap, 16)
            s.cross[h * cap : (h + 1) * cap, :] = s.flat[pl.ds(row, cap), :]
        wait()

    ins = dict(meta=meta, features=features, position=position, who=who, **dict(zip(WEIGHTS, weights)))
    outs = dict(
        {f"own{h}": sds((cap, width), BF16) for h in range(strips // 2)},
        cross=sds((buffer_rows // 2, width), BF16),
        xs=sds((units, width, UL), BF16), ps=sds((units, width, UL), BF16),
        ids=sds((units, 8, UL), F32), spot=sds((units, 8, UL), I32), seat=sds((8, total), I32),
        scal=sds((3 + 2 * units * UNIT,), I32),
    )
    scratch = dict(
        x=pltpu.VMEM((total, width), BF16), p=pltpu.VMEM((total, width), BF16),
        sem=pltpu.SemaphoreType.DMA((2,)), usem=pltpu.SemaphoreType.DMA((2, units)),
        pt=pltpu.VMEM((units, width, UL), BF16),
        pcol=pltpu.VMEM((total, BLK), I32), srct=pltpu.VMEM((2 * width + 16, total), BF16),
        flat=pltpu.VMEM((buffer_rows, width), BF16),
        acc=pltpu.VMEM((width, buffer_rows), F32), spotcol=pltpu.VMEM((units * UNIT, BLK, BLK), I32),
        **seat_scratch(WINDOWS // 2), **layer_scratch(units, False),
    )
    far = ("features", "position", "xs", "ps") + BIG_WEIGHTS
    return call(body, "forward_zero", ins, outs, scratch, far)


def scatter(s, u, n, pair):
    for lanes in ranges(s.seat.shape[1], 256):
        seat = s.seat[0:1, lanes] - u * UL
        hot = as_hot(iota((n * UL, lanes.stop - lanes.start), 0) == seat)
        s.acc[:, lanes] += dot(pair, hot)


def layer_one(first, arrived, weights, full, who):
    strips, width = 2 * len(arrived), arrived[0].shape[1]
    cap = arrived[0].shape[0] // 2
    total = strips * cap
    units = units_of(total)

    def body(s):
        s.backward = True
        near, tags, rest = [], [], []
        for d in range(strips):
            rows = pl.ds(d * cap, cap)
            tags.append(pltpu.make_async_copy(s.first.at[d, pl.ds(cap, 16), :], s.tagged.at[d], s.tsem.at[d]))
            rest.append(pltpu.make_async_copy(s.first.at[d, pl.ds(0, cap), :], s.pc.at[rows, :], s.rsem.at[d]))
            h, x = divmod(d, 2)
            row = pl.multiple_of((((s.who[2] - 2 * h) & (strips - 1)) ^ x) * cap, 16)
            source = getattr(s, f"arrived{h}").at[pl.ds(x * cap, cap), :]
            near.append(pltpu.make_async_copy(source, s.x.at[pl.ds(row, cap), :], s.sem.at[d]))
        copies = weight_copies(s, 1)
        for copy in tags + rest + near + copies:
            copy.start()
        zero_sums(s)
        s.acc[...] = jnp.zeros(s.acc.shape, F32)
        for copy in tags:
            copy.wait()
        for d in range(strips):
            s.tags[:, d * cap : (d + 1) * cap] = s.tagged[d, :, :cap].astype(F32)[:8]
        key, live = s.tags[0:1, :].astype(I32), s.tags[1:2, :] > 0.5
        s.over[0] = jnp.max(s.tags[2:3, :]).astype(I32)
        take_seats(key, live, WINDOWS, s.scal, s.cnt, s.start, s.seat, s.pcol)
        setup_weights(s, 1, copies)
        for copy in rest + near:
            copy.wait()
        for b in range(total // BLK):
            s.srct[:width, block(b)] = flip(s.x[block(b), :])
            s.srct[width : 3 * width, block(b)] = flip(s.pc[block(b), :])
        rows = jnp.where(iota((16, total), 0) == 0, key + 1, 0)
        s.srct[3 * width :, :] = rows.astype(F32).astype(BF16)

        def begin(u, n):
            moved = dot(s.srct[...], picked(s.pcol, u, n))
            put(s.dyt, u, n, moved[2 * width : 3 * width].astype(BF16))
            ids = moved[3 * width : 3 * width + 1]
            project(s, u, n, moved[:width].astype(BF16), moved[width : 2 * width], ids)

        def run(u, n, single):
            out = layer_units(s, u, n, single, lambda u, n: get(s.dyt, u, n).astype(F32))
            put(s.yt, u, n, out)

        def end(u, n):
            dx = finish_units(s, u, n)
            scatter(s, u, n, jnp.concatenate([get(s.yt, u, n), dx.astype(BF16)], axis=0))

        for_units(s, begin)
        for_units(s, run, True)
        for_units(s, end)
        for r in range(total // BLK):
            s.flat[block(r), :] = jnp.transpose(s.acc[:width, block(r)]).astype(BF16)
            s.dx[block(r), :] = jnp.transpose(s.acc[width:, block(r)]).astype(BF16)
        for d in range(strips):
            s.out[d, :cap, :] = s.flat[d * cap : (d + 1) * cap, :]
            if cap < full:
                s.out[d, cap:, :] = jnp.zeros((full - cap, width), BF16)
        write_sums(s, s.wg)

    ins = dict(
        first=first, who=who, **{f"arrived{d}": x for d, x in enumerate(arrived)}, **dict(zip(WEIGHTS, weights))
    )
    outs = dict(
        dx=sds((total, width), BF16), out=sds((strips, full, width), BF16), wg=sds((GRAD_ROWS, width), BF16),
        over=sds((1,), I32),
    )
    vm, lanes = pltpu.VMEM, pltpu.VMEM((units, width, UL), BF16)
    sems = pltpu.SemaphoreType.DMA((strips,))
    scratch = dict(
        x=vm((total, width), BF16), pc=vm((total, 2 * width), BF16), tagged=vm((strips, 16, 2 * width), BF16),
        tags=vm((8, total), F32), sem=sems, tsem=sems, rsem=sems, dyt=lanes, yt=lanes,
        scal=pltpu.SMEM((3 + 2 * units * UNIT,), I32), seat=vm((8, total), I32),
        flat=vm((total, width), BF16), pcol=vm((total, BLK), I32),
        srct=vm((3 * width + 16, total), BF16), acc=vm((2 * width, total), F32),
        **seat_scratch(WINDOWS), **layer_scratch(units, True),
    )
    far = ("first",) + tuple(f"arrived{h}" for h in range(strips // 2)) + BIG_WEIGHTS
    return call(body, "layer_one", ins, outs, scratch, far)


def layer_zero(ready, returned, weights, sums_one, who):
    total, width = ready["seat"].shape[1], returned.shape[1]
    units = units_of(total)
    buffer_rows = returned.shape[0]

    def body(s):
        s.backward = True
        near = [
            pltpu.make_async_copy(s.returned, s.x, s.sem.at[0]),
            pltpu.make_async_copy(s.sums_one, s.both.at[pl.ds(GRAD_ROWS, GRAD_ROWS), :], s.sem.at[1]),
        ]
        copies = weight_copies(s, 0)
        start, wait = unit_copies(s, [(s.xs, s.xz), (s.ps, s.pt)])
        start()
        for copy in copies + near:
            copy.start()
        zero_sums(s)
        s.acc[...] = jnp.zeros(s.acc.shape, F32)
        setup_weights(s, 0, copies)
        wait()
        near[0].wait()
        for b in range(buffer_rows // BLK):
            s.srct[:, block(b)] = flip(s.x[block(b), :])

        def begin(u, n):
            project(s, u, n, get(s.xz, u, n), get(s.pt, u, n).astype(F32), get(s.ids, u, n)[0:1])

        def upstream_of(u, n):
            return dot(s.srct[...], as_hot(iota((buffer_rows, n * UL), 0) == get(s.spot, u, n)[0:1]))

        def end(u, n):
            dx = finish_units(s, u, n)
            high = dx.astype(BF16)
            scatter(s, u, n, jnp.concatenate([high, (dx - high.astype(F32)).astype(BF16)], axis=0))

        for_units(s, begin)
        for_units(s, lambda u, n, single: layer_units(s, u, n, single, upstream_of), True)
        for_units(s, end)
        for r in range(total // BLK):
            s.grad[block(r), :] = jnp.transpose(s.acc[:width, block(r)] + s.acc[width:, block(r)])
        write_sums(s, s.both)
        near[1].wait()
        s.both[2 * GRAD_ROWS :, :] = jnp.zeros((2 * HALF_ROWS - 2 * GRAD_ROWS, width), BF16)
        start = pl.multiple_of(s.who[0] * HALF_ROWS, 16)
        s.keep[...] = s.both[pl.ds(start, HALF_ROWS), :]
        s.give[...] = s.both[pl.ds(pl.multiple_of(HALF_ROWS - start, 16), HALF_ROWS), :]

    ins = dict(
        {k: ready[k] for k in ("scal", "xs", "ps", "ids", "spot", "seat")}, returned=returned,
        sums_one=sums_one, who=who, **dict(zip(WEIGHTS, weights)),
    )
    half = sds((HALF_ROWS, width), BF16)
    outs = dict(grad=sds((total, width), F32), keep=half, give=half)
    lanes = pltpu.VMEM((units, width, UL), BF16)
    scratch = dict(
        x=pltpu.VMEM((buffer_rows, width), BF16), sem=pltpu.SemaphoreType.DMA((2,)),
        usem=pltpu.SemaphoreType.DMA((2, units)), xz=lanes, pt=lanes,
        both=pltpu.VMEM((2 * HALF_ROWS, width), BF16),
        srct=pltpu.VMEM((width, buffer_rows), BF16), acc=pltpu.VMEM((2 * width, total), F32),
        **layer_scratch(units, True),
    )
    far = ("returned", "sums_one", "xs", "ps") + BIG_WEIGHTS
    return call(body, "layer_zero", ins, outs, scratch, far)


def send_rows(ints, position, cotangent, strips, cap, full, balanced):
    total, width = cotangent.shape

    def body(s):
        near = [
            pltpu.make_async_copy(s.position.at[1], s.source.at[:, pl.ds(0, width)], s.sem.at[0]),
            pltpu.make_async_copy(s.cotangent, s.source.at[:, pl.ds(width, width)], s.sem.at[1]),
        ]
        for copy in near:
            copy.start()
        window, valid, dest, slot, shifted = [
            flat_row(r[...]) for r in (s.window, s.valid, s.dest, s.slot, s.shifted)
        ]
        live = valid > 0
        owner, key = dest, shifted
        if balanced:
            owner = (shifted + dest) & (strips - 1)
            key = dest * (WINDOWS // strips) + shifted // strips
            groups = max(strips, 16)
            hot = (iota((groups, total), 0) == jnp.where(live, owner, -1)).astype(F32)
            before, _ = counted(hot, groups)
            slot = jnp.concatenate(
                [
                    jnp.sum(hot[:, block(b)] * before[b], axis=0, keepdims=True)
                    for b in range(total // BLK)
                ],
                axis=1,
            ).astype(I32)
        fits = live & (slot < cap)
        over = jnp.max(jnp.where(live & (slot >= cap), 1, 0))
        place = jnp.where(fits, owner * cap + slot, -1)
        wide = jnp.where(fits, owner * full + slot, -1)
        s.meta[...] = jnp.concatenate([window, valid, place, wide, jnp.zeros((4, total), I32)], axis=0)
        at = iota((16, total), 0)
        rows = jnp.where(at == 0, key, jnp.where(at == 1, valid, 0)).astype(F32).astype(BF16)
        spot = iota((cap, total), 0)
        third = as_hot((iota((16, 2 * width), 0) == 2) & (over > 0))
        for copy in near:
            copy.wait()
        for d in range(strips):
            hot = as_hot(spot + d * cap == place)
            s.send[d, :cap, :] = dot(hot, s.source[...]).astype(BF16)
            tags = dot_nt(rows, hot)
            if cap < 2 * width:
                tags = jnp.concatenate([tags, jnp.zeros((16, 2 * width - cap), F32)], axis=1)
            s.send[d, cap:, :] = tags.astype(BF16) + third

    ins = dict(
        zip(("window", "valid", "dest", "slot", "shifted"), ints), position=position, cotangent=cotangent
    )
    outs = dict(send=sds((strips, cap + 16, 2 * width), BF16), meta=sds((8, total), I32))
    scratch = dict(source=pltpu.VMEM((total, 2 * width), BF16), sem=pltpu.SemaphoreType.DMA((2,)))
    return call(body, "send_rows", ins, outs, scratch, ("position", "cotangent"))


def fetch_rows(meta, rows):
    total = meta.shape[1]
    buffer_rows, width = rows.shape

    def body(s):
        at = iota((BLK, buffer_rows), 1)
        for b in range(total // BLK):
            col = column(s.meta[3:4, block(b)].astype(F32)).astype(I32)
            hot = as_hot(jnp.concatenate([col] * (buffer_rows // BLK), axis=1) == at)
            s.out[block(b), :] = dot(hot, s.rows[...]).astype(BF16)

    return call(body, "fetch_rows", dict(meta=meta, rows=rows), dict(out=sds((total, width), BF16)), {})["out"]


def cut_half(keep, got, who):
    def body(s):
        total = s.keep[...].astype(F32) + s.got[...].astype(F32)
        s.sums[...] = total.astype(BF16)
        for m, ref in enumerate((s.own, s.one, s.two, s.three)):
            start = pl.multiple_of((s.who[1] ^ m) * PART_ROWS, 16)
            ref[...] = s.sums[pl.ds(start, PART_ROWS), :]

    part = sds((PART_ROWS, keep.shape[1]), BF16)
    return call(
        body, "cut_half", dict(keep=keep, got=got, who=who), dict(own=part, one=part, two=part, three=part),
        dict(sums=pltpu.VMEM(keep.shape, BF16)),
    )


def unpack_sums(mine, other, who):
    width = mine.shape[1]

    def body(s):
        for a, ref in enumerate((s.mine, s.other)):
            for m in range(4):
                row = (s.who[0] ^ a) * HALF_ROWS + (s.who[1] ^ m) * PART_ROWS
                s.both[pl.ds(pl.multiple_of(row, 16), PART_ROWS), :] = ref[
                    m * PART_ROWS : (m + 1) * PART_ROWS, :
                ].astype(F32)
        for level in range(2):
            at = level * GRAD_ROWS
            for b in range(3):
                s.w_qkv[level, :, block(b)] = s.both[at + b * BLK : at + (b + 1) * BLK, :]
            s.w_out[level] = s.both[at + 384 : at + 512, :]
            for b in range(2):
                s.w_up[level, :, block(b)] = s.both[at + 512 + b * BLK : at + 640 + b * BLK, :]
                s.b_up[level : level + 1, block(b)] = s.both[at + 1030 + b : at + 1031 + b, :]
            s.w_down[level] = s.both[at + 768 : at + 1024, :]
            s.gains[level] = s.both[at + 1024 : at + 1026, :]
            s.shifts[level] = s.both[at + 1026 : at + 1030, :]

    outs = dict(
        w_qkv=sds((2, width, 384), F32), w_out=sds((2, width, width), F32), w_up=sds((2, width, 256), F32),
        w_down=sds((2, 256, width), F32), b_up=sds((2, 256), F32), gains=sds((2, 2, width), F32),
        shifts=sds((2, 4, width), F32),
    )
    done = call(
        body, "unpack_sums", dict(mine=mine, other=other, who=who), outs,
        dict(both=pltpu.VMEM((2 * HALF_ROWS, width), F32)),
    )
    return tuple(done[n] for n in WEIGHTS)


def paired_sum(parts):
    while len(parts) > 1:
        parts = [parts[i] + parts[i + 1] for i in range(0, len(parts), 2)]
    return parts[0]


def local(
    features, position, cotangent, w_qkv, w_out, w_up, w_down, b_up, gains, shifts,
    window, shifted_window, dest, slot, valid,
):
    strips, subs = lax.axis_size("strip"), lax.axis_size("sub")
    rows, width = features.shape
    full = 2 * rows // strips
    short = -(-(11 * full) // 256) * 16
    weights = (w_qkv, w_out, w_up, w_down, b_up, gains, shifts)

    def swap(x):
        return lax.all_to_all(x, "strip", split_axis=0, concat_axis=0, tiled=True)

    def trade(x, strip_mask, sub_mask):
        pairs = [
            (t * subs + u, (t ^ strip_mask) * subs + (u ^ sub_mask)) for t in range(strips) for u in range(subs)
        ]
        return lax.ppermute(x, ("strip", "sub"), pairs)

    at_strip, at_sub = lax.axis_index("strip"), lax.axis_index("sub")
    who = jnp.stack([at_sub & 1, ((at_sub >> 1) & 1) + 2 * (at_strip & 1), at_strip]).astype(I32)

    ints = [x.reshape(rows // BLK, BLK) for x in (window, valid, dest, slot, shifted_window)]

    def there(cap, balanced):
        sent = send_rows(ints, position, cotangent, strips, cap, full, balanced)
        arrived = swap(sent["send"])
        zero = forward_zero(sent["meta"], features, position, weights, strips, cap, who)
        cross = lax.ppermute(zero.pop("cross"), "strip", [(t, t ^ 1) for t in range(strips)])
        moved = []
        for h in range(strips // 2):
            pair = jnp.concatenate([zero.pop(f"own{h}"), cross[h * cap : (h + 1) * cap]], axis=0)
            moved.append(lax.ppermute(pair, "strip", [(t, (t + 2 * h) % strips) for t in range(strips)]) if h else pair)
        return sent["meta"], zero, layer_one(arrived, moved, weights, full, who)

    def back(meta, zero, one):
        returned = swap(one["dx"])
        out, sums_one, returned = lax.optimization_barrier((one["out"], one["wg"], returned))
        out = swap(out)
        last = layer_zero(zero, returned, weights, sums_one, who)
        return lax.optimization_barrier((last["keep"], last["give"], last["grad"], out, meta))

    first = there(short, True)
    over = first[2]["over"][0] > 0
    _, keep, give, grad, out, meta = lax.while_loop(
        lambda state: state[0], lambda _: (False, *back(*there(full, False))), (over, *back(*first))
    )

    square = ((0, 2), (1, 0), (1, 2))
    cut = cut_half(keep, trade(give, 0, 1), who)
    got = [trade(cut[n], *mask) for n, mask in zip(("one", "two", "three"), square)]
    part = paired_sum([x.astype(F32) for x in (cut["own"], *got)]).astype(BF16)
    got = [trade(part, m, 0) for m in range(2, strips, 2)]
    part = paired_sum([x.astype(F32) for x in (part, *got)]).astype(BF16)
    part, output = lax.optimization_barrier((part, fetch_rows(meta, out.reshape(strips * full, width))))
    mine = jnp.concatenate([part] + [trade(part, *mask) for mask in square], axis=0)
    return (output, grad) + unpack_sums(mine, trade(mine, 0, 1), who)


def solution(mesh):
    rows = P(("strip", "sub"), None)
    flat = P(("strip", "sub"))
    placed = (rows, P(None, ("strip", "sub"), None), rows) + (P(),) * 7 + (flat,) * 5
    return jax.shard_map(
        local,
        mesh=mesh,
        in_specs=placed,
        out_specs=(rows, rows) + (P(),) * 7,
        check_vma=False,
    )
```

```python
import functools
import types

import jax
import jax.numpy as jnp
from jax import lax
from jax.experimental import pallas as pl
from jax.experimental.pallas import tpu as pltpu
from jax.sharding import PartitionSpec as P

HEADS = 8
EPS = 1e-05
NEGATIVE = -1e30
BLK = 128
UNIT = 2
WIDE = 4
UL = UNIT * BLK
WINDOWS = 64
BINS = 4
PAIR = 2
MIB = 1024 * 1024
F32, BF16, I32 = jnp.float32, jnp.bfloat16, jnp.int32
GRAD_ROWS = 1040
PART_ROWS = 272
HALF_ROWS = 4 * PART_ROWS
MICROS = dict(
    send_rows=4, forward_zero=9, layer_one=17, layer_zero=14, fetch_rows=3, unpack_sums=2
)
GELU_A = 0.7978845608028654
GELU_B = 0.044715


def dot(a, b):
    return lax.dot_general(a, b, (((1,), (0,)), ((), ())), preferred_element_type=F32)


def dot_nt(a, b):
    return lax.dot_general(a, b, (((1,), (1,)), ((), ())), preferred_element_type=F32)


def flip(x):
    return jnp.transpose(x.astype(F32)).astype(BF16)


def iota(shape, dim):
    return lax.broadcasted_iota(I32, shape, dim)


def as_hot(mask):
    return mask.astype(F32).astype(BF16)


def column(row):
    return jnp.transpose(jnp.broadcast_to(row, (BLK, BLK)))


def spread(x, n):
    return jnp.concatenate([x] * (n * UNIT), axis=1)


def get(ref, u, n):
    return jnp.concatenate([ref[u + i] for i in range(n)], axis=1)


def put(ref, u, n, x):
    for i in range(n):
        ref[u + i] = x[:, i * UL : (i + 1) * UL]


def flat_row(x):
    return jnp.concatenate([x[i : i + 1] for i in range(x.shape[0])], axis=1)


def block(b):
    return slice(b * BLK, (b + 1) * BLK)


def ranges(total, step):
    return [slice(at, min(at + step, total)) for at in range(0, total, step)]


def counted(hot, groups):
    blocks = hot.shape[1] // BLK
    low = hot.astype(BF16)
    stacked = jnp.concatenate([low[:, block(b)] for b in range(blocks)], axis=0)
    row_at, col_at = iota((BLK, 2 * BLK), 0), iota((BLK, 2 * BLK), 1)
    sums = dot(stacked, as_hot((row_at < col_at) | (col_at >= BLK)))
    carry = jnp.zeros((groups, BLK), F32)
    before = []
    for b in range(blocks):
        part = sums[b * groups : (b + 1) * groups]
        before.append(part[:, :BLK] + carry)
        carry = carry + part[:, BLK:]
    return before, carry


def take_seats(win, live, windows, scal_ref, cnt_ref, start_ref, seat_ref, pcol_ref):
    total = win.shape[1]
    hot = (iota((windows, total), 0) == jnp.where(live, win, -1)).astype(F32)
    before, carry = counted(hot, windows)
    counts = carry.astype(I32)
    cnt_ref[...] = counts
    zero = jnp.zeros((8, BLK), I32)
    rooms, ends = [zero] * BINS, [zero] * BINS
    fresh, largest = zero, zero
    sub = iota((8, BLK), 0)
    for g in range(windows // 8):
        tile = zero
        for i in range(8):
            w = 8 * g + i
            count = jnp.broadcast_to(counts[w : w + 1, :], (8, BLK))
            fits = [count <= r for r in rooms]
            start, free = fresh, None
            for k in reversed(range(BINS)):
                start = jnp.where(fits[k], ends[k], start)
            tile = jnp.where(sub == i, start, tile)
            taken = jnp.zeros((8, BLK), jnp.bool_)
            next_rooms, next_ends = [], []
            for k in range(BINS):
                here = fits[k] & jnp.logical_not(taken)
                taken = taken | fits[k]
                gone = jnp.where(here, count, 0)
                next_rooms.append(rooms[k] - gone)
                next_ends.append(ends[k] + gone)
            room_new = (-count) & (BLK - 1)
            end_new = fresh + count
            shifted_rooms = rooms[1:] + [room_new]
            shifted_ends = ends[1:] + [end_new]
            rooms = [jnp.where(taken, a, b) for a, b in zip(next_rooms, shifted_rooms)]
            ends = [jnp.where(taken, a, b) for a, b in zip(next_ends, shifted_ends)]
            fresh = jnp.where(taken, fresh, end_new + room_new)
            largest = jnp.maximum(largest, count)
        start_ref[8 * g : 8 * g + 8, :] = tile
    starts = start_ref[...].astype(F32)
    for b in range(total // BLK):
        seat = jnp.sum(hot[:, block(b)] * (before[b] + starts), axis=0, keepdims=True)
        seat = jnp.where(live[:, block(b)], seat, -1.0)
        seat_ref[:, block(b)] = jnp.broadcast_to(seat, (8, BLK)).astype(I32)
        pcol_ref[block(b), :] = column(seat).astype(I32)
    several = jnp.max(largest) > BLK
    scal_ref[0] = (jnp.max(fresh) + (UL - 1)) // UL
    scal_ref[1] = several.astype(I32)

    @pl.when(several)
    def _():
        at = iota((windows, BLK), 1)
        count, start = cnt_ref[...], start_ref[...]
        first = lax.shift_right_logical(start, 7)
        final = lax.shift_right_logical(start + jnp.maximum(count, 1) - 1, 7)
        touch = (count > 0) & (first <= at) & (at <= final)
        low_at = jnp.min(jnp.where(touch, first, at), axis=0, keepdims=True)
        high_at = jnp.max(jnp.where(touch, final, at), axis=0, keepdims=True)
        for b in range((scal_ref.shape[0] - 3) // 2):
            scal_ref[2 + 2 * b] = jnp.max(jnp.where(at[0:1] == b, low_at, 0))
            scal_ref[3 + 2 * b] = jnp.max(jnp.where(at[0:1] == b, high_at, 0))


def picked(pcol_ref, u, n):
    seat = iota((BLK, BLK), 1) + u * UL
    return jnp.concatenate(
        [
            jnp.concatenate(
                [as_hot(pcol_ref[block(b), :] == seat + t * BLK) for t in range(n * UNIT)], axis=1
            )
            for b in range(pcol_ref.shape[0] // BLK)
        ],
        axis=0,
    )


def norm_forward(hidden, gain, shift):
    size = hidden.shape[0]
    average = jnp.sum(hidden, axis=0, keepdims=True) * (1.0 / size)
    centered = hidden - average
    inverse = lax.rsqrt(jnp.sum(centered * centered, axis=0, keepdims=True) * (1.0 / size) + EPS)
    normed = centered * inverse
    return normed * gain + shift, normed, inverse


def norm_backward(upstream, normed, inverse, gain):
    size = upstream.shape[0]
    scaled = upstream * gain
    center = jnp.sum(scaled, axis=0, keepdims=True) * (1.0 / size)
    along = jnp.sum(scaled * normed, axis=0, keepdims=True) * (1.0 / size)
    return inverse * (scaled - center - normed * along)


def tiles(x):
    return x.reshape(x.shape[0] // 8, 8, x.shape[1])


def own_heads(x):
    size = x.shape[0] // HEADS
    return jnp.concatenate([x[h * size : (h + 1) * size, block(h)] for h in range(HEADS)], axis=0)


def whole_rows(x):
    return jnp.broadcast_to(x, (8, x.shape[1]))


def put_heads(ref, t, at, x):
    size = x.shape[0] // HEADS
    for h in range(HEADS):
        ref[t, at + h * size : at + (h + 1) * size, block(h)] = x[h * size : (h + 1) * size]


BIG_WEIGHTS = ("w_qkv", "w_out", "w_up", "w_down")


def weight_copies(s, level):
    pairs = zip(BIG_WEIGHTS, (s.wqkv, s.wout, s.wup, s.wdown))
    return [
        pltpu.make_async_copy(getattr(s, name).at[level], ref, s.wsem.at[i])
        for i, (name, ref) in enumerate(pairs)
    ]


def setup_weights(s, level, copies):
    s.stack[...] = jnp.zeros(s.stack.shape, BF16)
    for b in range(2):
        s.cols[6 + b] = column(s.b_up[level : level + 1, block(b)])
        s.cols[b] = column(s.gains[level, b : b + 1, :])
    for b in range(4):
        s.cols[2 + b] = column(s.shifts[level, b : b + 1, :])
    for copy in copies:
        copy.wait()
    for b in range(3):
        s.wqkvt[block(b), :] = flip(s.wqkv[:, block(b)])
    s.woutt[...] = flip(s.wout[...])
    for b in range(2):
        s.wupt[block(b), :] = flip(s.wup[:, block(b)])
        s.wdownt[:, block(b)] = flip(s.wdown[block(b), :])


def project(s, u, n, low, placing, ids):
    width = low.shape[0]
    head = width // HEADS
    joined = (low.astype(F32) + placing).astype(BF16)
    put(s.xt, u, n, low)
    put(s.ut, u, n, joined)
    qk = dot(s.wqkvt[: 2 * width], joined).astype(BF16).astype(F32)
    vt = dot(s.wqkvt[2 * width :], low).astype(BF16).astype(F32)
    put(s.qt, u, n, (qk[:width] * (head ** (-0.5))).astype(BF16))
    kt = qk[width:]
    ones = jnp.ones((head, BLK), BF16)
    for t in range(n * UNIT):
        b = UNIT * u + t
        s.kt[b] = kt[:, block(t)].astype(BF16)
        for h in range(HEADS):
            s.vt[b, 2 * h * head : (2 * h + 1) * head, :] = vt[h * head : (h + 1) * head, block(t)].astype(BF16)
            s.vt[b, (2 * h + 1) * head : (2 * h + 2) * head, :] = ones
        s.k[b] = jnp.transpose(kt[:, block(t)]).astype(BF16)
        s.idcol[b] = column(ids[:, block(t)])
        s.idrow[b] = jnp.broadcast_to(ids[:, block(t)], (8, BLK))
        if s.backward:
            s.v[b] = jnp.transpose(vt[:, block(t)]).astype(BF16)
            s.dk[b] = jnp.zeros((width, BLK), F32)
            s.dv[b] = jnp.zeros((width, BLK), F32)


def other_window(s, keys, queries):
    return jnp.where(s.idcol[keys] == s.idrow[queries][0:1], 0.0, NEGATIVE)


def attend(s, u, n, single):
    qt = get(s.qt, u, n)
    width = qt.shape[0]
    head = width // HEADS
    mixed, inverses = [], []
    for t in range(n * UNIT):
        b = UNIT * u + t
        put_heads(s.stack, t, 0, qt[:, block(t)])
        if single:
            scores = dot(s.k[b], s.stack[t, :width])
            bias = other_window(s, b, b)
            sums = []
            for p in range(0, HEADS, PAIR):
                es = []
                for h in range(p, p + PAIR):
                    part = scores[:, block(h)] + bias
                    top = jnp.max(part, axis=0, keepdims=True)
                    es.append(jnp.exp(part - top).astype(BF16))
                es = jnp.concatenate(es, axis=1)
                if s.backward:
                    s.e[t, :, p * BLK : (p + PAIR) * BLK] = es
                got = dot(s.vt[b, 2 * p * head : 2 * (p + PAIR) * head, :], es)
                sums += [got[2 * i * head : (2 * i + 2) * head, block(i)] for i in range(PAIR)]
        else:
            lo, hi = s.scal[2 + 2 * b], s.scal[3 + 2 * b] + 1

            def step_top(j, top, t=t, b=b):
                return jnp.maximum(top, jnp.max(tiles(masked_scores(s, j, t, b)), axis=0))

            top = lax.fori_loop(lo, hi, step_top, jnp.full((8, HEADS * BLK), 2 * NEGATIVE, F32))
            s.stat[t] = whole_rows(jnp.max(top, axis=0, keepdims=True))

            def step_mix(j, out, t=t, b=b):
                e = weights_of(s, j, t, b)
                return out + own_heads(dot(s.vt[j], e))

            out = lax.fori_loop(lo, hi, step_mix, jnp.zeros((2 * width, BLK), F32))
            sums = [out[2 * h * head : (2 * h + 2) * head] for h in range(HEADS)]
        inverse = [1.0 / x[head : head + 1] for x in sums]
        mixed.append(jnp.concatenate([x[:head] * i for x, i in zip(sums, inverse)], axis=0))
        inverses.append(inverse)
    return jnp.concatenate(mixed, axis=1), inverses


def masked_scores(s, j, t, b):
    bias = jnp.concatenate([other_window(s, j, b)] * HEADS, axis=1)
    return dot(s.k[j], s.stack[t, : s.k.shape[2]]) + bias


def weights_of(s, j, t, b):
    scores = masked_scores(s, j, t, b)
    return jnp.exp(tiles(scores) - s.stat[t][None]).reshape(BLK, HEADS * BLK).astype(BF16)


def attend_back(s, u, n, single, mixed, inverses, mixed_grad):
    width = mixed.shape[0]
    head = width // HEADS
    dqs = []
    for t in range(n * UNIT):
        b = UNIT * u + t
        levels = []
        for h in range(HEADS):
            rows = slice(h * head, (h + 1) * head)
            pull = (mixed_grad[rows, block(t)] * inverses[t][h]).astype(BF16)
            levels.append(jnp.sum(pull.astype(F32) * mixed[rows, block(t)], axis=0, keepdims=True))
            s.stack[t, width + h * head : width + (h + 1) * head, block(h)] = pull
        if single:
            slopes = dot(s.v[b], s.stack[t, width:])
            parts = []
            for p in range(0, HEADS, PAIR):
                gs = []
                for h in range(p, p + PAIR):
                    e = s.e[t, :, block(h)].astype(F32)
                    gs.append((e * (slopes[:, block(h)] - levels[h])).astype(BF16))
                gs = jnp.concatenate(gs, axis=1)
                rows, lanes = slice(p * head, (p + PAIR) * head), slice(p * BLK, (p + PAIR) * BLK)
                s.dk[b, rows, :] = dot_nt(s.stack[t, rows, lanes], gs)
                pulled = slice(width + p * head, width + (p + PAIR) * head)
                s.dv[b, rows, :] = dot_nt(s.stack[t, pulled, lanes], s.e[t, :, lanes])
                got = dot(s.kt[b, p * head : (p + PAIR) * head, :], gs)
                parts += [got[i * head : (i + 1) * head, block(i)] for i in range(PAIR)]
            dq = jnp.concatenate(parts, axis=0)
        else:
            lo, hi = s.scal[2 + 2 * b], s.scal[3 + 2 * b] + 1
            s.level[t] = whole_rows(jnp.concatenate(levels, axis=1))

            def step(j, dq, t=t, b=b):
                e = weights_of(s, j, t, b)
                slopes = tiles(dot(s.v[j], s.stack[t, width:])) - s.level[t][None]
                g = (e.astype(F32) * slopes.reshape(BLK, HEADS * BLK)).astype(BF16)
                s.dv[j] += dot_nt(s.stack[t, width:], e)
                s.dk[j] += dot_nt(s.stack[t, :width], g)
                return dq + own_heads(dot(s.kt[j], g))

            dq = lax.fori_loop(lo, hi, step, jnp.zeros((width, BLK), F32))
        dqs.append((dq * (head ** (-0.5))).astype(BF16))
    put(s.dq, u, n, jnp.concatenate(dqs, axis=1))


def fold(x):
    return sum(x[:, block(t)] for t in range(x.shape[1] // BLK))


def layer_units(s, u, n, single, upstream_of):
    mixed, inverses = attend(s, u, n, single)
    mixed_low = mixed.astype(BF16)
    spread_n = functools.partial(spread, n=n)
    gain_one, gain_two = spread_n(s.cols[0]), spread_n(s.cols[1])
    attended = dot(s.woutt[...], mixed_low) + spread_n(s.cols[2])
    first_out, normed_one, inverse_one = norm_forward(
        get(s.xt, u, n).astype(F32) + attended, gain_one, spread_n(s.cols[3])
    )
    first_low = first_out.astype(BF16)
    bias_up = jnp.concatenate([spread_n(s.cols[6]), spread_n(s.cols[7])], axis=0)
    before = dot(s.wupt[...], first_low) + bias_up
    square = before * before
    bend = jnp.tanh(before * (GELU_A + (GELU_A * GELU_B) * square))
    half = 0.5 + 0.5 * bend
    activated = (before * half).astype(BF16)
    branch = dot(s.wdownt[...], activated) + spread_n(s.cols[4])
    result, normed_two, inverse_two = norm_forward(first_out + branch, gain_two, spread_n(s.cols[5]))
    if upstream_of is None:
        return result.astype(BF16)
    upstream = upstream_of(u, n)
    ones = jnp.ones((16, n * UL), BF16)
    s.gg[0] += fold(upstream * normed_two)
    s.gg[1] += fold(upstream)
    second = norm_backward(upstream, normed_two, inverse_two, gain_two)
    branch_low = second.astype(BF16)
    s.gd[...] += dot_nt(jnp.concatenate([activated, ones], axis=0), branch_low)
    slope = half + half * (1.0 - bend) * before * (GELU_A + (3.0 * GELU_A * GELU_B) * square)
    before_low = (dot(s.wdown[...], branch_low) * slope).astype(BF16)
    s.gu[...] += dot_nt(jnp.concatenate([first_low, ones], axis=0), before_low)
    first_grad = second + dot(s.wup[...], before_low)
    s.gg[2] += fold(first_grad * normed_one)
    s.gg[3] += fold(first_grad)
    residual = norm_backward(first_grad, normed_one, inverse_one, gain_one)
    put(s.dh, u, n, residual)
    attended_low = residual.astype(BF16)
    s.go[...] += dot_nt(jnp.concatenate([mixed_low, ones], axis=0), attended_low)
    attend_back(s, u, n, single, mixed, inverses, dot(s.wout[...], attended_low))
    return result.astype(BF16)


def finish_units(s, u, n):
    width = s.xt.shape[1]
    dq = get(s.dq, u, n)
    blocks = [UNIT * u + t for t in range(n * UNIT)]
    dk = jnp.concatenate([s.dk[b] for b in blocks], axis=1).astype(BF16)
    dv = jnp.concatenate([s.dv[b] for b in blocks], axis=1).astype(BF16)
    dx = get(s.dh, u, n) + dot(s.wqkv[...], jnp.concatenate([dq, dk, dv], axis=0))
    joined = get(s.ut, u, n)
    s.gq[0] += dot_nt(joined, dq)
    s.gq[1] += dot_nt(joined, dk)
    s.gq[2] += dot_nt(get(s.xt, u, n), dv)
    return dx


def write_sums(s, wg_ref, mark):
    width = s.xt.shape[1]
    for b in range(3):
        wg_ref[block(b), :] = s.gq[b].astype(BF16)
    wg_ref[384:512, :] = s.go[:width].astype(BF16)
    for b in range(2):
        wg_ref[512 + b * BLK : 640 + b * BLK, :] = s.gu[:width, block(b)].astype(BF16)
    wg_ref[768:1024, :] = s.gd[:256].astype(BF16)
    sums = [jnp.sum(jnp.transpose(s.gg[i]), axis=0, keepdims=True) for i in range(4)]
    out_bias, down_bias = s.go[width : width + 1], s.gd[256:257]
    up_bias = s.gu[width : width + 1]
    small = [
        sums[2], sums[0], out_bias, sums[3], down_bias, sums[1], up_bias[:, :BLK], up_bias[:, BLK:],
        jnp.full((8, BLK), mark, F32),
    ]
    wg_ref[1024:GRAD_ROWS, :] = jnp.concatenate(small, axis=0).astype(BF16)


def zero_sums(s):
    for ref in (s.gq, s.go, s.gu, s.gd, s.gg):
        ref[...] = jnp.zeros(ref.shape, F32)


WEIGHTS = ("w_qkv", "w_out", "w_up", "w_down", "b_up", "gains", "shifts")


def layer_scratch(units, backward):
    vm = pltpu.VMEM
    width, blocks, most = 128, units * UNIT, WIDE * UNIT
    lanes = lambda dtype: vm((units, width, UL), dtype)
    out = dict(
        wqkv=vm((width, 384), BF16), wout=vm((width, width), BF16), wup=vm((width, 256), BF16),
        wdown=vm((256, width), BF16), wsem=pltpu.SemaphoreType.DMA((4,)),
        wqkvt=vm((384, width), BF16), woutt=vm((width, width), BF16), wupt=vm((256, width), BF16),
        wdownt=vm((width, 256), BF16), cols=vm((8, BLK, BLK), F32),
        xt=lanes(BF16), ut=lanes(BF16), qt=lanes(BF16),
        kt=vm((blocks, width, BLK), BF16), vt=vm((blocks, 2 * width, BLK), BF16),
        k=vm((blocks, BLK, width), BF16),
        idcol=vm((blocks, BLK, BLK), F32), idrow=vm((blocks, 8, BLK), F32),
        stat=vm((UNIT, 8, HEADS * BLK), F32), level=vm((UNIT, 8, HEADS * BLK), F32),
        stack=vm((most, 2 * width, HEADS * BLK), BF16),
    )
    if backward:
        out.update(
            v=vm((blocks, BLK, width), BF16), e=vm((most, BLK, HEADS * BLK), BF16),
            dh=lanes(F32), dq=lanes(BF16),
            dk=vm((blocks, width, BLK), F32), dv=vm((blocks, width, BLK), F32),
            gq=vm((3, width, width), F32), go=vm((width + 16, width), F32), gu=vm((width + 16, 256), F32),
            gd=vm((256 + 16, width), F32), gg=vm((4, width, BLK), F32),
        )
    return out


def seat_scratch(windows):
    return dict(cnt=pltpu.VMEM((windows, BLK), I32), start=pltpu.VMEM((windows, BLK), I32))


def call(body, name, vmem, ins, outs, scratch, far=()):
    names = list(ins) + list(outs) + list(scratch)

    def kernel(*refs):
        body(types.SimpleNamespace(**dict(zip(names, refs))))

    def spec(n):
        space = pltpu.SMEM if n in ("scal", "who", "over") else pl.ANY if n in far else pltpu.VMEM
        return pl.BlockSpec(memory_space=space)

    result = pl.pallas_call(
        kernel,
        out_shape=tuple(outs.values()),
        in_specs=[spec(n) for n in ins],
        out_specs=tuple(spec(n) for n in outs),
        scratch_shapes=list(scratch.values()),
        compiler_params=pltpu.CompilerParams(vmem_limit_bytes=vmem * MIB),
        cost_estimate=pl.CostEstimate(flops=MICROS[name] * 10**9, bytes_accessed=2**20, transcendentals=0),
        name=name,
    )(*ins.values())
    return dict(zip(outs, result))


def sds(shape, dtype):
    return jax.ShapeDtypeStruct(shape, dtype)


def units_of(total):
    return -(-total // (64 * UNIT * WIDE)) * WIDE


def wide_steps(s):
    return (s.scal[0] + 1) // WIDE


def for_units(s, body, by_window=False):
    wide, last = wide_steps(s), s.scal[0]
    if by_window:
        last = jnp.where(s.scal[1] == 0, last, covered(s))
        wide = jnp.where(s.scal[1] == 0, wide, 0)

    @pl.loop(0, wide)
    def _(c):
        body(c * WIDE, WIDE, *([True] if by_window else []))

    @pl.loop(wide * WIDE, last)
    def _(u):
        if not by_window:
            body(u, 1)
            return

        @pl.when(s.scal[1] == 0)
        def _():
            body(u, 1, True)

        @pl.when(s.scal[1] != 0)
        def _():
            body(u, 1, False)


def covered(s):
    return jnp.maximum(s.scal[0], wide_steps(s) * WIDE)


def unit_copies(s, pairs):
    def copy(i, u):
        source, target = pairs[i]
        return pltpu.make_async_copy(source.at[u], target.at[u], s.usem.at[i, u])

    def start():
        @pl.loop(0, covered(s))
        def _(u):
            for i in range(len(pairs)):
                copy(i, u).start()

    def wait():
        @pl.loop(0, covered(s))
        def _(u):
            for i in range(len(pairs)):
                copy(i, u).wait()

    return start, wait


def forward_zero(meta, features, position, weights, strips, cap, who):
    total, width = features.shape
    units = units_of(total)
    buffer_rows = strips * cap

    def body(s):
        s.backward = False
        near = [
            pltpu.make_async_copy(s.features, s.x, s.sem.at[0]),
            pltpu.make_async_copy(s.position.at[0], s.p, s.sem.at[1]),
        ]
        copies = weight_copies(s, 0)
        for copy in near + copies:
            copy.start()
        meta = s.meta[...]
        live = meta[1:2] > 0
        take_seats(meta[0:1], live, WINDOWS // 2, s.scal, s.cnt, s.start, s.seat, s.pcol)
        setup_weights(s, 0, copies)
        for copy in near:
            copy.wait()
        for b in range(total // BLK):
            s.srct[:width, block(b)] = flip(s.x[block(b), :])
            s.srct[width : 2 * width, block(b)] = flip(s.p[block(b), :])
        at = iota((16, total), 0)
        place = meta[2:3]
        rows = jnp.where(at == 0, meta[0:1] + 1, jnp.where(at == 1, 1, 0))
        rows = jnp.where(at == 2, place >> 8, jnp.where(at == 3, place & 255, rows))
        s.srct[2 * width :, :] = rows.astype(F32).astype(BF16)
        s.acc[...] = jnp.zeros(s.acc.shape, F32)

        def begin(u, n):
            moved = dot(s.srct[...], picked(s.pcol, u, n))
            tags = moved[2 * width :]
            low = moved[:width].astype(BF16)
            put(s.pt, u, n, moved[width : 2 * width].astype(BF16))
            put(s.ids, u, n, whole_rows(tags[0:1]))
            spot = jnp.where(tags[1:2] > 0.5, tags[2:3] * 256 + tags[3:4], -1.0)
            put(s.spot, u, n, whole_rows(spot).astype(I32))
            for t in range(n * UNIT):
                s.spotcol[UNIT * u + t] = column(spot[:, block(t)]).astype(I32)
            project(s, u, n, low, moved[width : 2 * width], tags[0:1])

        for_units(s, begin)
        start, wait = unit_copies(s, [(s.xt, s.xs), (s.pt, s.ps)])
        start()

        def run(u, n, single):
            out = layer_units(s, u, n, single, None)
            for lanes in ranges(buffer_rows, 512):
                copies = (lanes.stop - lanes.start) // BLK
                at = iota((BLK, copies * BLK), 1) + lanes.start
                hot = jnp.concatenate(
                    [
                        as_hot(jnp.concatenate([s.spotcol[UNIT * u + t]] * copies, axis=1) == at)
                        for t in range(n * UNIT)
                    ],
                    axis=0,
                )
                s.acc[:, lanes] += dot(out, hot)

        for_units(s, run, True)
        for r in range(buffer_rows // BLK):
            s.flat[block(r), :] = jnp.transpose(s.acc[:, block(r)]).astype(BF16)
        for h in range(strips // 2):
            strip = (s.who[2] + 2 * h) & (strips - 1)
            getattr(s, f"own{h}")[...] = s.flat[pl.ds(pl.multiple_of(strip * cap, 16), cap), :]
            row = pl.multiple_of((strip ^ 1) * cap, 16)
            s.cross[h * cap : (h + 1) * cap, :] = s.flat[pl.ds(row, cap), :]
        wait()

    ins = dict(meta=meta, features=features, position=position, who=who, **dict(zip(WEIGHTS, weights)))
    outs = dict(
        {f"own{h}": sds((cap, width), BF16) for h in range(strips // 2)},
        cross=sds((buffer_rows // 2, width), BF16),
        xs=sds((units, width, UL), BF16), ps=sds((units, width, UL), BF16),
        ids=sds((units, 8, UL), F32), spot=sds((units, 8, UL), I32), seat=sds((8, total), I32),
        scal=sds((3 + 2 * units * UNIT,), I32),
    )
    scratch = dict(
        x=pltpu.VMEM((total, width), BF16), p=pltpu.VMEM((total, width), BF16),
        sem=pltpu.SemaphoreType.DMA((2,)), usem=pltpu.SemaphoreType.DMA((2, units)),
        pt=pltpu.VMEM((units, width, UL), BF16),
        pcol=pltpu.VMEM((total, BLK), I32), srct=pltpu.VMEM((2 * width + 16, total), BF16),
        flat=pltpu.VMEM((buffer_rows, width), BF16),
        acc=pltpu.VMEM((width, buffer_rows), F32), spotcol=pltpu.VMEM((units * UNIT, BLK, BLK), I32),
        **seat_scratch(WINDOWS // 2), **layer_scratch(units, False),
    )
    far = ("features", "position", "xs", "ps") + BIG_WEIGHTS
    return call(body, "forward_zero", 44, ins, outs, scratch, far)


def scatter(s, u, n, pair):
    for lanes in ranges(s.seat.shape[1], 256):
        seat = s.seat[0:1, lanes] - u * UL
        hot = as_hot(iota((n * UL, lanes.stop - lanes.start), 0) == seat)
        s.acc[:, lanes] += dot(pair, hot)


def layer_one(first, arrived, weights, full, who):
    strips, width = 2 * len(arrived), arrived[0].shape[1]
    cap = arrived[0].shape[0] // 2
    total = strips * cap
    units = units_of(total)

    def body(s):
        s.backward = True
        near, tags, rest = [], [], []
        for d in range(strips):
            rows = pl.ds(d * cap, cap)
            tags.append(pltpu.make_async_copy(s.first.at[d, pl.ds(cap, 16), :], s.tagged.at[d], s.tsem.at[d]))
            rest.append(pltpu.make_async_copy(s.first.at[d, pl.ds(0, cap), :], s.pc.at[rows, :], s.rsem.at[d]))
            h, x = divmod(d, 2)
            row = pl.multiple_of((((s.who[2] - 2 * h) & (strips - 1)) ^ x) * cap, 16)
            source = getattr(s, f"arrived{h}").at[pl.ds(x * cap, cap), :]
            near.append(pltpu.make_async_copy(source, s.x.at[pl.ds(row, cap), :], s.sem.at[d]))
        copies = weight_copies(s, 1)
        for copy in tags + rest + near + copies:
            copy.start()
        zero_sums(s)
        s.acc[...] = jnp.zeros(s.acc.shape, F32)
        for copy in tags:
            copy.wait()
        for d in range(strips):
            s.tags[:, d * cap : (d + 1) * cap] = s.tagged[d, :, :cap].astype(F32)[:8]
        key, live = s.tags[0:1, :].astype(I32), s.tags[1:2, :] > 0.5
        s.over[0] = jnp.max(s.tags[2:3, :]).astype(I32)
        take_seats(key, live, WINDOWS, s.scal, s.cnt, s.start, s.seat, s.pcol)
        setup_weights(s, 1, copies)
        for copy in rest + near:
            copy.wait()
        for b in range(total // BLK):
            s.srct[:width, block(b)] = flip(s.x[block(b), :])
            s.srct[width : 3 * width, block(b)] = flip(s.pc[block(b), :])
        rows = jnp.where(iota((16, total), 0) == 0, key + 1, 0)
        s.srct[3 * width :, :] = rows.astype(F32).astype(BF16)

        def begin(u, n):
            moved = dot(s.srct[...], picked(s.pcol, u, n))
            put(s.dyt, u, n, moved[2 * width : 3 * width].astype(BF16))
            ids = moved[3 * width : 3 * width + 1]
            project(s, u, n, moved[:width].astype(BF16), moved[width : 2 * width], ids)

        def run(u, n, single):
            out = layer_units(s, u, n, single, lambda u, n: get(s.dyt, u, n).astype(F32))
            put(s.yt, u, n, out)

        def end(u, n):
            dx = finish_units(s, u, n)
            scatter(s, u, n, jnp.concatenate([get(s.yt, u, n), dx.astype(BF16)], axis=0))

        for_units(s, begin)
        for_units(s, run, True)
        for_units(s, end)
        for r in range(total // BLK):
            s.flat[block(r), :] = jnp.transpose(s.acc[:width, block(r)]).astype(BF16)
            s.dx[block(r), :] = jnp.transpose(s.acc[width:, block(r)]).astype(BF16)
        for d in range(strips):
            s.out[d, :cap, :] = s.flat[d * cap : (d + 1) * cap, :]
            if cap < full:
                s.out[d, cap:, :] = jnp.zeros((full - cap, width), BF16)
        write_sums(s, s.wg, 0.0)

    ins = dict(
        first=first, who=who, **{f"arrived{d}": x for d, x in enumerate(arrived)}, **dict(zip(WEIGHTS, weights))
    )
    outs = dict(
        dx=sds((total, width), BF16), out=sds((strips, full, width), BF16), wg=sds((GRAD_ROWS, width), BF16),
        over=sds((1,), I32),
    )
    vm, lanes = pltpu.VMEM, pltpu.VMEM((units, width, UL), BF16)
    sems = pltpu.SemaphoreType.DMA((strips,))
    scratch = dict(
        x=vm((total, width), BF16), pc=vm((total, 2 * width), BF16), tagged=vm((strips, 16, 2 * width), BF16),
        tags=vm((8, total), F32), sem=sems, tsem=sems, rsem=sems, dyt=lanes, yt=lanes,
        scal=pltpu.SMEM((3 + 2 * units * UNIT,), I32), seat=vm((8, total), I32),
        flat=vm((total, width), BF16), pcol=vm((total, BLK), I32),
        srct=vm((3 * width + 16, total), BF16), acc=vm((2 * width, total), F32),
        **seat_scratch(WINDOWS), **layer_scratch(units, True),
    )
    far = ("first",) + tuple(f"arrived{h}" for h in range(strips // 2)) + BIG_WEIGHTS
    return call(body, "layer_one", 44 if cap < full else 56, ins, outs, scratch, far)


def layer_zero(ready, returned, weights, sums_one, over, who):
    total, width = ready["seat"].shape[1], returned.shape[1]
    units = units_of(total)
    buffer_rows = returned.shape[0]

    def body(s):
        s.backward = True
        near = [
            pltpu.make_async_copy(s.returned, s.x, s.sem.at[0]),
            pltpu.make_async_copy(s.sums_one, s.both.at[pl.ds(GRAD_ROWS, GRAD_ROWS), :], s.sem.at[1]),
        ]
        copies = weight_copies(s, 0)
        start, wait = unit_copies(s, [(s.xs, s.xz), (s.ps, s.pt)])
        start()
        for copy in copies + near:
            copy.start()
        zero_sums(s)
        s.acc[...] = jnp.zeros(s.acc.shape, F32)
        setup_weights(s, 0, copies)
        wait()
        near[0].wait()
        for b in range(buffer_rows // BLK):
            s.srct[:, block(b)] = flip(s.x[block(b), :])

        def begin(u, n):
            project(s, u, n, get(s.xz, u, n), get(s.pt, u, n).astype(F32), get(s.ids, u, n)[0:1])

        def upstream_of(u, n):
            return dot(s.srct[...], as_hot(iota((buffer_rows, n * UL), 0) == get(s.spot, u, n)[0:1]))

        def end(u, n):
            dx = finish_units(s, u, n)
            high = dx.astype(BF16)
            scatter(s, u, n, jnp.concatenate([high, (dx - high.astype(F32)).astype(BF16)], axis=0))

        for_units(s, begin)
        for_units(s, lambda u, n, single: layer_units(s, u, n, single, upstream_of), True)
        for_units(s, end)
        for r in range(total // BLK):
            s.grad[block(r), :] = jnp.transpose(s.acc[:width, block(r)] + s.acc[width:, block(r)])
        write_sums(s, s.both, s.over[0].astype(F32))
        near[1].wait()
        s.both[2 * GRAD_ROWS :, :] = jnp.zeros((2 * HALF_ROWS - 2 * GRAD_ROWS, width), BF16)
        for a, name in enumerate(("keep", "give")):
            for m in range(4):
                row = (s.who[0] ^ a) * HALF_ROWS + (s.who[1] ^ m) * PART_ROWS
                getattr(s, f"{name}{m}")[...] = s.both[pl.ds(pl.multiple_of(row, 16), PART_ROWS), :]

    ins = dict(
        {k: ready[k] for k in ("scal", "xs", "ps", "ids", "spot", "seat")}, returned=returned,
        sums_one=sums_one, over=over, who=who, **dict(zip(WEIGHTS, weights)),
    )
    part = pltpu.VMEM((PART_ROWS, width), BF16)
    outs = dict(grad=sds((total, width), F32), **{f"{n}{m}": part for n in ("keep", "give") for m in range(4)})
    lanes = pltpu.VMEM((units, width, UL), BF16)
    scratch = dict(
        x=pltpu.VMEM((buffer_rows, width), BF16), sem=pltpu.SemaphoreType.DMA((2,)),
        usem=pltpu.SemaphoreType.DMA((2, units)), xz=lanes, pt=lanes,
        both=pltpu.VMEM((2 * HALF_ROWS, width), BF16),
        srct=pltpu.VMEM((width, buffer_rows), BF16), acc=pltpu.VMEM((2 * width, total), F32),
        **layer_scratch(units, True),
    )
    far = ("returned", "sums_one", "xs", "ps") + BIG_WEIGHTS
    return call(body, "layer_zero", 44 if buffer_rows < 2 * total else 56, ins, outs, scratch, far)


def send_rows(ints, position, cotangent, strips, cap, full, balanced):
    total, width = cotangent.shape

    def body(s):
        near = [
            pltpu.make_async_copy(s.position.at[1], s.source.at[:, pl.ds(0, width)], s.sem.at[0]),
            pltpu.make_async_copy(s.cotangent, s.source.at[:, pl.ds(width, width)], s.sem.at[1]),
        ]
        for copy in near:
            copy.start()
        window, valid, dest, slot, shifted = [
            flat_row(r[...]) for r in (s.window, s.valid, s.dest, s.slot, s.shifted)
        ]
        live = valid > 0
        owner, key = dest, shifted
        if balanced:
            owner = (shifted + dest) & (strips - 1)
            key = dest * (WINDOWS // strips) + shifted // strips
            groups = max(strips, 16)
            hot = (iota((groups, total), 0) == jnp.where(live, owner, -1)).astype(F32)
            before, _ = counted(hot, groups)
            slot = jnp.concatenate(
                [
                    jnp.sum(hot[:, block(b)] * before[b], axis=0, keepdims=True)
                    for b in range(total // BLK)
                ],
                axis=1,
            ).astype(I32)
        fits = live & (slot < cap)
        over = jnp.max(jnp.where(live & (slot >= cap), 1, 0))
        place = jnp.where(fits, owner * cap + slot, -1)
        wide = jnp.where(fits, owner * full + slot, -1)
        s.meta[...] = jnp.concatenate([window, valid, place, wide, jnp.zeros((4, total), I32)], axis=0)
        at = iota((16, total), 0)
        rows = jnp.where(at == 0, key, jnp.where(at == 1, valid, 0)).astype(F32).astype(BF16)
        spot = iota((cap, total), 0)
        third = as_hot((iota((16, 2 * width), 0) == 2) & (over > 0))
        for copy in near:
            copy.wait()
        for d in range(strips):
            hot = as_hot(spot + d * cap == place)
            s.send[d, :cap, :] = dot(hot, s.source[...]).astype(BF16)
            tags = dot_nt(rows, hot)
            if cap < 2 * width:
                tags = jnp.concatenate([tags, jnp.zeros((16, 2 * width - cap), F32)], axis=1)
            s.send[d, cap:, :] = tags.astype(BF16) + third

    ins = dict(
        zip(("window", "valid", "dest", "slot", "shifted"), ints), position=position, cotangent=cotangent
    )
    outs = dict(send=sds((strips, cap + 16, 2 * width), BF16), meta=sds((8, total), I32))
    scratch = dict(source=pltpu.VMEM((total, 2 * width), BF16), sem=pltpu.SemaphoreType.DMA((2,)))
    return call(body, "send_rows", 24, ins, outs, scratch, ("position", "cotangent"))


def fetch_rows(meta, rows):
    total = meta.shape[1]
    buffer_rows, width = rows.shape

    def body(s):
        at = iota((BLK, buffer_rows), 1)
        for b in range(total // BLK):
            col = column(s.meta[3:4, block(b)].astype(F32)).astype(I32)
            hot = as_hot(jnp.concatenate([col] * (buffer_rows // BLK), axis=1) == at)
            s.out[block(b), :] = dot(hot, s.rows[...]).astype(BF16)

    return call(body, "fetch_rows", 16, dict(meta=meta, rows=rows), dict(out=sds((total, width), BF16)), {})["out"]


def unpack_sums(parts, who):
    width = parts[0].shape[1]

    def body(s):
        copies = [
            pltpu.make_async_copy(getattr(s, f"part{i}"), s.near.at[i], s.sem.at[i]) for i in range(len(parts))
        ]
        for copy in copies:
            copy.start()
        for i, copy in enumerate(copies):
            copy.wait()
            row = (s.who[0] ^ (i // 4)) * HALF_ROWS + (s.who[1] ^ (i % 4)) * PART_ROWS
            s.both[pl.ds(pl.multiple_of(row, 16), PART_ROWS), :] = s.near[i].astype(F32)
        s.over[0] = jnp.max(s.both[1032:GRAD_ROWS, :]).astype(I32)
        for level in range(2):
            at = level * GRAD_ROWS
            for b in range(3):
                s.w_qkv[level, :, block(b)] = s.both[at + b * BLK : at + (b + 1) * BLK, :]
            s.w_out[level] = s.both[at + 384 : at + 512, :]
            for b in range(2):
                s.w_up[level, :, block(b)] = s.both[at + 512 + b * BLK : at + 640 + b * BLK, :]
                s.b_up[level : level + 1, block(b)] = s.both[at + 1030 + b : at + 1031 + b, :]
            s.w_down[level] = s.both[at + 768 : at + 1024, :]
            s.gains[level] = s.both[at + 1024 : at + 1026, :]
            s.shifts[level] = s.both[at + 1026 : at + 1030, :]

    outs = dict(
        w_qkv=sds((2, width, 384), F32), w_out=sds((2, width, width), F32), w_up=sds((2, width, 256), F32),
        w_down=sds((2, 256, width), F32), b_up=sds((2, 256), F32), gains=sds((2, 2, width), F32),
        shifts=sds((2, 4, width), F32), over=sds((1,), I32),
    )
    names = [f"part{i}" for i in range(len(parts))]
    done = call(
        body, "unpack_sums", 16, dict(zip(names, parts), who=who), outs,
        dict(
            both=pltpu.VMEM((2 * HALF_ROWS, width), F32), near=pltpu.VMEM((len(parts), PART_ROWS, width), BF16),
            sem=pltpu.SemaphoreType.DMA((len(parts),)),
        ),
        names,
    )
    return tuple(done[n] for n in WEIGHTS), done["over"][0]


def paired_sum(parts):
    while len(parts) > 1:
        parts = [parts[i] + parts[i + 1] for i in range(0, len(parts), 2)]
    return parts[0]


def local(
    features, position, cotangent, w_qkv, w_out, w_up, w_down, b_up, gains, shifts,
    window, shifted_window, dest, slot, valid,
):
    strips, subs = lax.axis_size("strip"), lax.axis_size("sub")
    rows, width = features.shape
    full = 2 * rows // strips
    short = -(-(11 * full) // 256) * 16
    weights = (w_qkv, w_out, w_up, w_down, b_up, gains, shifts)

    def swap(x):
        return lax.all_to_all(x, "strip", split_axis=0, concat_axis=0, tiled=True)

    def trade(x, strip_mask, sub_mask):
        pairs = [
            (t * subs + u, (t ^ strip_mask) * subs + (u ^ sub_mask)) for t in range(strips) for u in range(subs)
        ]
        return lax.ppermute(x, ("strip", "sub"), pairs)

    at_strip, at_sub = lax.axis_index("strip"), lax.axis_index("sub")
    who = jnp.stack([at_sub & 1, ((at_sub >> 1) & 1) + 2 * (at_strip & 1), at_strip]).astype(I32)

    ints = [x.reshape(rows // BLK, BLK) for x in (window, valid, dest, slot, shifted_window)]

    square = ((0, 2), (1, 0), (1, 2))

    def total(parts):
        return paired_sum([x.astype(F32) for x in parts]).astype(BF16)

    def attempt(cap, balanced):
        sent = send_rows(ints, position, cotangent, strips, cap, full, balanced)
        arrived = swap(sent["send"])
        zero = forward_zero(sent["meta"], features, position, weights, strips, cap, who)
        cross = lax.ppermute(zero.pop("cross"), "strip", [(t, t ^ 1) for t in range(strips)])
        moved = []
        for h in range(strips // 2):
            pair = jnp.concatenate([zero.pop(f"own{h}"), cross[h * cap : (h + 1) * cap]], axis=0)
            moved.append(lax.ppermute(pair, "strip", [(t, (t + 2 * h) % strips) for t in range(strips)]) if h else pair)
        one = layer_one(arrived, moved, weights, full, who)
        returned = swap(one["dx"])
        out, sums_one, returned = lax.optimization_barrier((one["out"], one["wg"], returned))
        out = swap(out)
        last = layer_zero(zero, returned, weights, sums_one, one["over"], who)
        grad, out, *parts = lax.optimization_barrier(
            (last["grad"], out, *(last[f"{n}{m}"] for n in ("keep", "give") for m in range(4)))
        )
        cut = [total((k, trade(g, 0, 1))) for k, g in zip(parts[:4], parts[4:])]
        part = total([cut[0]] + [trade(x, *mask) for x, mask in zip(cut[1:], square)])
        part = total([part] + [trade(part, m, 0) for m in range(2, strips, 2)])
        output = fetch_rows(sent["meta"], out.reshape(strips * full, width))
        part, output = lax.optimization_barrier((part, output))
        mine = [part] + [trade(part, *mask) for mask in square]
        sums, over = unpack_sums(mine + [trade(x, 0, 1) for x in mine], who)
        return (output, grad) + sums, over > 0

    done, over = attempt(short, True)
    _, done = lax.while_loop(
        lambda state: state[0], lambda state: (state[0] & False, attempt(full, False)[0]), (over, done)
    )
    return done


def solution(mesh):
    rows = P(("strip", "sub"), None)
    flat = P(("strip", "sub"))
    placed = (rows, P(None, ("strip", "sub"), None), rows) + (P(),) * 7 + (flat,) * 5
    return jax.shard_map(
        local,
        mesh=mesh,
        in_specs=placed,
        out_specs=(rows, rows) + (P(),) * 7,
        check_vma=False,
    )
```

```python
import functools
import types

import jax
import jax.numpy as jnp
from jax import lax
from jax.experimental import pallas as pl
from jax.experimental.pallas import tpu as pltpu
from jax.sharding import PartitionSpec as P

HEADS = 8
EPS = 1e-05
NEGATIVE = -1e30
BLK = 128
UNIT = 2
WIDE = 4
UL = UNIT * BLK
WINDOWS = 64
BINS = 4
PAIR = 2
MIB = 1024 * 1024
F32, BF16, I32 = jnp.float32, jnp.bfloat16, jnp.int32
GRAD_ROWS = 1040
PART_ROWS = 272
HALF_ROWS = 4 * PART_ROWS
MICROS = dict(
    send_rows=4, forward_zero=9, layer_one=17, layer_zero=14, fetch_rows=3, unpack_sums=2
)
GELU_A = 0.7978845608028654
GELU_B = 0.044715


def dot(a, b):
    return lax.dot_general(a, b, (((1,), (0,)), ((), ())), preferred_element_type=F32)


def dot_nt(a, b):
    return lax.dot_general(a, b, (((1,), (1,)), ((), ())), preferred_element_type=F32)


def flip(x):
    return jnp.transpose(x.astype(F32)).astype(BF16)


def iota(shape, dim):
    return lax.broadcasted_iota(I32, shape, dim)


def as_hot(mask):
    return mask.astype(F32).astype(BF16)


def column(row):
    return jnp.transpose(jnp.broadcast_to(row, (BLK, BLK)))


def spread(x, n):
    return jnp.concatenate([x] * (n * UNIT), axis=1)


def get(ref, u, n):
    return jnp.concatenate([ref[u + i] for i in range(n)], axis=1)


def put(ref, u, n, x):
    for i in range(n):
        ref[u + i] = x[:, i * UL : (i + 1) * UL]


def flat_row(x):
    return jnp.concatenate([x[i : i + 1] for i in range(x.shape[0])], axis=1)


def block(b):
    return slice(b * BLK, (b + 1) * BLK)


def ranges(total, step):
    return [slice(at, min(at + step, total)) for at in range(0, total, step)]


def counted(hot, groups):
    blocks = hot.shape[1] // BLK
    low = hot.astype(BF16)
    stacked = jnp.concatenate([low[:, block(b)] for b in range(blocks)], axis=0)
    row_at, col_at = iota((BLK, 2 * BLK), 0), iota((BLK, 2 * BLK), 1)
    sums = dot(stacked, as_hot((row_at < col_at) | (col_at >= BLK)))
    carry = jnp.zeros((groups, BLK), F32)
    before = []
    for b in range(blocks):
        part = sums[b * groups : (b + 1) * groups]
        before.append(part[:, :BLK] + carry)
        carry = carry + part[:, BLK:]
    return before, carry


def take_seats(win, live, windows, scal_ref, cnt_ref, start_ref, seat_ref, pcol_ref):
    total = win.shape[1]
    hot = (iota((windows, total), 0) == jnp.where(live, win, -1)).astype(F32)
    before, carry = counted(hot, windows)
    counts = carry.astype(I32)
    cnt_ref[...] = counts
    zero = jnp.zeros((8, BLK), I32)
    rooms, ends = [zero] * BINS, [zero] * BINS
    fresh, largest = zero, zero
    sub = iota((8, BLK), 0)
    for g in range(windows // 8):
        tile = zero
        for i in range(8):
            w = 8 * g + i
            count = jnp.broadcast_to(counts[w : w + 1, :], (8, BLK))
            fits = [count <= r for r in rooms]
            start, free = fresh, None
            for k in reversed(range(BINS)):
                start = jnp.where(fits[k], ends[k], start)
            tile = jnp.where(sub == i, start, tile)
            taken = jnp.zeros((8, BLK), jnp.bool_)
            next_rooms, next_ends = [], []
            for k in range(BINS):
                here = fits[k] & jnp.logical_not(taken)
                taken = taken | fits[k]
                gone = jnp.where(here, count, 0)
                next_rooms.append(rooms[k] - gone)
                next_ends.append(ends[k] + gone)
            room_new = (-count) & (BLK - 1)
            end_new = fresh + count
            shifted_rooms = rooms[1:] + [room_new]
            shifted_ends = ends[1:] + [end_new]
            rooms = [jnp.where(taken, a, b) for a, b in zip(next_rooms, shifted_rooms)]
            ends = [jnp.where(taken, a, b) for a, b in zip(next_ends, shifted_ends)]
            fresh = jnp.where(taken, fresh, end_new + room_new)
            largest = jnp.maximum(largest, count)
        start_ref[8 * g : 8 * g + 8, :] = tile
    starts = start_ref[...].astype(F32)
    for b in range(total // BLK):
        seat = jnp.sum(hot[:, block(b)] * (before[b] + starts), axis=0, keepdims=True)
        seat = jnp.where(live[:, block(b)], seat, -1.0)
        seat_ref[:, block(b)] = jnp.broadcast_to(seat, (8, BLK)).astype(I32)
        pcol_ref[block(b), :] = column(seat).astype(I32)
    several = jnp.max(largest) > BLK
    scal_ref[0] = (jnp.max(fresh) + (UL - 1)) // UL
    scal_ref[1] = several.astype(I32)

    @pl.when(several)
    def _():
        at = iota((windows, BLK), 1)
        count, start = cnt_ref[...], start_ref[...]
        first = lax.shift_right_logical(start, 7)
        final = lax.shift_right_logical(start + jnp.maximum(count, 1) - 1, 7)
        touch = (count > 0) & (first <= at) & (at <= final)
        low_at = jnp.min(jnp.where(touch, first, at), axis=0, keepdims=True)
        high_at = jnp.max(jnp.where(touch, final, at), axis=0, keepdims=True)
        for b in range((scal_ref.shape[0] - 3) // 2):
            scal_ref[2 + 2 * b] = jnp.max(jnp.where(at[0:1] == b, low_at, 0))
            scal_ref[3 + 2 * b] = jnp.max(jnp.where(at[0:1] == b, high_at, 0))


def picked(pcol_ref, u, n):
    seat = iota((BLK, BLK), 1) + u * UL
    return jnp.concatenate(
        [
            jnp.concatenate(
                [as_hot(pcol_ref[block(b), :] == seat + t * BLK) for t in range(n * UNIT)], axis=1
            )
            for b in range(pcol_ref.shape[0] // BLK)
        ],
        axis=0,
    )


def norm_forward(hidden, gain, shift):
    size = hidden.shape[0]
    average = jnp.sum(hidden, axis=0, keepdims=True) * (1.0 / size)
    centered = hidden - average
    inverse = lax.rsqrt(jnp.sum(centered * centered, axis=0, keepdims=True) * (1.0 / size) + EPS)
    normed = centered * inverse
    return normed * gain + shift, normed, inverse


def norm_backward(upstream, normed, inverse, gain):
    size = upstream.shape[0]
    scaled = upstream * gain
    center = jnp.sum(scaled, axis=0, keepdims=True) * (1.0 / size)
    along = jnp.sum(scaled * normed, axis=0, keepdims=True) * (1.0 / size)
    return inverse * (scaled - center - normed * along)


def tiles(x):
    return x.reshape(x.shape[0] // 8, 8, x.shape[1])


def own_heads(x):
    size = x.shape[0] // HEADS
    return jnp.concatenate([x[h * size : (h + 1) * size, block(h)] for h in range(HEADS)], axis=0)


def whole_rows(x):
    return jnp.broadcast_to(x, (8, x.shape[1]))


def put_heads(ref, t, at, x):
    size = x.shape[0] // HEADS
    for h in range(HEADS):
        ref[t, at + h * size : at + (h + 1) * size, block(h)] = x[h * size : (h + 1) * size]


BIG_WEIGHTS = ("w_qkv", "w_out", "w_up", "w_down")


def weight_copies(s, level):
    pairs = zip(BIG_WEIGHTS, (s.wqkv, s.wout, s.wup, s.wdown))
    return [
        pltpu.make_async_copy(getattr(s, name).at[level], ref, s.wsem.at[i])
        for i, (name, ref) in enumerate(pairs)
    ]


def setup_weights(s, level, copies):
    s.stack[...] = jnp.zeros(s.stack.shape, BF16)
    for b in range(2):
        s.cols[6 + b] = column(s.b_up[level : level + 1, block(b)])
        s.cols[b] = column(s.gains[level, b : b + 1, :])
    for b in range(4):
        s.cols[2 + b] = column(s.shifts[level, b : b + 1, :])
    for copy in copies:
        copy.wait()
    for b in range(3):
        s.wqkvt[block(b), :] = flip(s.wqkv[:, block(b)])
    s.woutt[...] = flip(s.wout[...])
    for b in range(2):
        s.wupt[block(b), :] = flip(s.wup[:, block(b)])
        s.wdownt[:, block(b)] = flip(s.wdown[block(b), :])


def project(s, u, n, low, placing, ids):
    width = low.shape[0]
    head = width // HEADS
    joined = (low.astype(F32) + placing).astype(BF16)
    put(s.xt, u, n, low)
    put(s.ut, u, n, joined)
    qk = dot(s.wqkvt[: 2 * width], joined).astype(BF16).astype(F32)
    vt = dot(s.wqkvt[2 * width :], low).astype(BF16).astype(F32)
    put(s.qt, u, n, (qk[:width] * (head ** (-0.5))).astype(BF16))
    kt = qk[width:]
    ones = jnp.ones((head, BLK), BF16)
    for t in range(n * UNIT):
        b = UNIT * u + t
        s.kt[b] = kt[:, block(t)].astype(BF16)
        for h in range(HEADS):
            s.vt[b, 2 * h * head : (2 * h + 1) * head, :] = vt[h * head : (h + 1) * head, block(t)].astype(BF16)
            s.vt[b, (2 * h + 1) * head : (2 * h + 2) * head, :] = ones
        s.k[b] = jnp.transpose(kt[:, block(t)]).astype(BF16)
        s.idcol[b] = column(ids[:, block(t)])
        s.idrow[b] = jnp.broadcast_to(ids[:, block(t)], (8, BLK))
        if s.backward:
            s.v[b] = jnp.transpose(vt[:, block(t)]).astype(BF16)
            s.dk[b] = jnp.zeros((width, BLK), F32)
            s.dv[b] = jnp.zeros((width, BLK), F32)


def other_window(s, keys, queries):
    return jnp.where(s.idcol[keys] == s.idrow[queries][0:1], 0.0, NEGATIVE)


def attend(s, u, n, single):
    qt = get(s.qt, u, n)
    width = qt.shape[0]
    head = width // HEADS
    mixed, inverses = [], []
    for t in range(n * UNIT):
        b = UNIT * u + t
        put_heads(s.stack, t, 0, qt[:, block(t)])
        if single:
            scores = dot(s.k[b], s.stack[t, :width])
            bias = other_window(s, b, b)
            sums = []
            for p in range(0, HEADS, PAIR):
                es = []
                for h in range(p, p + PAIR):
                    part = scores[:, block(h)] + bias
                    top = jnp.max(part, axis=0, keepdims=True)
                    es.append(jnp.exp(part - top).astype(BF16))
                es = jnp.concatenate(es, axis=1)
                if s.backward:
                    s.e[t, :, p * BLK : (p + PAIR) * BLK] = es
                got = dot(s.vt[b, 2 * p * head : 2 * (p + PAIR) * head, :], es)
                sums += [got[2 * i * head : (2 * i + 2) * head, block(i)] for i in range(PAIR)]
        else:
            lo, hi = s.scal[2 + 2 * b], s.scal[3 + 2 * b] + 1

            def step_top(j, top, t=t, b=b):
                return jnp.maximum(top, jnp.max(tiles(masked_scores(s, j, t, b)), axis=0))

            top = lax.fori_loop(lo, hi, step_top, jnp.full((8, HEADS * BLK), 2 * NEGATIVE, F32))
            s.stat[t] = whole_rows(jnp.max(top, axis=0, keepdims=True))

            def step_mix(j, out, t=t, b=b):
                e = weights_of(s, j, t, b)
                return out + own_heads(dot(s.vt[j], e))

            out = lax.fori_loop(lo, hi, step_mix, jnp.zeros((2 * width, BLK), F32))
            sums = [out[2 * h * head : (2 * h + 2) * head] for h in range(HEADS)]
        inverse = [1.0 / x[head : head + 1] for x in sums]
        mixed.append(jnp.concatenate([x[:head] * i for x, i in zip(sums, inverse)], axis=0))
        inverses.append(inverse)
    return jnp.concatenate(mixed, axis=1), inverses


def masked_scores(s, j, t, b):
    bias = jnp.concatenate([other_window(s, j, b)] * HEADS, axis=1)
    return dot(s.k[j], s.stack[t, : s.k.shape[2]]) + bias


def weights_of(s, j, t, b):
    scores = masked_scores(s, j, t, b)
    return jnp.exp(tiles(scores) - s.stat[t][None]).reshape(BLK, HEADS * BLK).astype(BF16)


def attend_back(s, u, n, single, mixed, inverses, mixed_grad):
    width = mixed.shape[0]
    head = width // HEADS
    dqs = []
    for t in range(n * UNIT):
        b = UNIT * u + t
        levels = []
        for h in range(HEADS):
            rows = slice(h * head, (h + 1) * head)
            pull = (mixed_grad[rows, block(t)] * inverses[t][h]).astype(BF16)
            levels.append(jnp.sum(pull.astype(F32) * mixed[rows, block(t)], axis=0, keepdims=True))
            s.stack[t, width + h * head : width + (h + 1) * head, block(h)] = pull
        if single:
            slopes = dot(s.v[b], s.stack[t, width:])
            parts = []
            for p in range(0, HEADS, PAIR):
                gs = []
                for h in range(p, p + PAIR):
                    e = s.e[t, :, block(h)].astype(F32)
                    gs.append((e * (slopes[:, block(h)] - levels[h])).astype(BF16))
                gs = jnp.concatenate(gs, axis=1)
                rows, lanes = slice(p * head, (p + PAIR) * head), slice(p * BLK, (p + PAIR) * BLK)
                s.dk[b, rows, :] = dot_nt(s.stack[t, rows, lanes], gs)
                pulled = slice(width + p * head, width + (p + PAIR) * head)
                s.dv[b, rows, :] = dot_nt(s.stack[t, pulled, lanes], s.e[t, :, lanes])
                got = dot(s.kt[b, p * head : (p + PAIR) * head, :], gs)
                parts += [got[i * head : (i + 1) * head, block(i)] for i in range(PAIR)]
            dq = jnp.concatenate(parts, axis=0)
        else:
            lo, hi = s.scal[2 + 2 * b], s.scal[3 + 2 * b] + 1
            s.level[t] = whole_rows(jnp.concatenate(levels, axis=1))

            def step(j, dq, t=t, b=b):
                e = weights_of(s, j, t, b)
                slopes = tiles(dot(s.v[j], s.stack[t, width:])) - s.level[t][None]
                g = (e.astype(F32) * slopes.reshape(BLK, HEADS * BLK)).astype(BF16)
                s.dv[j] += dot_nt(s.stack[t, width:], e)
                s.dk[j] += dot_nt(s.stack[t, :width], g)
                return dq + own_heads(dot(s.kt[j], g))

            dq = lax.fori_loop(lo, hi, step, jnp.zeros((width, BLK), F32))
        dqs.append((dq * (head ** (-0.5))).astype(BF16))
    put(s.dq, u, n, jnp.concatenate(dqs, axis=1))


def fold(x):
    return sum(x[:, block(t)] for t in range(x.shape[1] // BLK))


def layer_units(s, u, n, single, upstream_of):
    mixed, inverses = attend(s, u, n, single)
    mixed_low = mixed.astype(BF16)
    spread_n = functools.partial(spread, n=n)
    gain_one, gain_two = spread_n(s.cols[0]), spread_n(s.cols[1])
    attended = dot(s.woutt[...], mixed_low) + spread_n(s.cols[2])
    first_out, normed_one, inverse_one = norm_forward(
        get(s.xt, u, n).astype(F32) + attended, gain_one, spread_n(s.cols[3])
    )
    first_low = first_out.astype(BF16)
    bias_up = jnp.concatenate([spread_n(s.cols[6]), spread_n(s.cols[7])], axis=0)
    before = dot(s.wupt[...], first_low) + bias_up
    square = before * before
    bend = jnp.tanh(before * (GELU_A + (GELU_A * GELU_B) * square))
    half = 0.5 + 0.5 * bend
    activated = (before * half).astype(BF16)
    branch = dot(s.wdownt[...], activated) + spread_n(s.cols[4])
    result, normed_two, inverse_two = norm_forward(first_out + branch, gain_two, spread_n(s.cols[5]))
    if upstream_of is None:
        return result.astype(BF16)
    upstream = upstream_of(u, n)
    ones = jnp.ones((16, n * UL), BF16)
    s.gg[0] += fold(upstream * normed_two)
    s.gg[1] += fold(upstream)
    second = norm_backward(upstream, normed_two, inverse_two, gain_two)
    branch_low = second.astype(BF16)
    s.gd[...] += dot_nt(jnp.concatenate([activated, ones], axis=0), branch_low)
    slope = half + half * (1.0 - bend) * before * (GELU_A + (3.0 * GELU_A * GELU_B) * square)
    before_low = (dot(s.wdown[...], branch_low) * slope).astype(BF16)
    s.gu[...] += dot_nt(jnp.concatenate([first_low, ones], axis=0), before_low)
    first_grad = second + dot(s.wup[...], before_low)
    s.gg[2] += fold(first_grad * normed_one)
    s.gg[3] += fold(first_grad)
    residual = norm_backward(first_grad, normed_one, inverse_one, gain_one)
    put(s.dh, u, n, residual)
    attended_low = residual.astype(BF16)
    s.go[...] += dot_nt(jnp.concatenate([mixed_low, ones], axis=0), attended_low)
    attend_back(s, u, n, single, mixed, inverses, dot(s.wout[...], attended_low))
    return result.astype(BF16)


def finish_units(s, u, n):
    width = s.xt.shape[1]
    dq = get(s.dq, u, n)
    blocks = [UNIT * u + t for t in range(n * UNIT)]
    dk = jnp.concatenate([s.dk[b] for b in blocks], axis=1).astype(BF16)
    dv = jnp.concatenate([s.dv[b] for b in blocks], axis=1).astype(BF16)
    dx = get(s.dh, u, n) + dot(s.wqkv[...], jnp.concatenate([dq, dk, dv], axis=0))
    joined = get(s.ut, u, n)
    s.gq[0] += dot_nt(joined, dq)
    s.gq[1] += dot_nt(joined, dk)
    s.gq[2] += dot_nt(get(s.xt, u, n), dv)
    return dx


def write_sums(s, wg_ref, mark):
    width = s.xt.shape[1]
    for b in range(3):
        wg_ref[block(b), :] = s.gq[b].astype(BF16)
    wg_ref[384:512, :] = s.go[:width].astype(BF16)
    for b in range(2):
        wg_ref[512 + b * BLK : 640 + b * BLK, :] = s.gu[:width, block(b)].astype(BF16)
    wg_ref[768:1024, :] = s.gd[:256].astype(BF16)
    sums = [jnp.sum(jnp.transpose(s.gg[i]), axis=0, keepdims=True) for i in range(4)]
    out_bias, down_bias = s.go[width : width + 1], s.gd[256:257]
    up_bias = s.gu[width : width + 1]
    small = [
        sums[2], sums[0], out_bias, sums[3], down_bias, sums[1], up_bias[:, :BLK], up_bias[:, BLK:],
        jnp.full((8, BLK), mark, F32),
    ]
    wg_ref[1024:GRAD_ROWS, :] = jnp.concatenate(small, axis=0).astype(BF16)


def zero_sums(s):
    for ref in (s.gq, s.go, s.gu, s.gd, s.gg):
        ref[...] = jnp.zeros(ref.shape, F32)


WEIGHTS = ("w_qkv", "w_out", "w_up", "w_down", "b_up", "gains", "shifts")


def layer_scratch(units, backward):
    vm = pltpu.VMEM
    width, blocks, most = 128, units * UNIT, WIDE * UNIT
    lanes = lambda dtype: vm((units, width, UL), dtype)
    out = dict(
        wqkv=vm((width, 384), BF16), wout=vm((width, width), BF16), wup=vm((width, 256), BF16),
        wdown=vm((256, width), BF16), wsem=pltpu.SemaphoreType.DMA((4,)),
        wqkvt=vm((384, width), BF16), woutt=vm((width, width), BF16), wupt=vm((256, width), BF16),
        wdownt=vm((width, 256), BF16), cols=vm((8, BLK, BLK), F32),
        xt=lanes(BF16), ut=lanes(BF16), qt=lanes(BF16),
        kt=vm((blocks, width, BLK), BF16), vt=vm((blocks, 2 * width, BLK), BF16),
        k=vm((blocks, BLK, width), BF16),
        idcol=vm((blocks, BLK, BLK), F32), idrow=vm((blocks, 8, BLK), F32),
        stat=vm((UNIT, 8, HEADS * BLK), F32), level=vm((UNIT, 8, HEADS * BLK), F32),
        stack=vm((most, 2 * width, HEADS * BLK), BF16),
    )
    if backward:
        out.update(
            v=vm((blocks, BLK, width), BF16), e=vm((most, BLK, HEADS * BLK), BF16),
            dh=lanes(F32), dq=lanes(BF16),
            dk=vm((blocks, width, BLK), F32), dv=vm((blocks, width, BLK), F32),
            gq=vm((3, width, width), F32), go=vm((width + 16, width), F32), gu=vm((width + 16, 256), F32),
            gd=vm((256 + 16, width), F32), gg=vm((4, width, BLK), F32),
        )
    return out


def seat_scratch(windows):
    return dict(cnt=pltpu.VMEM((windows, BLK), I32), start=pltpu.VMEM((windows, BLK), I32))


def call(body, name, vmem, ins, outs, scratch, far=()):
    names = list(ins) + list(outs) + list(scratch)

    def kernel(*refs):
        body(types.SimpleNamespace(**dict(zip(names, refs))))

    def spec(n):
        space = pltpu.SMEM if n in ("scal", "who", "over") else pl.ANY if n in far else pltpu.VMEM
        return pl.BlockSpec(memory_space=space)

    result = pl.pallas_call(
        kernel,
        out_shape=tuple(outs.values()),
        in_specs=[spec(n) for n in ins],
        out_specs=tuple(spec(n) for n in outs),
        scratch_shapes=list(scratch.values()),
        compiler_params=pltpu.CompilerParams(vmem_limit_bytes=vmem * MIB),
        cost_estimate=pl.CostEstimate(flops=MICROS[name] * 10**9, bytes_accessed=2**20, transcendentals=0),
        name=name,
    )(*ins.values())
    return dict(zip(outs, result))


def sds(shape, dtype):
    return jax.ShapeDtypeStruct(shape, dtype)


def units_of(total):
    return -(-total // (64 * UNIT * WIDE)) * WIDE


def wide_steps(s):
    return (s.scal[0] + 1) // WIDE


def for_units(s, body, by_window=False):
    wide, last = wide_steps(s), s.scal[0]
    if by_window:
        last = jnp.where(s.scal[1] == 0, last, covered(s))
        wide = jnp.where(s.scal[1] == 0, wide, 0)

    @pl.loop(0, wide)
    def _(c):
        body(c * WIDE, WIDE, *([True] if by_window else []))

    @pl.loop(wide * WIDE, last)
    def _(u):
        if not by_window:
            body(u, 1)
            return

        blocks = [UNIT * u + t for t in range(UNIT)]
        inside = [(s.scal[2 + 2 * b] == b) & (s.scal[3 + 2 * b] == b) for b in blocks]
        single = (s.scal[1] == 0) | functools.reduce(jnp.logical_and, inside)

        @pl.when(single)
        def _():
            body(u, 1, True)

        @pl.when(jnp.logical_not(single))
        def _():
            body(u, 1, False)


def covered(s):
    return jnp.maximum(s.scal[0], wide_steps(s) * WIDE)


def unit_copies(s, pairs):
    def copy(i, u):
        source, target = pairs[i]
        return pltpu.make_async_copy(source.at[u], target.at[u], s.usem.at[i, u])

    def start():
        @pl.loop(0, covered(s))
        def _(u):
            for i in range(len(pairs)):
                copy(i, u).start()

    def wait():
        @pl.loop(0, covered(s))
        def _(u):
            for i in range(len(pairs)):
                copy(i, u).wait()

    return start, wait


def forward_zero(meta, features, position, weights, strips, cap, who):
    total, width = features.shape
    units = units_of(total)
    buffer_rows = strips * cap

    def body(s):
        s.backward = False
        near = [
            pltpu.make_async_copy(s.features, s.x, s.sem.at[0]),
            pltpu.make_async_copy(s.position.at[0], s.p, s.sem.at[1]),
        ]
        copies = weight_copies(s, 0)
        for copy in near + copies:
            copy.start()
        meta = s.meta[...]
        live = meta[1:2] > 0
        take_seats(meta[0:1], live, WINDOWS // 2, s.scal, s.cnt, s.start, s.seat, s.pcol)
        setup_weights(s, 0, copies)
        for copy in near:
            copy.wait()
        for b in range(total // BLK):
            s.srct[:width, block(b)] = flip(s.x[block(b), :])
            s.srct[width : 2 * width, block(b)] = flip(s.p[block(b), :])
        at = iota((16, total), 0)
        place = meta[2:3]
        rows = jnp.where(at == 0, meta[0:1] + 1, jnp.where(at == 1, 1, 0))
        rows = jnp.where(at == 2, place >> 8, jnp.where(at == 3, place & 255, rows))
        s.srct[2 * width :, :] = rows.astype(F32).astype(BF16)
        s.acc[...] = jnp.zeros(s.acc.shape, F32)

        def begin(u, n):
            moved = dot(s.srct[...], picked(s.pcol, u, n))
            tags = moved[2 * width :]
            low = moved[:width].astype(BF16)
            put(s.pt, u, n, moved[width : 2 * width].astype(BF16))
            put(s.ids, u, n, whole_rows(tags[0:1]))
            spot = jnp.where(tags[1:2] > 0.5, tags[2:3] * 256 + tags[3:4], -1.0)
            put(s.spot, u, n, whole_rows(spot).astype(I32))
            for t in range(n * UNIT):
                s.spotcol[UNIT * u + t] = column(spot[:, block(t)]).astype(I32)
            project(s, u, n, low, moved[width : 2 * width], tags[0:1])

        for_units(s, begin)
        start, wait = unit_copies(s, [(s.xt, s.xs), (s.pt, s.ps)])
        start()

        def run(u, n, single):
            out = layer_units(s, u, n, single, None)
            for lanes in ranges(buffer_rows, 512):
                copies = (lanes.stop - lanes.start) // BLK
                at = iota((BLK, copies * BLK), 1) + lanes.start
                hot = jnp.concatenate(
                    [
                        as_hot(jnp.concatenate([s.spotcol[UNIT * u + t]] * copies, axis=1) == at)
                        for t in range(n * UNIT)
                    ],
                    axis=0,
                )
                s.acc[:, lanes] += dot(out, hot)

        for_units(s, run, True)
        for r in range(buffer_rows // BLK):
            s.flat[block(r), :] = jnp.transpose(s.acc[:, block(r)]).astype(BF16)
        for h in range(strips // 2):
            strip = (s.who[2] + 2 * h) & (strips - 1)
            getattr(s, f"own{h}")[...] = s.flat[pl.ds(pl.multiple_of(strip * cap, 16), cap), :]
            row = pl.multiple_of((strip ^ 1) * cap, 16)
            s.cross[h * cap : (h + 1) * cap, :] = s.flat[pl.ds(row, cap), :]
        wait()

    ins = dict(meta=meta, features=features, position=position, who=who, **dict(zip(WEIGHTS, weights)))
    outs = dict(
        {f"own{h}": sds((cap, width), BF16) for h in range(strips // 2)},
        cross=sds((buffer_rows // 2, width), BF16),
        xs=sds((units, width, UL), BF16), ps=sds((units, width, UL), BF16),
        ids=sds((units, 8, UL), F32), spot=sds((units, 8, UL), I32), seat=sds((8, total), I32),
        scal=sds((3 + 2 * units * UNIT,), I32),
    )
    scratch = dict(
        x=pltpu.VMEM((total, width), BF16), p=pltpu.VMEM((total, width), BF16),
        sem=pltpu.SemaphoreType.DMA((2,)), usem=pltpu.SemaphoreType.DMA((2, units)),
        pt=pltpu.VMEM((units, width, UL), BF16),
        pcol=pltpu.VMEM((total, BLK), I32), srct=pltpu.VMEM((2 * width + 16, total), BF16),
        flat=pltpu.VMEM((buffer_rows, width), BF16),
        acc=pltpu.VMEM((width, buffer_rows), F32), spotcol=pltpu.VMEM((units * UNIT, BLK, BLK), I32),
        **seat_scratch(WINDOWS // 2), **layer_scratch(units, False),
    )
    far = ("features", "position", "xs", "ps") + BIG_WEIGHTS
    return call(body, "forward_zero", 44, ins, outs, scratch, far)


def scatter(s, u, n, pair):
    for lanes in ranges(s.seat.shape[1], 256):
        seat = s.seat[0:1, lanes] - u * UL
        hot = as_hot(iota((n * UL, lanes.stop - lanes.start), 0) == seat)
        s.acc[:, lanes] += dot(pair, hot)


def layer_one(first, arrived, weights, full, who):
    strips, width = 2 * len(arrived), arrived[0].shape[1]
    cap = arrived[0].shape[0] // 2
    total = strips * cap
    units = units_of(total)

    def body(s):
        s.backward = True
        near, tags, rest = [], [], []
        for d in range(strips):
            rows = pl.ds(d * cap, cap)
            tags.append(pltpu.make_async_copy(s.first.at[d, pl.ds(cap, 16), :], s.tagged.at[d], s.tsem.at[d]))
            rest.append(pltpu.make_async_copy(s.first.at[d, pl.ds(0, cap), :], s.pc.at[rows, :], s.rsem.at[d]))
            h, x = divmod(d, 2)
            row = pl.multiple_of((((s.who[2] - 2 * h) & (strips - 1)) ^ x) * cap, 16)
            source = getattr(s, f"arrived{h}").at[pl.ds(x * cap, cap), :]
            near.append(pltpu.make_async_copy(source, s.x.at[pl.ds(row, cap), :], s.sem.at[d]))
        copies = weight_copies(s, 1)
        for copy in tags + rest + near + copies:
            copy.start()
        zero_sums(s)
        s.acc[...] = jnp.zeros(s.acc.shape, F32)
        for copy in tags:
            copy.wait()
        for d in range(strips):
            s.tags[:, d * cap : (d + 1) * cap] = s.tagged[d, :, :cap].astype(F32)[:8]
        key, live = s.tags[0:1, :].astype(I32), s.tags[1:2, :] > 0.5
        s.over[0] = jnp.max(s.tags[2:3, :]).astype(I32)
        take_seats(key, live, WINDOWS, s.scal, s.cnt, s.start, s.seat, s.pcol)
        setup_weights(s, 1, copies)
        for copy in rest + near:
            copy.wait()
        for b in range(total // BLK):
            s.srct[:width, block(b)] = flip(s.x[block(b), :])
            s.srct[width : 3 * width, block(b)] = flip(s.pc[block(b), :])
        rows = jnp.where(iota((16, total), 0) == 0, key + 1, 0)
        s.srct[3 * width :, :] = rows.astype(F32).astype(BF16)

        def begin(u, n):
            moved = dot(s.srct[...], picked(s.pcol, u, n))
            put(s.dyt, u, n, moved[2 * width : 3 * width].astype(BF16))
            ids = moved[3 * width : 3 * width + 1]
            project(s, u, n, moved[:width].astype(BF16), moved[width : 2 * width], ids)

        def run(u, n, single):
            out = layer_units(s, u, n, single, lambda u, n: get(s.dyt, u, n).astype(F32))
            put(s.yt, u, n, out)

        def end(u, n):
            dx = finish_units(s, u, n)
            scatter(s, u, n, jnp.concatenate([get(s.yt, u, n), dx.astype(BF16)], axis=0))

        for_units(s, begin)
        for_units(s, run, True)
        for_units(s, end)
        for r in range(total // BLK):
            s.flat[block(r), :] = jnp.transpose(s.acc[:width, block(r)]).astype(BF16)
            s.dx[block(r), :] = jnp.transpose(s.acc[width:, block(r)]).astype(BF16)
        for d in range(strips):
            s.out[d, :cap, :] = s.flat[d * cap : (d + 1) * cap, :]
            if cap < full:
                s.out[d, cap:, :] = jnp.zeros((full - cap, width), BF16)
        write_sums(s, s.wg, 0.0)

    ins = dict(
        first=first, who=who, **{f"arrived{d}": x for d, x in enumerate(arrived)}, **dict(zip(WEIGHTS, weights))
    )
    outs = dict(
        dx=sds((total, width), BF16), out=sds((strips, full, width), BF16), wg=sds((GRAD_ROWS, width), BF16),
        over=sds((1,), I32),
    )
    vm, lanes = pltpu.VMEM, pltpu.VMEM((units, width, UL), BF16)
    sems = pltpu.SemaphoreType.DMA((strips,))
    scratch = dict(
        x=vm((total, width), BF16), pc=vm((total, 2 * width), BF16), tagged=vm((strips, 16, 2 * width), BF16),
        tags=vm((8, total), F32), sem=sems, tsem=sems, rsem=sems, dyt=lanes, yt=lanes,
        scal=pltpu.SMEM((3 + 2 * units * UNIT,), I32), seat=vm((8, total), I32),
        flat=vm((total, width), BF16), pcol=vm((total, BLK), I32),
        srct=vm((3 * width + 16, total), BF16), acc=vm((2 * width, total), F32),
        **seat_scratch(WINDOWS), **layer_scratch(units, True),
    )
    far = ("first",) + tuple(f"arrived{h}" for h in range(strips // 2)) + BIG_WEIGHTS
    return call(body, "layer_one", 44 if cap < full else 56, ins, outs, scratch, far)


def layer_zero(ready, returned, weights, sums_one, over, who):
    total, width = ready["seat"].shape[1], returned.shape[1]
    units = units_of(total)
    buffer_rows = returned.shape[0]

    def body(s):
        s.backward = True
        near = [
            pltpu.make_async_copy(s.returned, s.x, s.sem.at[0]),
            pltpu.make_async_copy(s.sums_one, s.both.at[pl.ds(GRAD_ROWS, GRAD_ROWS), :], s.sem.at[1]),
        ]
        copies = weight_copies(s, 0)
        start, wait = unit_copies(s, [(s.xs, s.xz), (s.ps, s.pt)])
        start()
        for copy in copies + near:
            copy.start()
        zero_sums(s)
        s.acc[...] = jnp.zeros(s.acc.shape, F32)
        setup_weights(s, 0, copies)
        wait()
        near[0].wait()
        for b in range(buffer_rows // BLK):
            s.srct[:, block(b)] = flip(s.x[block(b), :])

        def begin(u, n):
            project(s, u, n, get(s.xz, u, n), get(s.pt, u, n).astype(F32), get(s.ids, u, n)[0:1])

        def upstream_of(u, n):
            return dot(s.srct[...], as_hot(iota((buffer_rows, n * UL), 0) == get(s.spot, u, n)[0:1]))

        def end(u, n):
            dx = finish_units(s, u, n)
            high = dx.astype(BF16)
            scatter(s, u, n, jnp.concatenate([high, (dx - high.astype(F32)).astype(BF16)], axis=0))

        for_units(s, begin)
        for_units(s, lambda u, n, single: layer_units(s, u, n, single, upstream_of), True)
        for_units(s, end)
        for r in range(total // BLK):
            s.grad[block(r), :] = jnp.transpose(s.acc[:width, block(r)] + s.acc[width:, block(r)])
        write_sums(s, s.both, s.over[0].astype(F32))
        near[1].wait()
        s.both[2 * GRAD_ROWS :, :] = jnp.zeros((2 * HALF_ROWS - 2 * GRAD_ROWS, width), BF16)
        for a, name in enumerate(("keep", "give")):
            for m in range(4):
                row = (s.who[0] ^ a) * HALF_ROWS + (s.who[1] ^ m) * PART_ROWS
                getattr(s, f"{name}{m}")[...] = s.both[pl.ds(pl.multiple_of(row, 16), PART_ROWS), :]

    ins = dict(
        {k: ready[k] for k in ("scal", "xs", "ps", "ids", "spot", "seat")}, returned=returned,
        sums_one=sums_one, over=over, who=who, **dict(zip(WEIGHTS, weights)),
    )
    part = pltpu.VMEM((PART_ROWS, width), BF16)
    outs = dict(grad=sds((total, width), F32), **{f"{n}{m}": part for n in ("keep", "give") for m in range(4)})
    lanes = pltpu.VMEM((units, width, UL), BF16)
    scratch = dict(
        x=pltpu.VMEM((buffer_rows, width), BF16), sem=pltpu.SemaphoreType.DMA((2,)),
        usem=pltpu.SemaphoreType.DMA((2, units)), xz=lanes, pt=lanes,
        both=pltpu.VMEM((2 * HALF_ROWS, width), BF16),
        srct=pltpu.VMEM((width, buffer_rows), BF16), acc=pltpu.VMEM((2 * width, total), F32),
        **layer_scratch(units, True),
    )
    far = ("returned", "sums_one", "xs", "ps") + BIG_WEIGHTS
    return call(body, "layer_zero", 44 if buffer_rows < 2 * total else 56, ins, outs, scratch, far)


def send_rows(ints, position, cotangent, strips, cap, full, balanced):
    total, width = cotangent.shape

    def body(s):
        near = [
            pltpu.make_async_copy(s.position.at[1], s.source.at[:, pl.ds(0, width)], s.sem.at[0]),
            pltpu.make_async_copy(s.cotangent, s.source.at[:, pl.ds(width, width)], s.sem.at[1]),
        ]
        for copy in near:
            copy.start()
        window, valid, dest, slot, shifted = [
            flat_row(r[...]) for r in (s.window, s.valid, s.dest, s.slot, s.shifted)
        ]
        live = valid > 0
        owner, key = dest, shifted
        if balanced:
            owner = (shifted + dest) & (strips - 1)
            key = dest * (WINDOWS // strips) + shifted // strips
            groups = max(strips, 16)
            hot = (iota((groups, total), 0) == jnp.where(live, owner, -1)).astype(F32)
            before, _ = counted(hot, groups)
            slot = jnp.concatenate(
                [
                    jnp.sum(hot[:, block(b)] * before[b], axis=0, keepdims=True)
                    for b in range(total // BLK)
                ],
                axis=1,
            ).astype(I32)
        fits = live & (slot < cap)
        over = jnp.max(jnp.where(live & (slot >= cap), 1, 0))
        place = jnp.where(fits, owner * cap + slot, -1)
        wide = jnp.where(fits, owner * full + slot, -1)
        s.meta[...] = jnp.concatenate([window, valid, place, wide, jnp.zeros((4, total), I32)], axis=0)
        at = iota((16, total), 0)
        rows = jnp.where(at == 0, key, jnp.where(at == 1, valid, 0)).astype(F32).astype(BF16)
        spot = iota((cap, total), 0)
        third = as_hot((iota((16, 2 * width), 0) == 2) & (over > 0))
        for copy in near:
            copy.wait()
        for d in range(strips):
            hot = as_hot(spot + d * cap == place)
            s.send[d, :cap, :] = dot(hot, s.source[...]).astype(BF16)
            tags = dot_nt(rows, hot)
            if cap < 2 * width:
                tags = jnp.concatenate([tags, jnp.zeros((16, 2 * width - cap), F32)], axis=1)
            s.send[d, cap:, :] = tags.astype(BF16) + third

    ins = dict(
        zip(("window", "valid", "dest", "slot", "shifted"), ints), position=position, cotangent=cotangent
    )
    outs = dict(send=sds((strips, cap + 16, 2 * width), BF16), meta=sds((8, total), I32))
    scratch = dict(source=pltpu.VMEM((total, 2 * width), BF16), sem=pltpu.SemaphoreType.DMA((2,)))
    return call(body, "send_rows", 24, ins, outs, scratch, ("position", "cotangent"))


def fetch_rows(meta, rows):
    total = meta.shape[1]
    buffer_rows, width = rows.shape

    def body(s):
        at = iota((BLK, buffer_rows), 1)
        for b in range(total // BLK):
            col = column(s.meta[3:4, block(b)].astype(F32)).astype(I32)
            hot = as_hot(jnp.concatenate([col] * (buffer_rows // BLK), axis=1) == at)
            s.out[block(b), :] = dot(hot, s.rows[...]).astype(BF16)

    return call(body, "fetch_rows", 16, dict(meta=meta, rows=rows), dict(out=sds((total, width), BF16)), {})["out"]


def unpack_sums(parts, who):
    width = parts[0].shape[1]

    def body(s):
        copies = [
            pltpu.make_async_copy(getattr(s, f"part{i}"), s.near.at[i], s.sem.at[i]) for i in range(len(parts))
        ]
        for copy in copies:
            copy.start()
        for i, copy in enumerate(copies):
            copy.wait()
            row = (s.who[0] ^ (i // 4)) * HALF_ROWS + (s.who[1] ^ (i % 4)) * PART_ROWS
            s.both[pl.ds(pl.multiple_of(row, 16), PART_ROWS), :] = s.near[i].astype(F32)
        s.over[0] = jnp.max(s.both[1032:GRAD_ROWS, :]).astype(I32)
        for level in range(2):
            at = level * GRAD_ROWS
            for b in range(3):
                s.w_qkv[level, :, block(b)] = s.both[at + b * BLK : at + (b + 1) * BLK, :]
            s.w_out[level] = s.both[at + 384 : at + 512, :]
            for b in range(2):
                s.w_up[level, :, block(b)] = s.both[at + 512 + b * BLK : at + 640 + b * BLK, :]
                s.b_up[level : level + 1, block(b)] = s.both[at + 1030 + b : at + 1031 + b, :]
            s.w_down[level] = s.both[at + 768 : at + 1024, :]
            s.gains[level] = s.both[at + 1024 : at + 1026, :]
            s.shifts[level] = s.both[at + 1026 : at + 1030, :]

    outs = dict(
        w_qkv=sds((2, width, 384), F32), w_out=sds((2, width, width), F32), w_up=sds((2, width, 256), F32),
        w_down=sds((2, 256, width), F32), b_up=sds((2, 256), F32), gains=sds((2, 2, width), F32),
        shifts=sds((2, 4, width), F32), over=sds((1,), I32),
    )
    names = [f"part{i}" for i in range(len(parts))]
    done = call(
        body, "unpack_sums", 16, dict(zip(names, parts), who=who), outs,
        dict(
            both=pltpu.VMEM((2 * HALF_ROWS, width), F32), near=pltpu.VMEM((len(parts), PART_ROWS, width), BF16),
            sem=pltpu.SemaphoreType.DMA((len(parts),)),
        ),
        names,
    )
    return tuple(done[n] for n in WEIGHTS), done["over"][0]


def paired_sum(parts):
    while len(parts) > 1:
        parts = [parts[i] + parts[i + 1] for i in range(0, len(parts), 2)]
    return parts[0]


def local(
    features, position, cotangent, w_qkv, w_out, w_up, w_down, b_up, gains, shifts,
    window, shifted_window, dest, slot, valid,
):
    strips, subs = lax.axis_size("strip"), lax.axis_size("sub")
    rows, width = features.shape
    full = 2 * rows // strips
    short = -(-(11 * full) // 256) * 16
    weights = (w_qkv, w_out, w_up, w_down, b_up, gains, shifts)

    def swap(x):
        return lax.all_to_all(x, "strip", split_axis=0, concat_axis=0, tiled=True)

    def trade(x, strip_mask, sub_mask):
        pairs = [
            (t * subs + u, (t ^ strip_mask) * subs + (u ^ sub_mask)) for t in range(strips) for u in range(subs)
        ]
        return lax.ppermute(x, ("strip", "sub"), pairs)

    at_strip, at_sub = lax.axis_index("strip"), lax.axis_index("sub")
    who = jnp.stack([at_sub & 1, ((at_sub >> 1) & 1) + 2 * (at_strip & 1), at_strip]).astype(I32)

    ints = [x.reshape(rows // BLK, BLK) for x in (window, valid, dest, slot, shifted_window)]

    square = ((0, 2), (1, 0), (1, 2))

    def total(parts):
        return paired_sum([x.astype(F32) for x in parts]).astype(BF16)

    def attempt(cap, balanced):
        sent = send_rows(ints, position, cotangent, strips, cap, full, balanced)
        arrived = swap(sent["send"])
        zero = forward_zero(sent["meta"], features, position, weights, strips, cap, who)
        cross = lax.ppermute(zero.pop("cross"), "strip", [(t, t ^ 1) for t in range(strips)])
        moved = []
        for h in range(strips // 2):
            pair = jnp.concatenate([zero.pop(f"own{h}"), cross[h * cap : (h + 1) * cap]], axis=0)
            moved.append(lax.ppermute(pair, "strip", [(t, (t + 2 * h) % strips) for t in range(strips)]) if h else pair)
        one = layer_one(arrived, moved, weights, full, who)
        returned = swap(one["dx"])
        out, sums_one, returned = lax.optimization_barrier((one["out"], one["wg"], returned))
        out = swap(out)
        last = layer_zero(zero, returned, weights, sums_one, one["over"], who)
        grad, out, *parts = lax.optimization_barrier(
            (last["grad"], out, *(last[f"{n}{m}"] for n in ("keep", "give") for m in range(4)))
        )
        cut = [total((k, trade(g, 0, 1))) for k, g in zip(parts[:4], parts[4:])]
        part = total([cut[0]] + [trade(x, *mask) for x, mask in zip(cut[1:], square)])
        part = total([part] + [trade(part, m, 0) for m in range(2, strips, 2)])
        output = fetch_rows(sent["meta"], out.reshape(strips * full, width))
        part, output = lax.optimization_barrier((part, output))
        mine = [part] + [trade(part, *mask) for mask in square]
        sums, over = unpack_sums(mine + [trade(x, 0, 1) for x in mine], who)
        return (output, grad) + sums, over > 0

    done, over = attempt(short, True)
    _, done = lax.while_loop(
        lambda state: state[0], lambda state: (state[0] & False, attempt(full, False)[0]), (over, done)
    )
    return done


def solution(mesh):
    rows = P(("strip", "sub"), None)
    flat = P(("strip", "sub"))
    placed = (rows, P(None, ("strip", "sub"), None), rows) + (P(),) * 7 + (flat,) * 5
    return jax.shard_map(
        local,
        mesh=mesh,
        in_specs=placed,
        out_specs=(rows, rows) + (P(),) * 7,
        check_vma=False,
    )
```

```python
import functools
import types

import jax
import jax.numpy as jnp
from jax import lax
from jax.experimental import pallas as pl
from jax.experimental.pallas import tpu as pltpu
from jax.sharding import PartitionSpec as P

HEADS = 8
EPS = 1e-05
NEGATIVE = -1e30
BLK = 128
UNIT = 2
WIDE = 4
UL = UNIT * BLK
WINDOWS = 64
BINS = 4
PAIR = 2
MIB = 1024 * 1024
F32, BF16, I32 = jnp.float32, jnp.bfloat16, jnp.int32
GRAD_ROWS = 1040
PART_ROWS = 272
HALF_ROWS = 4 * PART_ROWS
MICROS = dict(
    send_rows=4, forward_zero=9, layer_one=17, layer_zero=14, fetch_rows=3, unpack_sums=2
)
GELU_A = 0.7978845608028654
GELU_B = 0.044715


def dot(a, b):
    return lax.dot_general(a, b, (((1,), (0,)), ((), ())), preferred_element_type=F32)


def dot_nt(a, b):
    return lax.dot_general(a, b, (((1,), (1,)), ((), ())), preferred_element_type=F32)


def flip(x):
    return jnp.transpose(x.astype(F32)).astype(BF16)


def iota(shape, dim):
    return lax.broadcasted_iota(I32, shape, dim)


def as_hot(mask):
    return mask.astype(F32).astype(BF16)


def column(row):
    return jnp.transpose(jnp.broadcast_to(row, (BLK, BLK)))


def spread(x, n):
    return jnp.concatenate([x] * (n * UNIT), axis=1)


def get(ref, u, n):
    return jnp.concatenate([ref[u + i] for i in range(n)], axis=1)


def put(ref, u, n, x):
    for i in range(n):
        ref[u + i] = x[:, i * UL : (i + 1) * UL]


def flat_row(x):
    return jnp.concatenate([x[i : i + 1] for i in range(x.shape[0])], axis=1)


def block(b):
    return slice(b * BLK, (b + 1) * BLK)


def ranges(total, step):
    return [slice(at, min(at + step, total)) for at in range(0, total, step)]


def counted(hot, groups):
    blocks = hot.shape[1] // BLK
    low = hot.astype(BF16)
    stacked = jnp.concatenate([low[:, block(b)] for b in range(blocks)], axis=0)
    row_at, col_at = iota((BLK, 2 * BLK), 0), iota((BLK, 2 * BLK), 1)
    sums = dot(stacked, as_hot((row_at < col_at) | (col_at >= BLK)))
    carry = jnp.zeros((groups, BLK), F32)
    before = []
    for b in range(blocks):
        part = sums[b * groups : (b + 1) * groups]
        before.append(part[:, :BLK] + carry)
        carry = carry + part[:, BLK:]
    return before, carry


def take_seats(win, live, windows, scal_ref, cnt_ref, start_ref, seat_ref, pcol_ref):
    total = win.shape[1]
    hot = (iota((windows, total), 0) == jnp.where(live, win, -1)).astype(F32)
    before, carry = counted(hot, windows)
    counts = carry.astype(I32)
    cnt_ref[...] = counts
    zero = jnp.zeros((8, BLK), I32)
    rooms, ends = [zero] * BINS, [zero] * BINS
    fresh, largest = zero, zero
    sub = iota((8, BLK), 0)
    for g in range(windows // 8):
        tile = zero
        for i in range(8):
            w = 8 * g + i
            count = jnp.broadcast_to(counts[w : w + 1, :], (8, BLK))
            fits = [count <= r for r in rooms]
            start, free = fresh, None
            for k in reversed(range(BINS)):
                start = jnp.where(fits[k], ends[k], start)
            tile = jnp.where(sub == i, start, tile)
            taken = jnp.zeros((8, BLK), jnp.bool_)
            next_rooms, next_ends = [], []
            for k in range(BINS):
                here = fits[k] & jnp.logical_not(taken)
                taken = taken | fits[k]
                gone = jnp.where(here, count, 0)
                next_rooms.append(rooms[k] - gone)
                next_ends.append(ends[k] + gone)
            room_new = (-count) & (BLK - 1)
            end_new = fresh + count
            shifted_rooms = rooms[1:] + [room_new]
            shifted_ends = ends[1:] + [end_new]
            rooms = [jnp.where(taken, a, b) for a, b in zip(next_rooms, shifted_rooms)]
            ends = [jnp.where(taken, a, b) for a, b in zip(next_ends, shifted_ends)]
            fresh = jnp.where(taken, fresh, end_new + room_new)
            largest = jnp.maximum(largest, count)
        start_ref[8 * g : 8 * g + 8, :] = tile
    starts = start_ref[...].astype(F32)
    for b in range(total // BLK):
        seat = jnp.sum(hot[:, block(b)] * (before[b] + starts), axis=0, keepdims=True)
        seat = jnp.where(live[:, block(b)], seat, -1.0)
        seat_ref[:, block(b)] = jnp.broadcast_to(seat, (8, BLK)).astype(I32)
        pcol_ref[block(b), :] = column(seat).astype(I32)
    several = jnp.max(largest) > BLK
    scal_ref[0] = (jnp.max(fresh) + (UL - 1)) // UL
    scal_ref[1] = several.astype(I32)

    @pl.when(several)
    def _():
        at = iota((windows, BLK), 1)
        count, start = cnt_ref[...], start_ref[...]
        first = lax.shift_right_logical(start, 7)
        final = lax.shift_right_logical(start + jnp.maximum(count, 1) - 1, 7)
        touch = (count > 0) & (first <= at) & (at <= final)
        low_at = jnp.min(jnp.where(touch, first, at), axis=0, keepdims=True)
        high_at = jnp.max(jnp.where(touch, final, at), axis=0, keepdims=True)
        for b in range((scal_ref.shape[0] - 3) // 2):
            scal_ref[2 + 2 * b] = jnp.max(jnp.where(at[0:1] == b, low_at, 0))
            scal_ref[3 + 2 * b] = jnp.max(jnp.where(at[0:1] == b, high_at, 0))


def picked(pcol_ref, u, n):
    seat = iota((BLK, BLK), 1) + u * UL
    return jnp.concatenate(
        [
            jnp.concatenate(
                [as_hot(pcol_ref[block(b), :] == seat + t * BLK) for t in range(n * UNIT)], axis=1
            )
            for b in range(pcol_ref.shape[0] // BLK)
        ],
        axis=0,
    )


def norm_forward(hidden, gain, shift):
    size = hidden.shape[0]
    average = jnp.sum(hidden, axis=0, keepdims=True) * (1.0 / size)
    centered = hidden - average
    inverse = lax.rsqrt(jnp.sum(centered * centered, axis=0, keepdims=True) * (1.0 / size) + EPS)
    normed = centered * inverse
    return normed * gain + shift, normed, inverse


def norm_backward(upstream, normed, inverse, gain):
    size = upstream.shape[0]
    scaled = upstream * gain
    center = jnp.sum(scaled, axis=0, keepdims=True) * (1.0 / size)
    along = jnp.sum(scaled * normed, axis=0, keepdims=True) * (1.0 / size)
    return inverse * (scaled - center - normed * along)


def tiles(x):
    return x.reshape(x.shape[0] // 8, 8, x.shape[1])


def own_heads(x):
    size = x.shape[0] // HEADS
    return jnp.concatenate([x[h * size : (h + 1) * size, block(h)] for h in range(HEADS)], axis=0)


def whole_rows(x):
    return jnp.broadcast_to(x, (8, x.shape[1]))


def put_heads(ref, t, at, x):
    size = x.shape[0] // HEADS
    for h in range(HEADS):
        ref[t, at + h * size : at + (h + 1) * size, block(h)] = x[h * size : (h + 1) * size]


BIG_WEIGHTS = ("w_qkv", "w_out", "w_up", "w_down")


def weight_copies(s, level):
    pairs = zip(BIG_WEIGHTS, (s.wqkv, s.wout, s.wup, s.wdown))
    return [
        pltpu.make_async_copy(getattr(s, name).at[level], ref, s.wsem.at[i])
        for i, (name, ref) in enumerate(pairs)
    ]


def setup_weights(s, level, copies):
    s.stack[...] = jnp.zeros(s.stack.shape, BF16)
    for b in range(2):
        s.cols[6 + b] = column(s.b_up[level : level + 1, block(b)])
        s.cols[b] = column(s.gains[level, b : b + 1, :])
    for b in range(4):
        s.cols[2 + b] = column(s.shifts[level, b : b + 1, :])
    for copy in copies:
        copy.wait()
    for b in range(3):
        s.wqkvt[block(b), :] = flip(s.wqkv[:, block(b)])
    s.woutt[...] = flip(s.wout[...])
    for b in range(2):
        s.wupt[block(b), :] = flip(s.wup[:, block(b)])
        s.wdownt[:, block(b)] = flip(s.wdown[block(b), :])


def project(s, u, n, low, placing, ids):
    width = low.shape[0]
    head = width // HEADS
    joined = (low.astype(F32) + placing).astype(BF16)
    put(s.xt, u, n, low)
    put(s.ut, u, n, joined)
    qk = dot(s.wqkvt[: 2 * width], joined).astype(BF16).astype(F32)
    vt = dot(s.wqkvt[2 * width :], low).astype(BF16).astype(F32)
    put(s.qt, u, n, (qk[:width] * (head ** (-0.5))).astype(BF16))
    kt = qk[width:]
    ones = jnp.ones((head, BLK), BF16)
    for t in range(n * UNIT):
        b = UNIT * u + t
        s.kt[b] = kt[:, block(t)].astype(BF16)
        for h in range(HEADS):
            s.vt[b, 2 * h * head : (2 * h + 1) * head, :] = vt[h * head : (h + 1) * head, block(t)].astype(BF16)
            s.vt[b, (2 * h + 1) * head : (2 * h + 2) * head, :] = ones
        s.k[b] = jnp.transpose(kt[:, block(t)]).astype(BF16)
        s.idcol[b] = column(ids[:, block(t)])
        s.idrow[b] = jnp.broadcast_to(ids[:, block(t)], (8, BLK))
        if s.backward:
            s.v[b] = jnp.transpose(vt[:, block(t)]).astype(BF16)
            s.dk[b] = jnp.zeros((width, BLK), F32)
            s.dv[b] = jnp.zeros((width, BLK), F32)


def other_window(s, keys, queries):
    return jnp.where(s.idcol[keys] == s.idrow[queries][0:1], 0.0, NEGATIVE)


def attend(s, u, n, single):
    qt = get(s.qt, u, n)
    width = qt.shape[0]
    head = width // HEADS
    mixed, inverses = [], []
    for t in range(n * UNIT):
        b = UNIT * u + t
        put_heads(s.stack, t, 0, qt[:, block(t)])
        if single:
            scores = dot(s.k[b], s.stack[t, :width])
            bias = other_window(s, b, b)
            sums = []
            for p in range(0, HEADS, PAIR):
                es = []
                for h in range(p, p + PAIR):
                    part = scores[:, block(h)] + bias
                    top = jnp.max(part, axis=0, keepdims=True)
                    es.append(jnp.exp(part - top).astype(BF16))
                es = jnp.concatenate(es, axis=1)
                if s.backward:
                    s.e[t, :, p * BLK : (p + PAIR) * BLK] = es
                got = dot(s.vt[b, 2 * p * head : 2 * (p + PAIR) * head, :], es)
                sums += [got[2 * i * head : (2 * i + 2) * head, block(i)] for i in range(PAIR)]
        else:
            lo, hi = s.scal[2 + 2 * b], s.scal[3 + 2 * b] + 1

            def step_top(j, top, t=t, b=b):
                return jnp.maximum(top, jnp.max(tiles(masked_scores(s, j, t, b)), axis=0))

            top = lax.fori_loop(lo, hi, step_top, jnp.full((8, HEADS * BLK), 2 * NEGATIVE, F32))
            s.stat[t] = whole_rows(jnp.max(top, axis=0, keepdims=True))

            def step_mix(j, out, t=t, b=b):
                e = weights_of(s, j, t, b)
                return out + own_heads(dot(s.vt[j], e))

            out = lax.fori_loop(lo, hi, step_mix, jnp.zeros((2 * width, BLK), F32))
            sums = [out[2 * h * head : (2 * h + 2) * head] for h in range(HEADS)]
        inverse = [1.0 / x[head : head + 1] for x in sums]
        mixed.append(jnp.concatenate([x[:head] * i for x, i in zip(sums, inverse)], axis=0))
        inverses.append(inverse)
    return jnp.concatenate(mixed, axis=1), inverses


def masked_scores(s, j, t, b):
    bias = jnp.concatenate([other_window(s, j, b)] * HEADS, axis=1)
    return dot(s.k[j], s.stack[t, : s.k.shape[2]]) + bias


def weights_of(s, j, t, b):
    scores = masked_scores(s, j, t, b)
    return jnp.exp(tiles(scores) - s.stat[t][None]).reshape(BLK, HEADS * BLK).astype(BF16)


def attend_back(s, u, n, single, mixed, inverses, mixed_grad):
    width = mixed.shape[0]
    head = width // HEADS
    dqs = []
    for t in range(n * UNIT):
        b = UNIT * u + t
        levels = []
        for h in range(HEADS):
            rows = slice(h * head, (h + 1) * head)
            pull = (mixed_grad[rows, block(t)] * inverses[t][h]).astype(BF16)
            levels.append(jnp.sum(pull.astype(F32) * mixed[rows, block(t)], axis=0, keepdims=True))
            s.stack[t, width + h * head : width + (h + 1) * head, block(h)] = pull
        if single:
            slopes = dot(s.v[b], s.stack[t, width:])
            parts = []
            for p in range(0, HEADS, PAIR):
                gs = []
                for h in range(p, p + PAIR):
                    e = s.e[t, :, block(h)].astype(F32)
                    gs.append((e * (slopes[:, block(h)] - levels[h])).astype(BF16))
                gs = jnp.concatenate(gs, axis=1)
                rows, lanes = slice(p * head, (p + PAIR) * head), slice(p * BLK, (p + PAIR) * BLK)
                s.dk[b, rows, :] = dot_nt(s.stack[t, rows, lanes], gs)
                pulled = slice(width + p * head, width + (p + PAIR) * head)
                s.dv[b, rows, :] = dot_nt(s.stack[t, pulled, lanes], s.e[t, :, lanes])
                got = dot(s.kt[b, p * head : (p + PAIR) * head, :], gs)
                parts += [got[i * head : (i + 1) * head, block(i)] for i in range(PAIR)]
            dq = jnp.concatenate(parts, axis=0)
        else:
            lo, hi = s.scal[2 + 2 * b], s.scal[3 + 2 * b] + 1
            s.level[t] = whole_rows(jnp.concatenate(levels, axis=1))

            def step(j, dq, t=t, b=b):
                e = weights_of(s, j, t, b)
                slopes = tiles(dot(s.v[j], s.stack[t, width:])) - s.level[t][None]
                g = (e.astype(F32) * slopes.reshape(BLK, HEADS * BLK)).astype(BF16)
                s.dv[j] += dot_nt(s.stack[t, width:], e)
                s.dk[j] += dot_nt(s.stack[t, :width], g)
                return dq + own_heads(dot(s.kt[j], g))

            dq = lax.fori_loop(lo, hi, step, jnp.zeros((width, BLK), F32))
        dqs.append((dq * (head ** (-0.5))).astype(BF16))
    put(s.dq, u, n, jnp.concatenate(dqs, axis=1))


def fold(x):
    return sum(x[:, block(t)] for t in range(x.shape[1] // BLK))


def layer_units(s, u, n, single, upstream_of):
    mixed, inverses = attend(s, u, n, single)
    mixed_low = mixed.astype(BF16)
    spread_n = functools.partial(spread, n=n)
    gain_one, gain_two = spread_n(s.cols[0]), spread_n(s.cols[1])
    attended = dot(s.woutt[...], mixed_low) + spread_n(s.cols[2])
    first_out, normed_one, inverse_one = norm_forward(
        get(s.xt, u, n).astype(F32) + attended, gain_one, spread_n(s.cols[3])
    )
    first_low = first_out.astype(BF16)
    bias_up = jnp.concatenate([spread_n(s.cols[6]), spread_n(s.cols[7])], axis=0)
    before = dot(s.wupt[...], first_low) + bias_up
    square = before * before
    bend = jnp.tanh(before * (GELU_A + (GELU_A * GELU_B) * square))
    half = 0.5 + 0.5 * bend
    activated = (before * half).astype(BF16)
    branch = dot(s.wdownt[...], activated) + spread_n(s.cols[4])
    result, normed_two, inverse_two = norm_forward(first_out + branch, gain_two, spread_n(s.cols[5]))
    if upstream_of is None:
        return result.astype(BF16)
    upstream = upstream_of(u, n)
    ones = jnp.ones((16, n * UL), BF16)
    s.gg[0] += fold(upstream * normed_two)
    s.gg[1] += fold(upstream)
    second = norm_backward(upstream, normed_two, inverse_two, gain_two)
    branch_low = second.astype(BF16)
    s.gd[...] += dot_nt(jnp.concatenate([activated, ones], axis=0), branch_low)
    slope = half + half * (1.0 - bend) * before * (GELU_A + (3.0 * GELU_A * GELU_B) * square)
    before_low = (dot(s.wdown[...], branch_low) * slope).astype(BF16)
    s.gu[...] += dot_nt(jnp.concatenate([first_low, ones], axis=0), before_low)
    first_grad = second + dot(s.wup[...], before_low)
    s.gg[2] += fold(first_grad * normed_one)
    s.gg[3] += fold(first_grad)
    residual = norm_backward(first_grad, normed_one, inverse_one, gain_one)
    put(s.dh, u, n, residual)
    attended_low = residual.astype(BF16)
    s.go[...] += dot_nt(jnp.concatenate([mixed_low, ones], axis=0), attended_low)
    attend_back(s, u, n, single, mixed, inverses, dot(s.wout[...], attended_low))
    return result.astype(BF16)


def finish_units(s, u, n):
    width = s.xt.shape[1]
    dq = get(s.dq, u, n)
    blocks = [UNIT * u + t for t in range(n * UNIT)]
    dk = jnp.concatenate([s.dk[b] for b in blocks], axis=1).astype(BF16)
    dv = jnp.concatenate([s.dv[b] for b in blocks], axis=1).astype(BF16)
    dx = get(s.dh, u, n) + dot(s.wqkv[...], jnp.concatenate([dq, dk, dv], axis=0))
    joined = get(s.ut, u, n)
    s.gq[0] += dot_nt(joined, dq)
    s.gq[1] += dot_nt(joined, dk)
    s.gq[2] += dot_nt(get(s.xt, u, n), dv)
    return dx


def write_sums(s, wg_ref, mark):
    width = s.xt.shape[1]
    for b in range(3):
        wg_ref[block(b), :] = s.gq[b].astype(BF16)
    wg_ref[384:512, :] = s.go[:width].astype(BF16)
    for b in range(2):
        wg_ref[512 + b * BLK : 640 + b * BLK, :] = s.gu[:width, block(b)].astype(BF16)
    wg_ref[768:1024, :] = s.gd[:256].astype(BF16)
    sums = [jnp.sum(jnp.transpose(s.gg[i]), axis=0, keepdims=True) for i in range(4)]
    out_bias, down_bias = s.go[width : width + 1], s.gd[256:257]
    up_bias = s.gu[width : width + 1]
    small = [
        sums[2], sums[0], out_bias, sums[3], down_bias, sums[1], up_bias[:, :BLK], up_bias[:, BLK:],
        jnp.full((8, BLK), mark, F32),
    ]
    wg_ref[1024:GRAD_ROWS, :] = jnp.concatenate(small, axis=0).astype(BF16)


def zero_sums(s):
    for ref in (s.gq, s.go, s.gu, s.gd, s.gg):
        ref[...] = jnp.zeros(ref.shape, F32)


WEIGHTS = ("w_qkv", "w_out", "w_up", "w_down", "b_up", "gains", "shifts")


def layer_scratch(units, backward):
    vm = pltpu.VMEM
    width, blocks, most = 128, units * UNIT, WIDE * UNIT
    lanes = lambda dtype: vm((units, width, UL), dtype)
    out = dict(
        wqkv=vm((width, 384), BF16), wout=vm((width, width), BF16), wup=vm((width, 256), BF16),
        wdown=vm((256, width), BF16), wsem=pltpu.SemaphoreType.DMA((4,)),
        wqkvt=vm((384, width), BF16), woutt=vm((width, width), BF16), wupt=vm((256, width), BF16),
        wdownt=vm((width, 256), BF16), cols=vm((8, BLK, BLK), F32),
        xt=lanes(BF16), ut=lanes(BF16), qt=lanes(BF16),
        kt=vm((blocks, width, BLK), BF16), vt=vm((blocks, 2 * width, BLK), BF16),
        k=vm((blocks, BLK, width), BF16),
        idcol=vm((blocks, BLK, BLK), F32), idrow=vm((blocks, 8, BLK), F32),
        stat=vm((UNIT, 8, HEADS * BLK), F32), level=vm((UNIT, 8, HEADS * BLK), F32),
        stack=vm((most, 2 * width, HEADS * BLK), BF16),
    )
    if backward:
        out.update(
            v=vm((blocks, BLK, width), BF16), e=vm((most, BLK, HEADS * BLK), BF16),
            dh=lanes(F32), dq=lanes(BF16),
            dk=vm((blocks, width, BLK), F32), dv=vm((blocks, width, BLK), F32),
            gq=vm((3, width, width), F32), go=vm((width + 16, width), F32), gu=vm((width + 16, 256), F32),
            gd=vm((256 + 16, width), F32), gg=vm((4, width, BLK), F32),
        )
    return out


def seat_scratch(windows):
    return dict(cnt=pltpu.VMEM((windows, BLK), I32), start=pltpu.VMEM((windows, BLK), I32))


def call(body, name, vmem, ins, outs, scratch, far=()):
    names = list(ins) + list(outs) + list(scratch)

    def kernel(*refs):
        body(types.SimpleNamespace(**dict(zip(names, refs))))

    def spec(n):
        space = pltpu.SMEM if n in ("scal", "who", "over") else pl.ANY if n in far else pltpu.VMEM
        return pl.BlockSpec(memory_space=space)

    result = pl.pallas_call(
        kernel,
        out_shape=tuple(outs.values()),
        in_specs=[spec(n) for n in ins],
        out_specs=tuple(spec(n) for n in outs),
        scratch_shapes=list(scratch.values()),
        compiler_params=pltpu.CompilerParams(vmem_limit_bytes=vmem * MIB),
        cost_estimate=pl.CostEstimate(flops=MICROS[name] * 10**9, bytes_accessed=2**20, transcendentals=0),
        name=name,
    )(*ins.values())
    return dict(zip(outs, result))


def sds(shape, dtype):
    return jax.ShapeDtypeStruct(shape, dtype)


def units_of(total):
    return -(-total // (64 * UNIT * WIDE)) * WIDE


def wide_steps(s):
    return (s.scal[0] + 1) // WIDE


def for_units(s, body, by_window=False):
    wide, last = wide_steps(s), s.scal[0]
    if by_window:
        last = jnp.where(s.scal[1] == 0, last, covered(s))
        wide = jnp.where(s.scal[1] == 0, wide, 0)

    @pl.loop(0, wide)
    def _(c):
        body(c * WIDE, WIDE, *([True] if by_window else []))

    @pl.loop(wide * WIDE, last)
    def _(u):
        if not by_window:
            body(u, 1)
            return

        blocks = [UNIT * u + t for t in range(UNIT)]
        inside = [(s.scal[2 + 2 * b] == b) & (s.scal[3 + 2 * b] == b) for b in blocks]
        single = (s.scal[1] == 0) | functools.reduce(jnp.logical_and, inside)

        @pl.when(single)
        def _():
            body(u, 1, True)

        @pl.when(jnp.logical_not(single))
        def _():
            body(u, 1, False)


def covered(s):
    return jnp.maximum(s.scal[0], wide_steps(s) * WIDE)


def unit_copies(s, pairs):
    def copy(i, u):
        source, target = pairs[i]
        return pltpu.make_async_copy(source.at[u], target.at[u], s.usem.at[i, u])

    def start():
        @pl.loop(0, covered(s))
        def _(u):
            for i in range(len(pairs)):
                copy(i, u).start()

    def wait():
        @pl.loop(0, covered(s))
        def _(u):
            for i in range(len(pairs)):
                copy(i, u).wait()

    return start, wait


def forward_zero(meta, features, position, weights, strips, cap, who):
    total, width = features.shape
    units = units_of(total)
    buffer_rows = strips * cap

    def body(s):
        s.backward = False
        near = [
            pltpu.make_async_copy(s.features, s.x, s.sem.at[0]),
            pltpu.make_async_copy(s.position.at[0], s.p, s.sem.at[1]),
        ]
        copies = weight_copies(s, 0)
        for copy in near + copies:
            copy.start()
        meta = s.meta[...]
        live = meta[1:2] > 0
        take_seats(meta[0:1], live, WINDOWS // 2, s.scal, s.cnt, s.start, s.seat, s.pcol)
        setup_weights(s, 0, copies)
        for copy in near:
            copy.wait()
        for b in range(total // BLK):
            s.srct[:width, block(b)] = flip(s.x[block(b), :])
            s.srct[width : 2 * width, block(b)] = flip(s.p[block(b), :])
        at = iota((16, total), 0)
        place = meta[2:3]
        rows = jnp.where(at == 0, meta[0:1] + 1, jnp.where(at == 1, 1, 0))
        rows = jnp.where(at == 2, place >> 8, jnp.where(at == 3, place & 255, rows))
        s.srct[2 * width :, :] = rows.astype(F32).astype(BF16)
        s.acc[...] = jnp.zeros(s.acc.shape, F32)

        def begin(u, n):
            moved = dot(s.srct[...], picked(s.pcol, u, n))
            tags = moved[2 * width :]
            low = moved[:width].astype(BF16)
            put(s.pt, u, n, moved[width : 2 * width].astype(BF16))
            put(s.ids, u, n, whole_rows(tags[0:1]))
            spot = jnp.where(tags[1:2] > 0.5, tags[2:3] * 256 + tags[3:4], -1.0)
            put(s.spot, u, n, whole_rows(spot).astype(I32))
            for t in range(n * UNIT):
                s.spotcol[UNIT * u + t] = column(spot[:, block(t)]).astype(I32)
            project(s, u, n, low, moved[width : 2 * width], tags[0:1])

        for_units(s, begin)
        start, wait = unit_copies(s, [(s.xt, s.xs), (s.pt, s.ps)])
        start()

        def run(u, n, single):
            out = layer_units(s, u, n, single, None)
            for lanes in ranges(buffer_rows, 512):
                copies = (lanes.stop - lanes.start) // BLK
                at = iota((BLK, copies * BLK), 1) + lanes.start
                hot = jnp.concatenate(
                    [
                        as_hot(jnp.concatenate([s.spotcol[UNIT * u + t]] * copies, axis=1) == at)
                        for t in range(n * UNIT)
                    ],
                    axis=0,
                )
                s.acc[:, lanes] += dot(out, hot)

        for_units(s, run, True)
        for r in range(buffer_rows // BLK):
            s.flat[block(r), :] = jnp.transpose(s.acc[:, block(r)]).astype(BF16)
        for h in range(strips // 2):
            strip = (s.who[2] + 2 * h) & (strips - 1)
            getattr(s, f"own{h}")[...] = s.flat[pl.ds(pl.multiple_of(strip * cap, 16), cap), :]
            row = pl.multiple_of((strip ^ 1) * cap, 16)
            s.cross[h * cap : (h + 1) * cap, :] = s.flat[pl.ds(row, cap), :]
        wait()

    ins = dict(meta=meta, features=features, position=position, who=who, **dict(zip(WEIGHTS, weights)))
    outs = dict(
        {f"own{h}": sds((cap, width), BF16) for h in range(strips // 2)},
        cross=sds((buffer_rows // 2, width), BF16),
        xs=sds((units, width, UL), BF16), ps=sds((units, width, UL), BF16),
        ids=sds((units, 8, UL), F32), spot=sds((units, 8, UL), I32), seat=sds((8, total), I32),
        scal=sds((3 + 2 * units * UNIT,), I32),
    )
    scratch = dict(
        x=pltpu.VMEM((total, width), BF16), p=pltpu.VMEM((total, width), BF16),
        sem=pltpu.SemaphoreType.DMA((2,)), usem=pltpu.SemaphoreType.DMA((2, units)),
        pt=pltpu.VMEM((units, width, UL), BF16),
        pcol=pltpu.VMEM((total, BLK), I32), srct=pltpu.VMEM((2 * width + 16, total), BF16),
        flat=pltpu.VMEM((buffer_rows, width), BF16),
        acc=pltpu.VMEM((width, buffer_rows), F32), spotcol=pltpu.VMEM((units * UNIT, BLK, BLK), I32),
        **seat_scratch(WINDOWS // 2), **layer_scratch(units, False),
    )
    far = ("features", "position", "xs", "ps") + BIG_WEIGHTS
    return call(body, "forward_zero", 44, ins, outs, scratch, far)


def scatter(s, u, n, pair):
    for lanes in ranges(s.seat.shape[1], 256):
        seat = s.seat[0:1, lanes] - u * UL
        hot = as_hot(iota((n * UL, lanes.stop - lanes.start), 0) == seat)
        s.acc[:, lanes] += dot(pair, hot)


def layer_one(first, arrived, weights, full, who):
    strips, width = 2 * len(arrived), arrived[0].shape[1]
    cap = arrived[0].shape[0] // 2
    total = strips * cap
    units = units_of(total)

    def body(s):
        s.backward = True
        near, tags, rest = [], [], []
        for d in range(strips):
            rows = pl.ds(d * cap, cap)
            tags.append(pltpu.make_async_copy(s.first.at[d, pl.ds(cap, 16), :], s.tagged.at[d], s.tsem.at[d]))
            rest.append(pltpu.make_async_copy(s.first.at[d, pl.ds(0, cap), :], s.pc.at[rows, :], s.rsem.at[d]))
            h, x = divmod(d, 2)
            row = pl.multiple_of((((s.who[2] - 2 * h) & (strips - 1)) ^ x) * cap, 16)
            source = getattr(s, f"arrived{h}").at[pl.ds(x * cap, cap), :]
            near.append(pltpu.make_async_copy(source, s.x.at[pl.ds(row, cap), :], s.sem.at[d]))
        copies = weight_copies(s, 1)
        for copy in tags + rest + near + copies:
            copy.start()
        zero_sums(s)
        s.acc[...] = jnp.zeros(s.acc.shape, F32)
        for copy in tags:
            copy.wait()
        for d in range(strips):
            s.tags[:, d * cap : (d + 1) * cap] = s.tagged[d, :, :cap].astype(F32)[:8]
        key, live = s.tags[0:1, :].astype(I32), s.tags[1:2, :] > 0.5
        s.over[0] = jnp.max(s.tags[2:3, :]).astype(I32)
        take_seats(key, live, WINDOWS, s.scal, s.cnt, s.start, s.seat, s.pcol)
        setup_weights(s, 1, copies)
        for copy in rest + near:
            copy.wait()
        for b in range(total // BLK):
            s.srct[:width, block(b)] = flip(s.x[block(b), :])
            s.srct[width : 3 * width, block(b)] = flip(s.pc[block(b), :])
        rows = jnp.where(iota((16, total), 0) == 0, key + 1, 0)
        s.srct[3 * width :, :] = rows.astype(F32).astype(BF16)

        def begin(u, n):
            moved = dot(s.srct[...], picked(s.pcol, u, n))
            put(s.dyt, u, n, moved[2 * width : 3 * width].astype(BF16))
            ids = moved[3 * width : 3 * width + 1]
            project(s, u, n, moved[:width].astype(BF16), moved[width : 2 * width], ids)

        def run(u, n, single):
            out = layer_units(s, u, n, single, lambda u, n: get(s.dyt, u, n).astype(F32))
            put(s.yt, u, n, out)

        def end(u, n):
            dx = finish_units(s, u, n)
            scatter(s, u, n, jnp.concatenate([get(s.yt, u, n), dx.astype(BF16)], axis=0))

        for_units(s, begin)
        for_units(s, run, True)
        for_units(s, end)
        for r in range(total // BLK):
            s.flat[block(r), :] = jnp.transpose(s.acc[:width, block(r)]).astype(BF16)
            s.dx[block(r), :] = jnp.transpose(s.acc[width:, block(r)]).astype(BF16)
        for d in range(strips):
            s.out[d, :cap, :] = s.flat[d * cap : (d + 1) * cap, :]
            if cap < full:
                s.out[d, cap:, :] = jnp.zeros((full - cap, width), BF16)
        write_sums(s, s.wg, 0.0)

    ins = dict(
        first=first, who=who, **{f"arrived{d}": x for d, x in enumerate(arrived)}, **dict(zip(WEIGHTS, weights))
    )
    outs = dict(
        dx=sds((total, width), BF16), out=sds((strips, full, width), BF16), wg=sds((GRAD_ROWS, width), BF16),
        over=sds((1,), I32),
    )
    vm, lanes = pltpu.VMEM, pltpu.VMEM((units, width, UL), BF16)
    sems = pltpu.SemaphoreType.DMA((strips,))
    scratch = dict(
        x=vm((total, width), BF16), pc=vm((total, 2 * width), BF16), tagged=vm((strips, 16, 2 * width), BF16),
        tags=vm((8, total), F32), sem=sems, tsem=sems, rsem=sems, dyt=lanes, yt=lanes,
        scal=pltpu.SMEM((3 + 2 * units * UNIT,), I32), seat=vm((8, total), I32),
        flat=vm((total, width), BF16), pcol=vm((total, BLK), I32),
        srct=vm((3 * width + 16, total), BF16), acc=vm((2 * width, total), F32),
        **seat_scratch(WINDOWS), **layer_scratch(units, True),
    )
    far = ("first",) + tuple(f"arrived{h}" for h in range(strips // 2)) + BIG_WEIGHTS
    return call(body, "layer_one", 44 if cap < full else 56, ins, outs, scratch, far)


def layer_zero(ready, returned, weights, sums_one, over, who):
    total, width = ready["seat"].shape[1], returned.shape[1]
    units = units_of(total)
    buffer_rows = returned.shape[0]

    def body(s):
        s.backward = True
        near = [
            pltpu.make_async_copy(s.returned, s.x, s.sem.at[0]),
            pltpu.make_async_copy(s.sums_one, s.both.at[pl.ds(GRAD_ROWS, GRAD_ROWS), :], s.sem.at[1]),
        ]
        copies = weight_copies(s, 0)
        start, wait = unit_copies(s, [(s.xs, s.xz), (s.ps, s.pt)])
        start()
        for copy in copies + near:
            copy.start()
        zero_sums(s)
        s.acc[...] = jnp.zeros(s.acc.shape, F32)
        setup_weights(s, 0, copies)
        wait()
        near[0].wait()
        for b in range(buffer_rows // BLK):
            s.srct[:, block(b)] = flip(s.x[block(b), :])

        def begin(u, n):
            project(s, u, n, get(s.xz, u, n), get(s.pt, u, n).astype(F32), get(s.ids, u, n)[0:1])

        def upstream_of(u, n):
            return dot(s.srct[...], as_hot(iota((buffer_rows, n * UL), 0) == get(s.spot, u, n)[0:1]))

        def end(u, n):
            dx = finish_units(s, u, n)
            high = dx.astype(BF16)
            scatter(s, u, n, jnp.concatenate([high, (dx - high.astype(F32)).astype(BF16)], axis=0))

        for_units(s, begin)
        for_units(s, lambda u, n, single: layer_units(s, u, n, single, upstream_of), True)
        for_units(s, end)
        for r in range(total // BLK):
            s.grad[block(r), :] = jnp.transpose(s.acc[:width, block(r)] + s.acc[width:, block(r)])
        write_sums(s, s.both, s.over[0].astype(F32))
        near[1].wait()
        s.both[2 * GRAD_ROWS :, :] = jnp.zeros((2 * HALF_ROWS - 2 * GRAD_ROWS, width), BF16)
        for a, name in enumerate(("keep", "give")):
            for m in range(4):
                row = (s.who[0] ^ a) * HALF_ROWS + (s.who[1] ^ m) * PART_ROWS
                getattr(s, f"{name}{m}")[...] = s.both[pl.ds(pl.multiple_of(row, 16), PART_ROWS), :]

    ins = dict(
        {k: ready[k] for k in ("scal", "xs", "ps", "ids", "spot", "seat")}, returned=returned,
        sums_one=sums_one, over=over, who=who, **dict(zip(WEIGHTS, weights)),
    )
    part = pltpu.VMEM((PART_ROWS, width), BF16)
    outs = dict(grad=sds((total, width), F32), **{f"{n}{m}": part for n in ("keep", "give") for m in range(4)})
    lanes = pltpu.VMEM((units, width, UL), BF16)
    scratch = dict(
        x=pltpu.VMEM((buffer_rows, width), BF16), sem=pltpu.SemaphoreType.DMA((2,)),
        usem=pltpu.SemaphoreType.DMA((2, units)), xz=lanes, pt=lanes,
        both=pltpu.VMEM((2 * HALF_ROWS, width), BF16),
        srct=pltpu.VMEM((width, buffer_rows), BF16), acc=pltpu.VMEM((2 * width, total), F32),
        **layer_scratch(units, True),
    )
    far = ("returned", "sums_one", "xs", "ps") + BIG_WEIGHTS
    return call(body, "layer_zero", 44 if buffer_rows < 2 * total else 56, ins, outs, scratch, far)


def send_rows(ints, position, cotangent, strips, cap, full, balanced):
    total, width = cotangent.shape

    def body(s):
        near = [
            pltpu.make_async_copy(s.position.at[1], s.source.at[:, pl.ds(0, width)], s.sem.at[0]),
            pltpu.make_async_copy(s.cotangent, s.source.at[:, pl.ds(width, width)], s.sem.at[1]),
        ]
        for copy in near:
            copy.start()
        window, valid, dest, slot, shifted = [
            flat_row(r[...]) for r in (s.window, s.valid, s.dest, s.slot, s.shifted)
        ]
        live = valid > 0
        owner, key = dest, shifted
        if balanced:
            owner = (shifted + dest) & (strips - 1)
            key = dest * (WINDOWS // strips) + shifted // strips
            groups = max(strips, 16)
            hot = (iota((groups, total), 0) == jnp.where(live, owner, -1)).astype(F32)
            before, _ = counted(hot, groups)
            slot = jnp.concatenate(
                [
                    jnp.sum(hot[:, block(b)] * before[b], axis=0, keepdims=True)
                    for b in range(total // BLK)
                ],
                axis=1,
            ).astype(I32)
        fits = live & (slot < cap)
        over = jnp.max(jnp.where(live & (slot >= cap), 1, 0))
        place = jnp.where(fits, owner * cap + slot, -1)
        wide = jnp.where(fits, owner * full + slot, -1)
        s.meta[...] = jnp.concatenate([window, valid, place, wide, jnp.zeros((4, total), I32)], axis=0)
        at = iota((16, total), 0)
        rows = jnp.where(at == 0, key, jnp.where(at == 1, valid, 0)).astype(F32).astype(BF16)
        spot = iota((cap, total), 0)
        third = as_hot((iota((16, 2 * width), 0) == 2) & (over > 0))
        for copy in near:
            copy.wait()
        for d in range(strips):
            hot = as_hot(spot + d * cap == place)
            s.send[d, :cap, :] = dot(hot, s.source[...]).astype(BF16)
            tags = dot_nt(rows, hot)
            if cap < 2 * width:
                tags = jnp.concatenate([tags, jnp.zeros((16, 2 * width - cap), F32)], axis=1)
            s.send[d, cap:, :] = tags.astype(BF16) + third

    ins = dict(
        zip(("window", "valid", "dest", "slot", "shifted"), ints), position=position, cotangent=cotangent
    )
    outs = dict(send=sds((strips, cap + 16, 2 * width), BF16), meta=sds((8, total), I32))
    scratch = dict(source=pltpu.VMEM((total, 2 * width), BF16), sem=pltpu.SemaphoreType.DMA((2,)))
    return call(body, "send_rows", 24, ins, outs, scratch, ("position", "cotangent"))


def fetch_rows(meta, rows):
    total = meta.shape[1]
    buffer_rows, width = rows.shape

    def body(s):
        at = iota((BLK, buffer_rows), 1)
        for b in range(total // BLK):
            col = column(s.meta[3:4, block(b)].astype(F32)).astype(I32)
            hot = as_hot(jnp.concatenate([col] * (buffer_rows // BLK), axis=1) == at)
            s.out[block(b), :] = dot(hot, s.rows[...]).astype(BF16)

    return call(body, "fetch_rows", 16, dict(meta=meta, rows=rows), dict(out=sds((total, width), BF16)), {})["out"]


def unpack_sums(parts, who):
    width = parts[0].shape[1]

    def body(s):
        copies = [
            pltpu.make_async_copy(getattr(s, f"part{i}"), s.near.at[i], s.sem.at[i]) for i in range(len(parts))
        ]
        for copy in copies:
            copy.start()
        for i, copy in enumerate(copies):
            copy.wait()
            row = (s.who[0] ^ (i // 4)) * HALF_ROWS + (s.who[1] ^ (i % 4)) * PART_ROWS
            s.both[pl.ds(pl.multiple_of(row, 16), PART_ROWS), :] = s.near[i].astype(F32)
        s.over[0] = jnp.max(s.both[1032:GRAD_ROWS, :]).astype(I32)
        for level in range(2):
            at = level * GRAD_ROWS
            for b in range(3):
                s.w_qkv[level, :, block(b)] = s.both[at + b * BLK : at + (b + 1) * BLK, :]
            s.w_out[level] = s.both[at + 384 : at + 512, :]
            for b in range(2):
                s.w_up[level, :, block(b)] = s.both[at + 512 + b * BLK : at + 640 + b * BLK, :]
                s.b_up[level : level + 1, block(b)] = s.both[at + 1030 + b : at + 1031 + b, :]
            s.w_down[level] = s.both[at + 768 : at + 1024, :]
            s.gains[level] = s.both[at + 1024 : at + 1026, :]
            s.shifts[level] = s.both[at + 1026 : at + 1030, :]

    outs = dict(
        w_qkv=sds((2, width, 384), F32), w_out=sds((2, width, width), F32), w_up=sds((2, width, 256), F32),
        w_down=sds((2, 256, width), F32), b_up=sds((2, 256), F32), gains=sds((2, 2, width), F32),
        shifts=sds((2, 4, width), F32), over=sds((1,), I32),
    )
    names = [f"part{i}" for i in range(len(parts))]
    done = call(
        body, "unpack_sums", 16, dict(zip(names, parts), who=who), outs,
        dict(
            both=pltpu.VMEM((2 * HALF_ROWS, width), F32), near=pltpu.VMEM((len(parts), PART_ROWS, width), BF16),
            sem=pltpu.SemaphoreType.DMA((len(parts),)),
        ),
        names,
    )
    return tuple(done[n] for n in WEIGHTS), done["over"][0]


def paired_sum(parts):
    while len(parts) > 1:
        parts = [parts[i] + parts[i + 1] for i in range(0, len(parts), 2)]
    return parts[0]


def local(
    features, position, cotangent, w_qkv, w_out, w_up, w_down, b_up, gains, shifts,
    window, shifted_window, dest, slot, valid,
):
    strips, subs = lax.axis_size("strip"), lax.axis_size("sub")
    rows, width = features.shape
    full = 2 * rows // strips
    short = -(-(10 * full) // 256) * 16
    weights = (w_qkv, w_out, w_up, w_down, b_up, gains, shifts)

    def swap(x):
        return lax.all_to_all(x, "strip", split_axis=0, concat_axis=0, tiled=True)

    def trade(x, strip_mask, sub_mask):
        pairs = [
            (t * subs + u, (t ^ strip_mask) * subs + (u ^ sub_mask)) for t in range(strips) for u in range(subs)
        ]
        return lax.ppermute(x, ("strip", "sub"), pairs)

    at_strip, at_sub = lax.axis_index("strip"), lax.axis_index("sub")
    who = jnp.stack([at_sub & 1, ((at_sub >> 1) & 1) + 2 * (at_strip & 1), at_strip]).astype(I32)

    ints = [x.reshape(rows // BLK, BLK) for x in (window, valid, dest, slot, shifted_window)]

    square = ((0, 2), (1, 0), (1, 2))

    def total(parts):
        return paired_sum([x.astype(F32) for x in parts]).astype(BF16)

    def attempt(cap, balanced):
        sent = send_rows(ints, position, cotangent, strips, cap, full, balanced)
        arrived = swap(sent["send"])
        zero = forward_zero(sent["meta"], features, position, weights, strips, cap, who)
        cross = lax.ppermute(zero.pop("cross"), "strip", [(t, t ^ 1) for t in range(strips)])
        moved = []
        for h in range(strips // 2):
            pair = jnp.concatenate([zero.pop(f"own{h}"), cross[h * cap : (h + 1) * cap]], axis=0)
            moved.append(lax.ppermute(pair, "strip", [(t, (t + 2 * h) % strips) for t in range(strips)]) if h else pair)
        one = layer_one(arrived, moved, weights, full, who)
        returned = swap(one["dx"])
        out, sums_one, returned = lax.optimization_barrier((one["out"], one["wg"], returned))
        out = swap(out)
        last = layer_zero(zero, returned, weights, sums_one, one["over"], who)
        grad, out, *parts = lax.optimization_barrier(
            (last["grad"], out, *(last[f"{n}{m}"] for n in ("keep", "give") for m in range(4)))
        )
        cut = [total((k, trade(g, 0, 1))) for k, g in zip(parts[:4], parts[4:])]
        part = total([cut[0]] + [trade(x, *mask) for x, mask in zip(cut[1:], square)])
        part = total([part] + [trade(part, m, 0) for m in range(2, strips, 2)])
        output = fetch_rows(sent["meta"], out.reshape(strips * full, width))
        part, output = lax.optimization_barrier((part, output))
        mine = [part] + [trade(part, *mask) for mask in square]
        sums, over = unpack_sums(mine + [trade(x, 0, 1) for x in mine], who)
        return (output, grad) + sums, over > 0

    done, over = attempt(short, True)
    _, done = lax.while_loop(
        lambda state: state[0], lambda state: (state[0] & False, attempt(full, False)[0]), (over, done)
    )
    return done


def solution(mesh):
    rows = P(("strip", "sub"), None)
    flat = P(("strip", "sub"))
    placed = (rows, P(None, ("strip", "sub"), None), rows) + (P(),) * 7 + (flat,) * 5
    return jax.shard_map(
        local,
        mesh=mesh,
        in_specs=placed,
        out_specs=(rows, rows) + (P(),) * 7,
        check_vma=False,
    )
```
